32 devices in a mesh: rep: 4 (over x, core), fsdp: 8 (over z, y).
Axes of the slice: x: 2, y: 2, z: 4, core: 2. Of those that a mesh axis runs over, the one named last changes fastest.
Arguments:
- tokens: bfloat16 [4096, 1536], P(('rep', 'fsdp')), may hold values from -6 to 6
- context: bfloat16 [4, 512, 1536], P('rep', 'fsdp'), may hold values from -6 to 6
- cotangent: bfloat16 [4096, 1536], P(('rep', 'fsdp')), may hold values from -6 to 6
- positions: int32 [3, 4096], P(None, ('rep', 'fsdp')), may hold values from 0 to 63
- sequence_lengths: int32 [4], P('rep'), may hold values from 512 to 1024, as said below
- sequence_adapter: int32 [4], P('rep'), may hold values from 0 to 7
- text_token_count: int32 [4], P('rep'), may hold values from 64 to 512, as said below
- timestep_modulation: float32 [4, 6, 1536], P('rep'), may hold values from -4 to 4
- modulation: float32 [2, 6, 1536], replicated, may hold values from -2 to 2
- gains: float32 [2, 5, 1536], replicated, may hold values from 0.5 to 1.5
- query_key_value_weight: bfloat16 [2, 6, 1536, 1536], P(None, None, 'fsdp'), may hold values from -0.15625 to 0.15625
- output_weight: bfloat16 [2, 2, 1536, 1536], P(None, None, 'fsdp'), may hold values from -0.3125 to 0.3125
- up_weight: bfloat16 [2, 1536, 8960], P(None, 'fsdp'), may hold values from -0.15625 to 0.15625
- down_weight: bfloat16 [2, 8960, 1536], P(None, 'fsdp'), may hold values from -0.0625 to 0.0625
- first_factors: bfloat16 [2, 9, 1536, 128], P(None, None, 'fsdp'), may hold values from -0.15625 to 0.15625
- down_first_factor: bfloat16 [2, 8960, 128], P(None, 'fsdp'), may hold values from -0.0625 to 0.0625
- second_factors: bfloat16 [2, 9, 128, 1536], P(None, None, None, 'fsdp'), may hold values from -1.5 to 1.5
- up_second_factor: bfloat16 [2, 128, 8960], P(None, None, 'fsdp'), may hold values from -1.5 to 1.5
Outputs:
- block_out: bfloat16 [4096, 1536], P(('rep', 'fsdp'))
- grad_tokens: float32 [4096, 1536], P(('rep', 'fsdp'))
- grad_context: float32 [4, 512, 1536], P('rep', 'fsdp')
- grad_lora_a: float32 [2, 9, 1536, 128], P(None, None, 'fsdp')
- grad_lora_a_down: float32 [2, 8960, 128], P(None, 'fsdp')
- grad_lora_b: float32 [2, 9, 128, 1536], P(None, None, None, 'fsdp')
- grad_lora_b_up: float32 [2, 128, 8960], P(None, None, 'fsdp')
The draws below stay inside these ranges and needn't reach their ends.
Inputs may be any that keep to these rules, and one draw needn't show every extreme that they name: `sequence_lengths`: the 1 entries of a group hold its sequences' valid lengths; at least one sequence in all has exactly 1024 tokens. `text_token_count`: some sequence uses all 512 text slots.
All inputs are finite; a program needn't handle non-finite values.
Results may differ from the reference program's by a relative error of at most 0.035.
Values may be sent and summed in bfloat16 or wider, within the bound.
No kernel may reach another device: no remote copies, remote signals or barrier semaphores. Data moves between devices by JAX's collectives and lax.ppermute only.
A program may use at most 704 MiB of HBM per device.

```python
import math
import jax
import jax.numpy as jnp
from jax import lax

MODEL_WIDTH = 1536
HIDDEN_UNITS = 8960
TEXT = 512
HD = 128
ADAPTER_RANK = 16
ADAPTERS = 8
BLOCK_COUNT = 2
TOK_DEV = 128
ADAPTER_COLUMNS = 128
GROUP = 1024
SEQS = 1
SEQ_ALL = 4
TOKENS = 4096
N_FSDP = 8


def draw_sequence_lengths(key, part):
    key = jax.random.fold_in(key, 11)
    first_key, second_key = jax.random.split(key)
    lengths = jax.random.randint(first_key, (SEQ_ALL,), GROUP // (2 * SEQS), GROUP // SEQS + 1)
    longest = jax.random.randint(second_key, (), 0, SEQ_ALL)
    lengths = jnp.where(jnp.arange(SEQ_ALL) == longest, GROUP // SEQS, lengths)
    return lengths.astype(jnp.int32)


def draw_text_token_count(key, part):
    key = jax.random.fold_in(key, 23)
    first_key, second_key = jax.random.split(key)
    counts = jax.random.randint(first_key, (SEQ_ALL,), TEXT // 8, TEXT + 1)
    fullest = jax.random.randint(second_key, (), 0, SEQ_ALL)
    counts = jnp.where(jnp.arange(SEQ_ALL) == fullest, TEXT, counts)
    return counts.astype(jnp.int32)


def plant(values, own_key, low, largest):
    dims = values.shape
    spot = [jax.random.randint(jax.random.fold_in(own_key, axis), (), 0, dims[axis]) for axis in range(len(dims))]
    values = values.at[tuple(spot)].set(low)
    longest = dims.index(max(dims))
    spot[longest] = (spot[longest] + 1) % dims[longest]
    return values.at[tuple(spot)].set(largest)


def block_levels(rng, dims, cuts, smallest, largest):
    def one(axis_at, blocks):
        steps = jax.random.uniform(jax.random.fold_in(jax.random.fold_in(rng, 6), axis_at), (blocks,), jnp.float32, smallest / len(cuts), largest / len(cuts))
        return jnp.repeat(jnp.exp(steps), dims[axis_at] // blocks).reshape((-1,) + (1,) * (len(dims) - axis_at - 1))

    loudness = one(*cuts[0])
    for cut in cuts[1:]:
        loudness = loudness * one(*cut)
    return loudness


def normal_values(key, dims, scale, most, cuts=(), held_as=jnp.bfloat16):
    entries = scale * jax.random.normal(key, dims, jnp.float32)
    if cuts:
        entries = entries * block_levels(key, dims, cuts, -0.22, 0.18)
    return jnp.clip(entries, -most, most).astype(held_as)


def setup_inputs(seed: int = 0) -> dict:
    seeds = jax.random.split(jax.random.key(seed), 19)
    tokens = normal_values(seeds[0], (TOKENS, MODEL_WIDTH), 1.0, 6.0, ((0, 32),))
    context = normal_values(seeds[1], (SEQ_ALL, TEXT, MODEL_WIDTH), 1.0, 6.0, ((0, 4), (1, 8)))
    cotangent = normal_values(seeds[2], (TOKENS, MODEL_WIDTH), 1.0, 6.0, ((0, 32),))
    positions = plant(jax.random.randint(seeds[3], (3, TOKENS), 0, 64), jax.random.fold_in(seeds[3], 1), 0, 63).astype(jnp.int32)
    sequence_lengths = draw_sequence_lengths(jax.random.fold_in(seeds[18], 71), 0)
    sequence_adapter = plant(jax.random.randint(seeds[5], (SEQ_ALL,), 0, ADAPTERS), jax.random.fold_in(seeds[5], 1), 0, ADAPTERS - 1).astype(jnp.int32)
    text_token_count = draw_text_token_count(jax.random.fold_in(seeds[18], 71), 0)
    timestep_modulation = normal_values(seeds[7], (SEQ_ALL, 6, MODEL_WIDTH), 0.5, 4.0, ((0, 4),), jnp.float32)
    modulation = normal_values(seeds[8], (BLOCK_COUNT, 6, MODEL_WIDTH), 0.3, 2.0, (), jnp.float32)
    gains = jnp.clip(1.0 + 0.1 * jax.random.normal(seeds[9], (BLOCK_COUNT, 5, MODEL_WIDTH), jnp.float32), 0.5, 1.5)
    query_key_value_weight = normal_values(seeds[10], (BLOCK_COUNT, 6, MODEL_WIDTH, MODEL_WIDTH), MODEL_WIDTH ** -0.5, 0.15625, ((2, 8),))
    output_weight = normal_values(seeds[11], (BLOCK_COUNT, 2, MODEL_WIDTH, MODEL_WIDTH), (MODEL_WIDTH // 4) ** -0.5, 0.3125, ((2, 8),))
    up_weight = normal_values(seeds[12], (BLOCK_COUNT, MODEL_WIDTH, HIDDEN_UNITS), MODEL_WIDTH ** -0.5, 0.15625, ((1, 8),))
    down_weight = normal_values(seeds[13], (BLOCK_COUNT, HIDDEN_UNITS, MODEL_WIDTH), HIDDEN_UNITS ** -0.5, 0.0625, ((1, 8),))
    first_factors = normal_values(seeds[14], (BLOCK_COUNT, 9, MODEL_WIDTH, ADAPTER_COLUMNS), MODEL_WIDTH ** -0.5, 0.15625, ((2, 8),))
    down_first_factor = normal_values(seeds[15], (BLOCK_COUNT, HIDDEN_UNITS, ADAPTER_COLUMNS), HIDDEN_UNITS ** -0.5, 0.0625, ((1, 8),))
    second_factors = normal_values(seeds[16], (BLOCK_COUNT, 9, ADAPTER_COLUMNS, MODEL_WIDTH), ADAPTER_RANK ** -0.5, 1.5, ((3, 8),))
    up_second_factor = normal_values(seeds[17], (BLOCK_COUNT, ADAPTER_COLUMNS, HIDDEN_UNITS), ADAPTER_RANK ** -0.5, 1.5, ((2, 8),))
    return {"tokens": tokens, "context": context, "cotangent": cotangent, "positions": positions, "sequence_lengths": sequence_lengths, "sequence_adapter": sequence_adapter, "text_token_count": text_token_count, "timestep_modulation": timestep_modulation, "modulation": modulation, "gains": gains, "query_key_value_weight": query_key_value_weight, "output_weight": output_weight, "up_weight": up_weight, "down_weight": down_weight, "first_factors": first_factors, "down_first_factor": down_first_factor, "second_factors": second_factors, "up_second_factor": up_second_factor}


epsilon = 1e-06
highest = lax.Precision.HIGHEST
masked_score = -1e+30

@jax.custom_vjp
def low(v):
    return lax.optimization_barrier(v.astype(jnp.bfloat16)).astype(jnp.float32)

@jax.custom_vjp
def low_back(v):
    return v

def low_keep(v):
    return (low(v), None)

def low_pass(kept, grad):
    return (grad,)

def back_keep(v):
    return (v, None)

def back_low(kept, grad):
    return (low(grad),)
low.defvjp(low_keep, low_pass)
low_back.defvjp(back_keep, back_low)

def matmul(left, right):
    return jnp.dot(left, right, precision=highest, preferred_element_type=jnp.float32)

def layer_norm(values):
    centred = values - lax.optimization_barrier(jnp.mean(values, -1, keepdims=True))
    return centred * lax.rsqrt(lax.optimization_barrier(jnp.mean(centred * centred, -1, keepdims=True)) + epsilon)

def rms_norm(values, weight_row):
    return values * lax.rsqrt(lax.optimization_barrier(jnp.mean(values * values, -1, keepdims=True)) + epsilon) * weight_row

def rotary_tables(positions, head_size):
    pair_count = head_size // 2
    third_part = pair_count // 3
    first_part = pair_count - 2 * third_part
    pieces = []
    for column, amount in ((0, first_part), (1, third_part), (2, third_part)):
        frequency = jnp.power(10000.0, -jnp.arange(amount, dtype=jnp.float32) / amount)
        pieces.append(positions[column].astype(jnp.float32)[:, None] * frequency[None, :])
    angles = jnp.concatenate(pieces, 1)
    return (jnp.cos(angles), jnp.sin(angles))

def rotate(values, cosine, sine):
    row_count = values.shape[0]
    paired = values.reshape(row_count, -1, cosine.shape[1], 2)
    real_part = paired[..., 0]
    imag_part = paired[..., 1]
    cosine = cosine[:, None, :]
    sine = sine[:, None, :]
    turned = jnp.stack((real_part * cosine - imag_part * sine, real_part * sine + imag_part * cosine), -1)
    return turned.reshape(values.shape)

def project(source, weight, down_a, up_b, adapter_mask):
    inner = low_back(matmul(source, down_a))
    inner = low(inner * adapter_mask)
    return low_back(matmul(source, weight) + matmul(inner, up_b))

def softmax_rows(scores, allowed):
    scores = jnp.where(allowed, scores, masked_score)
    weights = jnp.exp(scores - lax.optimization_barrier(jnp.max(scores, -1, keepdims=True)))
    return weights / lax.optimization_barrier(jnp.sum(weights, -1, keepdims=True))

def self_attention(query, keys, values, segment):
    group_rows, width = query.shape
    heads = width // HD
    block = min(512, group_rows)
    key_heads = keys.reshape(group_rows, heads, HD)
    value_heads = values.reshape(group_rows, heads, HD)
    score_scale = 1.0 / math.sqrt(HD)

    def one_block(pieces):
        query_piece, segment_piece = pieces
        scores = low_back(jnp.einsum('qhd,khd->hqk', query_piece.reshape(block, heads, HD), key_heads, precision=highest) * score_scale)
        probs = softmax_rows(scores, (segment_piece[:, None] == segment[None, :])[None])
        result = jnp.einsum('hqk,khd->qhd', low(probs), value_heads, precision=highest)
        return result.reshape(block, width)
    result = lax.map(jax.checkpoint(one_block), (query.reshape(-1, block, width), segment.reshape(-1, block)))
    return result.reshape(group_rows, width)

def cross_attention(query, text_keys, text_values, sequence, key_sequence, key_live):
    group_rows, width = query.shape
    heads = width // HD
    block = min(512, group_rows)
    key_rows = text_keys.shape[0]
    key_heads = text_keys.reshape(key_rows, heads, HD)
    value_heads = text_values.reshape(key_rows, heads, HD)
    score_scale = 1.0 / math.sqrt(HD)

    def one_block(pieces):
        query_piece, sequence_piece = pieces
        scores = low_back(jnp.einsum('qhd,khd->hqk', query_piece.reshape(block, heads, HD), key_heads, precision=highest) * score_scale)
        allowed = ((sequence_piece[:, None] == key_sequence[None, :]) & key_live[None, :])[None]
        probs = softmax_rows(scores, allowed)
        result = jnp.einsum('hqk,khd->qhd', low(probs), value_heads, precision=highest)
        return result.reshape(block, width)
    result = lax.map(jax.checkpoint(one_block), (query.reshape(-1, block, width), sequence.reshape(-1, block)))
    return result.reshape(group_rows, width)

def block_forward(state, context_rows, matrices, adapters, weight_rows, token_mods, masks):
    w_in, w_proj, w_upper, w_lower = matrices
    down_main, down_ffn, up_main, up_ffn = adapters
    valid, token_mask, text_mask, segment, sequence, key_sequence, key_live, cosine, sine = masks
    shift_one, scale_one, gate_one, shift_two, scale_two, gate_two = [token_mods[:, member] for member in range(6)]
    normed = low(layer_norm(state) * (1.0 + scale_one) + shift_one)
    query_raw = project(normed, w_in[0], down_main[0], up_main[0], token_mask)
    key_raw = project(normed, w_in[1], down_main[1], up_main[1], token_mask)
    value_raw = project(normed, w_in[2], down_main[2], up_main[2], token_mask)
    query = low(rotate(rms_norm(query_raw, weight_rows[0]), cosine, sine))
    keys = low(rotate(rms_norm(key_raw, weight_rows[1]), cosine, sine))
    values = low(value_raw)
    attended = low(low_back(self_attention(query, keys, values, segment)))
    self_branch = project(attended, w_proj[0], down_main[3], up_main[3], token_mask)
    state_one = state + valid * gate_one * self_branch
    normed_cross = low(layer_norm(state_one) * weight_rows[4])
    cross_query = low(rms_norm(project(normed_cross, w_in[3], down_main[4], up_main[4], token_mask), weight_rows[2]))
    text_keys = low(rms_norm(project(context_rows, w_in[4], down_main[5], up_main[5], text_mask), weight_rows[3]))
    text_values = low(project(context_rows, w_in[5], down_main[6], up_main[6], text_mask))
    crossed = low(low_back(cross_attention(cross_query, text_keys, text_values, sequence, key_sequence, key_live)))
    cross_branch = project(crossed, w_proj[1], down_main[7], up_main[7], token_mask)
    state_two = state_one + valid * cross_branch
    normed_ffn = low(layer_norm(state_two) * (1.0 + scale_two) + shift_two)
    up_raw = project(normed_ffn, w_upper, down_main[8], up_ffn, token_mask)
    hidden = low(jax.nn.gelu(up_raw, approximate=True))
    down_raw = project(hidden, w_lower, down_ffn, up_main[8], token_mask)
    return state_two + valid * gate_two * down_raw

def reference(tokens, context, cotangent, positions, sequence_lengths, sequence_adapter, text_token_count, timestep_modulation, modulation, gains, query_key_value_weight, output_weight, up_weight, down_weight, first_factors, down_first_factor, second_factors, up_second_factor):
    matrices_all = (query_key_value_weight.astype(jnp.float32), output_weight.astype(jnp.float32), up_weight.astype(jnp.float32), down_weight.astype(jnp.float32))
    every_adapter = (first_factors.astype(jnp.float32), down_first_factor.astype(jnp.float32), second_factors.astype(jnp.float32), up_second_factor.astype(jnp.float32))
    group_count = TOKENS // GROUP
    group_tokens = tokens.astype(jnp.float32).reshape(group_count, GROUP, MODEL_WIDTH)
    group_context = context.astype(jnp.float32).reshape(group_count, SEQS * TEXT, MODEL_WIDTH)
    group_positions = jnp.transpose(positions.reshape(3, group_count, GROUP), (1, 0, 2))
    group_lengths = sequence_lengths.reshape(group_count, SEQS)
    group_choice = sequence_adapter.reshape(group_count, SEQS)
    group_counts = text_token_count.reshape(group_count, SEQS)
    group_times = timestep_modulation.reshape(group_count, SEQS, 6, MODEL_WIDTH)

    def forward(state_all, context_all, adapters):

        def one_group(pieces):
            state, context_rows, place, lengths, chosen, counts, times = pieces
            slot_index = jnp.arange(GROUP, dtype=jnp.int32)
            packed = slot_index % TOK_DEV * N_FSDP + slot_index // TOK_DEV
            bounds = jnp.cumsum(lengths)
            segment = lax.optimization_barrier(jnp.sum((packed[:, None] >= bounds[None, :]).astype(jnp.int32), 1))
            valid = (segment < SEQS).astype(jnp.float32)[:, None]
            sequence = jnp.minimum(segment, SEQS - 1)
            columns = jnp.arange(ADAPTER_COLUMNS) // ADAPTER_RANK
            token_mask = (columns[None, :] == chosen[sequence][:, None]).astype(jnp.float32) * valid
            text_mask = jnp.repeat((columns[None, :] == chosen[:, None]).astype(jnp.float32), TEXT, 0)
            key_sequence = jnp.repeat(jnp.arange(SEQS), TEXT)
            key_live = jnp.tile(jnp.arange(TEXT), SEQS) < jnp.repeat(counts, TEXT)
            cosine, sine = rotary_tables(place, HD)
            masks = (valid, token_mask, text_mask, segment, sequence, key_sequence, key_live, cosine, sine)
            for block_index in range(BLOCK_COUNT):
                token_mods = (modulation[block_index][None] + times)[sequence]
                matrices = tuple((matrix[block_index] for matrix in matrices_all))
                layer_adapters = tuple((factor[block_index] for factor in adapters))
                state = block_forward(state, context_rows, matrices, layer_adapters, gains[block_index], token_mods, masks)
            return state
        return lax.map(jax.checkpoint(one_group), (state_all, context_all, group_positions, group_lengths, group_choice, group_counts, group_times))
    output, pull = jax.vjp(forward, group_tokens, group_context, every_adapter)
    grad_state, grad_text, grad_adapters = pull(cotangent.astype(jnp.float32).reshape(group_count, GROUP, MODEL_WIDTH))
    return (output.reshape(TOKENS, MODEL_WIDTH).astype(jnp.bfloat16), grad_state.reshape(TOKENS, MODEL_WIDTH), grad_text.reshape(SEQ_ALL, TEXT, MODEL_WIDTH), grad_adapters[0], grad_adapters[1], grad_adapters[2], grad_adapters[3])
```

```python
import math

import jax
import jax.numpy as jnp
from jax import lax
from jax.sharding import PartitionSpec as P

HD = 128
ADAPTER_RANK = 16
TENSOR = 4

AXES = ("rep", "fsdp")
epsilon = 1e-06
masked_score = -1e30
f32 = jnp.float32
bf16 = jnp.bfloat16


def dot(left, right):
    return jnp.dot(left, right, preferred_element_type=f32)


def dot_nt(left, right):
    return lax.dot_general(left, right, (((1,), (1,)), ((), ())), preferred_element_type=f32)


def dot_tn(left, right):
    return lax.dot_general(left, right, (((0,), (0,)), ((), ())), preferred_element_type=f32)


class Place:
    def __init__(self):
        self.rep = lax.axis_size(AXES[0])
        self.size = lax.axis_size(AXES[1])
        self.outer = self.rep // 2
        self.half = self.size // 2
        self.blocks = self.half // TENSOR
        self.shards = self.size // TENSOR
        self.r = lax.axis_index(AXES[0])
        self.f = lax.axis_index(AXES[1])
        self.c = self.r % 2
        self.h = self.f // self.half
        self.b = (self.f // TENSOR) % self.blocks
        self.p = self.f % TENSOR

    def send(self, values, move):
        pairs = []
        for r in range(self.rep):
            for f in range(self.size):
                o, c = divmod(r, 2)
                h, rest = divmod(f, self.half)
                b, p = divmod(rest, TENSOR)
                o, c, h, b, p = move(o, c, h, b, p)
                target = (2 * o + c) * self.size + h * self.half + b * TENSOR + p
                pairs.append((r * self.size + f, target))
        return lax.ppermute(values, AXES, pairs)

    def send_rows(self, values, move):
        pairs = [(f, move(f)) for f in range(self.size)]
        return lax.ppermute(values, AXES[1], pairs)

    def swap(self, values):
        return self.send(values, lambda o, c, h, b, p: (o, h, c, b, p))

    def part(self, values, k):
        return self.send_rows(values, lambda f: f ^ k)

    def other_block(self, values, k):
        return self.send_rows(values, lambda f: f ^ (TENSOR * k))

    def other_core(self, values):
        return self.send(values, lambda o, c, h, b, p: (o, 1 - c, h, b, p))

    def other_outer(self, values, k):
        return self.send(values, lambda o, c, h, b, p: (o ^ k, c, h, b, p))

    def gather(self, rows):
        cut = rows.shape[1] // 2
        one = self.part(rows, 1)
        two = self.part(rows, 2)
        far = jnp.concatenate([self.part(one[:, :cut], 2), self.part(two[:, cut:], 1)], 1)
        return jnp.concatenate([rows, one, two, far], 0)

    def scatter(self, rows):
        cut = rows.shape[1] // 2
        count = rows.shape[0] // TENSOR
        rows = rows.astype(bf16)
        left = [rows[k * count : (k + 1) * count, :cut] for k in range(TENSOR)]
        right = [rows[k * count : (k + 1) * count, cut:] for k in range(TENSOR)]
        from_one = self.part(jnp.concatenate([left[1], left[3]], 0), 1).astype(f32)
        from_two = self.part(jnp.concatenate([right[2], right[3]], 0), 2).astype(f32)
        left_far = (left[2].astype(f32) + from_one[count:]).astype(bf16)
        right_far = (right[1].astype(f32) + from_two[count:]).astype(bf16)
        left_sum = left[0].astype(f32) + from_one[:count] + self.part(left_far, 2).astype(f32)
        right_sum = right[0].astype(f32) + from_two[:count] + self.part(right_far, 1).astype(f32)
        return jnp.concatenate([left_sum, right_sum], 1)

    def total(self, stats):
        result = stats
        for k in range(1, TENSOR):
            arrived = self.part(stats, k)
            result = result + jnp.stack([arrived[:, j ^ k] for j in range(TENSOR)], 1)
        return result

    def spread(self, rows):
        own = [rows] + [self.other_block(rows, k) for k in range(1, self.blocks)]
        stacked = jnp.concatenate(own, 0) if len(own) > 1 else rows
        return jnp.concatenate([stacked, self.other_core(stacked)], 0)

    def collect(self, rows):
        count = rows.shape[0] // 2
        block = count // self.blocks
        total = rows[:count] + self.other_core(rows[count:].astype(bf16)).astype(f32)
        result = total[:block]
        for k in range(1, self.blocks):
            piece = total[k * block : (k + 1) * block].astype(bf16)
            result = result + self.other_block(piece, k).astype(f32)
        return result

    def gather_rep(self, rows):
        n, q, w = rows.shape
        whole = jnp.zeros((n, self.rep, q, w), rows.dtype)

        def put(whole, piece, index):
            return lax.dynamic_update_slice(whole, piece[:, None], (0, index, 0, 0))

        for k in range(self.outer):
            piece = rows if k == 0 else self.other_outer(rows, k)
            whole = put(whole, piece, self.r ^ (2 * k))
            whole = put(whole, self.other_core(piece), self.r ^ (2 * k + 1))
        return whole.reshape(n * self.rep * q, w)

    def quarter(self, rows):
        count = rows.shape[0] // self.rep
        return lax.dynamic_slice_in_dim(rows, self.r * count, count, 0)

    def fetch_columns(self, matrices, extras, after):
        matrices = [self.quarter(m) for m in matrices]
        extras = [self.quarter(e) for e in extras]
        matrices, extras, _ = lax.optimization_barrier((matrices, extras, after))
        pieces = []
        for k in range(TENSOR):
            part = self.p ^ k
            pieces.append(
                [
                    lax.dynamic_slice_in_dim(
                        m, part * (m.shape[1] // TENSOR), m.shape[1] // TENSOR, 1
                    )
                    for m in matrices
                ]
            )
        width = sum(m.shape[1] // TENSOR for m in matrices) + sum(e.shape[2] for e in extras)
        whole = jnp.zeros((self.size, matrices[0].shape[0], width), bf16)
        arrived = []
        for k in range(self.size):
            to_half = self.h ^ (k // self.half)
            chosen = [jnp.where(to_half == 0, e[:, 0], e[:, 1]) for e in extras]
            piece = jnp.concatenate(pieces[k % TENSOR] + chosen, 1)
            if k:
                piece = self.send_rows(piece, lambda f, k=k: f ^ k)
            arrived.append(piece)
            whole = lax.dynamic_update_slice(whole, piece[None], (self.f ^ k, 0, 0))
        return self.gather_rep(whole), arrived[-1]

    def fetch_rows(self, matrix, extras, after):
        matrix = self.quarter(matrix)
        extras = [self.quarter(e) for e in extras]
        matrix, extras, _ = lax.optimization_barrier((matrix, extras, after))
        width = matrix.shape[1] + sum(e.shape[2] for e in extras)
        whole = jnp.zeros((self.shards, matrix.shape[0], width), bf16)
        shard = self.f % self.shards
        arrived = []
        for k in range(self.shards):
            to_half = ((shard + k) % self.shards) // self.blocks
            chosen = [jnp.where(to_half == 0, e[:, 0], e[:, 1]) for e in extras]
            piece = jnp.concatenate([matrix] + chosen, 1)
            piece = self.send_rows(
                piece,
                lambda f, k=k: f // self.shards + TENSOR * ((f % self.shards + k) % self.shards),
            )
            arrived.append(piece)
            source = (self.f // TENSOR - k) % self.shards
            whole = lax.dynamic_update_slice(whole, piece[None], (source, 0, 0))
        return self.gather_rep(whole), arrived[-1]


def norm_parts(values):
    centred = values - jnp.mean(values, -1, keepdims=True)
    scale = lax.rsqrt(jnp.mean(centred * centred, -1, keepdims=True) + epsilon)
    return centred * scale, scale


def layer_norm_back(values, grad):
    hat, scale = norm_parts(values)
    along = jnp.mean(grad * hat, -1, keepdims=True)
    return scale * (grad - jnp.mean(grad, -1, keepdims=True) - hat * along)


def rotary_tables(positions):
    pair_count = HD // 2
    third_part = pair_count // 3
    first_part = pair_count - 2 * third_part
    pieces = []
    for column, amount in ((0, first_part), (1, third_part), (2, third_part)):
        frequency = jnp.power(10000.0, -jnp.arange(amount, dtype=f32) / amount)
        pieces.append(positions[column].astype(f32)[:, None] * frequency[None, :])
    angles = jnp.repeat(jnp.concatenate(pieces, 1), 2, 1)
    sign = jnp.where(jnp.arange(HD) % 2 == 0, -1.0, 1.0)
    return jnp.cos(angles), jnp.sin(angles) * sign


def swap_pairs(values):
    rows, width = values.shape
    index = jnp.arange(HD)
    exchange = (index[:, None] == (index[None, :] ^ 1)).astype(f32)
    flat = values.reshape(rows, width // HD, HD)
    turned = lax.dot_general(
        flat, exchange, (((2,), (0,)), ((), ())), precision=lax.Precision.HIGHEST
    )
    return turned.reshape(rows, width)


def rotate(values, cosine, sine):
    heads = values.shape[1] // HD
    return values * jnp.tile(cosine, (1, heads)) + swap_pairs(values) * jnp.tile(sine, (1, heads))


def rotate_back(grad, cosine, sine):
    heads = grad.shape[1] // HD
    return grad * jnp.tile(cosine, (1, heads)) + swap_pairs(grad * jnp.tile(sine, (1, heads)))


def attend(query, keys, values, allowed):
    scale = 1.0 / math.sqrt(HD)
    results, totals = [], []
    for head in range(query.shape[1] // HD):
        at = slice(head * HD, (head + 1) * HD)
        scores = jnp.where(allowed, dot_nt(query[:, at], keys[:, at]) * scale, masked_score)
        peak = jnp.max(scores, -1, keepdims=True)
        weights = jnp.where(allowed, jnp.exp(scores - peak), 0.0)
        total = jnp.sum(weights, -1, keepdims=True)
        results.append(dot(weights.astype(bf16), values[:, at]) / total)
        totals.append(peak + jnp.log(total))
    return jnp.concatenate(results, 1), totals


def attend_back(query, keys, values, grad, out, totals, allowed):
    scale = 1.0 / math.sqrt(HD)
    grad_query, grad_keys, grad_values = [], [], []
    for head in range(query.shape[1] // HD):
        at = slice(head * HD, (head + 1) * HD)
        q, k, v, g = query[:, at], keys[:, at], values[:, at], grad[:, at]
        delta = jnp.sum(g.astype(f32) * out[:, at], -1, keepdims=True)
        probs = jnp.where(allowed, jnp.exp(dot_nt(q, k) * scale - totals[head]), 0.0)
        grad_scores = (probs * (dot_nt(g, v) - delta)).astype(bf16)
        grad_query.append(dot(grad_scores, k) * scale)
        grad_keys.append(dot_tn(grad_scores, q) * scale)
        grad_values.append(dot_tn(probs.astype(bf16), g))
    return tuple(jnp.concatenate(parts, 1) for parts in (grad_query, grad_keys, grad_values))


def on_device(
    tokens,
    context,
    cotangent,
    positions,
    sequence_lengths,
    sequence_adapter,
    text_token_count,
    timestep_modulation,
    modulation,
    gains,
    query_key_value_weight,
    output_weight,
    up_weight,
    down_weight,
    first_factors,
    down_first_factor,
    second_factors,
    up_second_factor,
):
    place = Place()
    rows, width = tokens.shape
    seq_count, text_local = context.shape[:2]
    layers = query_key_value_weight.shape[0]
    columns = first_factors.shape[3]
    rank = place.outer * seq_count * ADAPTER_RANK
    own = width // TENSOR
    wide = up_weight.shape[2] // TENSOR
    set_rows = TENSOR * rows

    table = jnp.zeros((place.rep, seq_count), jnp.int32)
    arrived = sequence_adapter
    for k in range(place.outer):
        arrived = sequence_adapter if k == 0 else place.other_outer(sequence_adapter, k)
        for m, values in enumerate((arrived, place.other_core(arrived))):
            here = jnp.arange(place.rep) == (place.r ^ (2 * k + m))
            table = jnp.where(here[:, None], values[None], table)

    def chooser(adapters):
        column = (adapters[:, None] * ADAPTER_RANK + jnp.arange(ADAPTER_RANK)[None, :]).reshape(-1)
        return (jnp.arange(columns)[:, None] == column[None, :]).astype(bf16)

    choosers = [chooser(table[half::2].reshape(-1)) for half in range(2)]
    choose = jnp.concatenate(choosers, 1)

    def down_columns(factor):
        return dot(factor, choose).astype(bf16).reshape(factor.shape[0], 2, rank)

    def up_columns(factor):
        return dot_tn(factor, choose).astype(bf16).reshape(factor.shape[1], 2, rank)

    numbers = jnp.concatenate([positions.reshape(-1), sequence_lengths, text_token_count])
    numbers = place.swap(numbers)
    state = place.swap(tokens).astype(f32)
    times = place.swap(timestep_modulation)
    positions = numbers[: 3 * rows].reshape(3, rows)
    lengths, counts = [
        numbers[3 * rows + k * seq_count : 3 * rows + (k + 1) * seq_count] for k in range(2)
    ]

    bounds = jnp.cumsum(lengths)

    def first_index(core, block, part):
        return core * place.half + block * TENSOR + part

    def token_segments(index):
        packed = jnp.arange(rows, dtype=jnp.int32) * place.size + index
        return jnp.sum((packed[:, None] >= bounds[None, :]).astype(jnp.int32), 1)

    def text_marks(index):
        at = index * text_local + jnp.arange(text_local)
        marks = jnp.where(at[None, :] < counts[:, None], jnp.arange(seq_count)[:, None], -1)
        return marks.reshape(-1)

    def over_set(function, core, block):
        return jnp.concatenate(
            [function(first_index(core, block, place.p ^ k)) for k in range(TENSOR)]
        )

    def over_group(function):
        return jnp.concatenate(
            [
                over_set(function, core, place.b ^ k)
                for core in (place.c, 1 - place.c)
                for k in range(place.blocks)
            ]
        )

    segment = over_set(token_segments, place.c, place.b)
    sequence = jnp.minimum(segment, seq_count - 1)
    self_allowed = segment[:, None] == over_group(token_segments)[None, :]
    cross_allowed = sequence[:, None] == over_group(text_marks)[None, :]
    column_sequence = jnp.arange(rank) // ADAPTER_RANK - (place.r // 2) * seq_count
    mask = (sequence[:, None] == column_sequence[None, :]) & (segment < seq_count)[:, None]
    mask = mask.astype(f32)
    text_sequence = jnp.tile(jnp.repeat(jnp.arange(seq_count), text_local), TENSOR)
    text_mask = (text_sequence[:, None] == column_sequence[None, :]).astype(f32)
    valid = (segment[:rows] < seq_count).astype(f32)[:, None]

    def mods_of(layer):
        table = modulation[layer][None] + times
        chosen = [table[0, k][None] for k in range(6)]
        for s in range(1, seq_count):
            here = (sequence[:rows] == s)[:, None]
            chosen = [jnp.where(here, table[s, k][None], chosen[k]) for k in range(6)]
        return chosen

    def own_gain(layer, index):
        return lax.dynamic_slice_in_dim(gains[layer, index], place.p * own, own, 0)[None]

    fetched = []
    after = choose
    for layer in range(layers):
        qkv, proj = query_key_value_weight[layer], output_weight[layer]
        first, second = first_factors[layer], second_factors[layer]
        down = [down_columns(first[k]) for k in range(9)]
        up = [up_columns(second[k]) for k in range(9)]
        self_in, after = place.fetch_columns(
            [qkv[0], qkv[1], qkv[2]], [down[0], down[1], down[2], up[3]], after
        )
        self_out, after = place.fetch_rows(proj[0], [down[3], up[0], up[1], up[2]], after)
        cross_in, after = place.fetch_columns(
            [qkv[3], qkv[4], qkv[5]], [down[4], down[5], down[6], up[7]], after
        )
        cross_out, after = place.fetch_rows(proj[1], [down[7], up[4], up[5], up[6]], after)
        ffn_in, after = place.fetch_columns([up_weight[layer]], [down[8], up[8]], after)
        ffn_out, after = place.fetch_rows(
            down_weight[layer],
            [down_columns(down_first_factor[layer]), up_columns(up_second_factor[layer])],
            after,
        )
        fetched.append((self_in, self_out, cross_in, cross_out, ffn_in, ffn_out))

    cotangent = place.swap(cotangent)
    text = place.gather(place.swap(context.reshape(seq_count * text_local, width)))
    positions = jnp.stack([positions] + [place.part(positions, k) for k in range(1, TENSOR)], 1)
    cosine, sine = rotary_tables(positions.reshape(3, set_rows))

    def column(value):
        return value.reshape(-1, 1)

    def rms_scales(values):
        squares = jnp.stack([jnp.sum(v * v, -1).reshape(TENSOR, -1) for v in values])
        total = place.total(squares)
        return [column(lax.rsqrt(t / width + epsilon)) for t in total]

    def rms_backs(items):
        scaled = [(v * s, s, g * w) for v, s, w, g in items]
        along = jnp.stack([jnp.sum(h * g, -1).reshape(TENSOR, -1) for h, s, g in scaled])
        along = place.total(along) / width
        return [s * (g - h * column(a)) for (h, s, g), a in zip(scaled, along)]

    def extra(bundle, start, index):
        return bundle[:, start + index * rank : start + (index + 1) * rank]

    def narrow(values, mask):
        return (values * mask).astype(bf16)

    saved = []
    for layer in range(layers):
        self_in, self_out, cross_in, cross_out, ffn_in, ffn_out = fetched[layer]
        shift_one, scale_one, gate_one, shift_two, scale_two, gate_two = mods_of(layer)
        normed = (norm_parts(state)[0] * (1.0 + scale_one) + shift_one).astype(bf16)
        normed = place.gather(normed)
        raw = dot(normed, self_in)
        self_inner = [
            narrow(raw[:, 3 * own + k * rank : 3 * own + (k + 1) * rank], mask) for k in range(3)
        ]
        query_raw, key_raw, value_raw = [
            raw[:, k * own : (k + 1) * own] + dot_nt(self_inner[k], extra(self_out, width, 1 + k))
            for k in range(3)
        ]
        query_scale, key_scale = rms_scales([query_raw, key_raw])
        query = rotate(query_raw * query_scale * own_gain(layer, 0), cosine, sine).astype(bf16)
        keys = rotate(key_raw * key_scale * own_gain(layer, 1), cosine, sine).astype(bf16)
        both = place.spread(jnp.concatenate([keys, value_raw.astype(bf16)], 1))
        keys, values = both[:, :own], both[:, own:]
        self_result, self_totals = attend(query, keys, values, self_allowed)
        attended = self_result.astype(bf16)
        raw = dot(attended, self_out[:, : width + rank])
        out_inner = narrow(raw[:, width:], mask)
        branch = raw[:, :width] + dot_nt(out_inner, extra(self_in, 3 * own, 3))
        state_one = state + valid * gate_one * place.scatter(branch)

        normed_cross = (norm_parts(state_one)[0] * gains[layer, 4][None]).astype(bf16)
        normed_cross = place.gather(normed_cross)
        cross_inner = narrow(dot(normed_cross, extra(cross_in, 3 * own, 0)), mask)
        cross_raw = dot(normed_cross, cross_in[:, :own]) + dot_nt(
            cross_inner, extra(cross_out, width, 1)
        )
        text_raw = dot(text, cross_in[:, own : 3 * own])
        text_inner = [narrow(dot(text, extra(cross_in, 3 * own, k)), text_mask) for k in (1, 2)]
        text_key_raw, text_value_raw = [
            text_raw[:, k * own : (k + 1) * own]
            + dot_nt(text_inner[k], extra(cross_out, width, 2 + k))
            for k in range(2)
        ]
        (text_scale,) = rms_scales([text_key_raw])
        text_keys = (text_key_raw * text_scale * own_gain(layer, 3)).astype(bf16)
        both = place.spread(jnp.concatenate([text_keys, text_value_raw.astype(bf16)], 1))
        text_keys, text_values = both[:, :own], both[:, own:]
        (cross_scale,) = rms_scales([cross_raw])
        cross_query = (cross_raw * cross_scale * own_gain(layer, 2)).astype(bf16)
        cross_result, cross_totals = attend(cross_query, text_keys, text_values, cross_allowed)
        crossed = cross_result.astype(bf16)
        raw = dot(crossed, cross_out[:, : width + rank])
        crossed_inner = narrow(raw[:, width:], mask)
        branch = raw[:, :width] + dot_nt(crossed_inner, extra(cross_in, 3 * own, 3))
        state_two = state_one + valid * place.scatter(branch)

        normed_ffn = (norm_parts(state_two)[0] * (1.0 + scale_two) + shift_two).astype(bf16)
        normed_ffn = place.gather(normed_ffn)
        up_inner = narrow(dot(normed_ffn, extra(ffn_in, wide, 0)), mask)
        up_raw = dot(normed_ffn, ffn_in[:, :wide]) + dot_nt(up_inner, extra(ffn_out, width, 1))
        hidden = jax.nn.gelu(up_raw, approximate=True).astype(bf16)
        raw = dot(hidden, ffn_out[:, : width + rank])
        down_inner = narrow(raw[:, width:], mask)
        branch = raw[:, :width] + dot_nt(down_inner, extra(ffn_in, wide, 1))
        saved.append(
            (
                (state, state_one, state_two),
                (scale_one, gate_one, scale_two, gate_two),
                (normed, self_inner, query_raw, key_raw, query_scale, key_scale),
                (query, keys, values, self_result, self_totals, attended, out_inner),
                (normed_cross, cross_inner, cross_raw, cross_scale, cross_query),
                (text_inner, text_key_raw, text_scale, text_keys, text_values),
                (cross_result, cross_totals, crossed, crossed_inner),
                (normed_ffn, up_inner, up_raw, hidden, down_inner),
            )
        )
        state = state_two + valid * gate_two * place.scatter(branch)

    grad = cotangent.astype(f32)
    grad_text = jnp.zeros((TENSOR * seq_count * text_local, width), f32)
    whole_grads, part_grads, wide_grads = [], [], []
    for layer in reversed(range(layers)):
        self_in, self_out, cross_in, cross_out, ffn_in, ffn_out = fetched[layer]
        (
            (state_zero, state_one, state_two),
            (scale_one, gate_one, scale_two, gate_two),
            (normed, self_inner, query_raw, key_raw, query_scale, key_scale),
            (query, keys, values, self_result, self_totals, attended, out_inner),
            (normed_cross, cross_inner, cross_raw, cross_scale, cross_query),
            (text_inner, text_key_raw, text_scale, text_keys, text_values),
            (cross_result, cross_totals, crossed, crossed_inner),
            (normed_ffn, up_inner, up_raw, hidden, down_inner),
        ) = saved[layer]

        grad_down = place.gather((grad * (valid * gate_two)).astype(bf16))
        down_back = narrow(dot(grad_down, extra(ffn_in, wide, 1)), mask)
        grad_hidden = dot_nt(
            jnp.concatenate([grad_down, down_back], 1), ffn_out[:, : width + rank]
        )
        gelu_back = jax.vjp(lambda raw: jax.nn.gelu(raw, approximate=True), up_raw)[1]
        grad_up = gelu_back(grad_hidden)[0].astype(bf16)
        up_back = narrow(dot(grad_up, extra(ffn_out, width, 1)), mask)
        grad_normed = place.scatter(
            dot_nt(jnp.concatenate([grad_up, up_back], 1), ffn_in[:, : wide + rank])
        )
        grad_two = grad + layer_norm_back(state_two, grad_normed * (1.0 + scale_two))

        grad_branch = place.gather((grad_two * valid).astype(bf16))
        crossed_back = narrow(dot(grad_branch, extra(cross_in, 3 * own, 3)), mask)
        grad_crossed = dot_nt(
            jnp.concatenate([grad_branch, crossed_back], 1), cross_out[:, : width + rank]
        ).astype(bf16)
        grad_query, grad_keys, grad_values = attend_back(
            cross_query, text_keys, text_values, grad_crossed, cross_result, cross_totals,
            cross_allowed,
        )
        (grad_cross_raw,) = rms_backs([(cross_raw, cross_scale, own_gain(layer, 2), grad_query)])
        grad_cross_raw = grad_cross_raw.astype(bf16)
        cross_back = narrow(dot(grad_cross_raw, extra(cross_out, width, 1)), mask)
        grad_normed = place.scatter(
            dot_nt(grad_cross_raw, cross_in[:, :own])
            + dot_nt(cross_back, extra(cross_in, 3 * own, 0))
        )
        grad_one = grad_two + layer_norm_back(state_one, grad_normed * gains[layer, 4][None])

        both = place.collect(jnp.concatenate([grad_keys, grad_values], 1))
        (grad_text_key,) = rms_backs(
            [(text_key_raw, text_scale, own_gain(layer, 3), both[:, :own])]
        )
        grad_text_raw = jnp.concatenate([grad_text_key, both[:, own:]], 1).astype(bf16)
        grad_text_key, grad_text_value = grad_text_raw[:, :own], grad_text_raw[:, own:]
        text_key_back = narrow(dot(grad_text_key, extra(cross_out, width, 2)), text_mask)
        text_value_back = narrow(dot(grad_text_value, extra(cross_out, width, 3)), text_mask)
        grad_text = (
            grad_text
            + dot_nt(grad_text_raw, cross_in[:, own : 3 * own])
            + dot_nt(text_key_back, extra(cross_in, 3 * own, 1))
            + dot_nt(text_value_back, extra(cross_in, 3 * own, 2))
        )

        grad_branch_self = place.gather((grad_one * (valid * gate_one)).astype(bf16))
        out_back = narrow(dot(grad_branch_self, extra(self_in, 3 * own, 3)), mask)
        grad_attended = dot_nt(
            jnp.concatenate([grad_branch_self, out_back], 1), self_out[:, : width + rank]
        ).astype(bf16)
        grad_query, grad_keys, grad_values = attend_back(
            query, keys, values, grad_attended, self_result, self_totals, self_allowed
        )
        both = place.collect(jnp.concatenate([grad_keys, grad_values], 1))
        grad_query_raw, grad_key_raw = rms_backs(
            [
                (query_raw, query_scale, own_gain(layer, 0), rotate_back(grad_query, cosine, sine)),
                (key_raw, key_scale, own_gain(layer, 1), rotate_back(both[:, :own], cosine, sine)),
            ]
        )
        raw_grads = [
            grad_query_raw.astype(bf16), grad_key_raw.astype(bf16), both[:, own:].astype(bf16)
        ]
        self_backs = [
            narrow(dot(raw_grads[k], extra(self_out, width, 1 + k)), mask) for k in range(3)
        ]
        grad_normed = place.scatter(
            dot_nt(
                jnp.concatenate(raw_grads + self_backs, 1), self_in[:, : 3 * own + 3 * rank]
            )
        )
        grad = grad_one + layer_norm_back(state_zero, grad_normed * (1.0 + scale_one))

        whole_grads.append(
            [
                dot_tn(normed, jnp.concatenate(self_backs, 1)),
                dot_tn(normed_cross, cross_back),
                dot_tn(text, jnp.concatenate([text_key_back, text_value_back], 1)),
                dot_tn(normed_ffn, up_back),
                dot_tn(grad_branch_self, out_inner),
                dot_tn(grad_branch, crossed_inner),
                dot_tn(grad_down, down_inner),
            ]
        )
        part_grads.append(
            [
                dot_tn(attended, out_back),
                dot_tn(crossed, crossed_back),
                dot_tn(raw_grads[0], self_inner[0]),
                dot_tn(raw_grads[1], self_inner[1]),
                dot_tn(raw_grads[2], self_inner[2]),
                dot_tn(grad_cross_raw, cross_inner),
                dot_tn(grad_text_key, text_inner[0]),
                dot_tn(grad_text_value, text_inner[1]),
            ]
        )
        wide_grads.append([dot_tn(hidden, down_back), dot_tn(grad_up, up_inner)])

    def flat(lists):
        return jnp.concatenate([item for items in reversed(lists) for item in items], 1)

    whole_all = flat(whole_grads).astype(bf16)
    whole_all = jnp.concatenate(
        [lax.dynamic_slice_in_dim(whole_all, (place.p ^ k) * own, own, 0) for k in range(TENSOR)]
    )
    from_parts = place.scatter(whole_all)

    def sum_set(values):
        values = values + place.other_core(values.astype(bf16)).astype(f32)
        result = values
        for k in range(1, place.blocks):
            result = result + place.other_block(values.astype(bf16), k).astype(f32)
        return result.astype(bf16)

    narrow_all = sum_set(jnp.concatenate([from_parts, flat(part_grads)], 1))
    wide_all = sum_set(flat(wide_grads))

    def to_owner(values, turn):
        count = values.shape[0] // place.shards
        shard = place.b + place.blocks * (place.h ^ turn)
        piece = lax.dynamic_slice_in_dim(values, shard * count, count, 0)

        def move(f):
            h, rest = divmod(f, place.half)
            b, p = divmod(rest, TENSOR)
            return place.shards * p + b + place.blocks * (h ^ turn)

        return place.send_rows(piece, move)

    def all_groups(values):
        pieces = jnp.concatenate([to_owner(values, 0), to_owner(values, 1)], 1)
        total = pieces.astype(f32)
        for k in range(1, place.outer):
            total = total + place.other_outer(pieces, k).astype(f32)
        total = total.astype(bf16)
        return total[:, : values.shape[1]], total[:, values.shape[1] :]

    narrow_pieces = all_groups(narrow_all)
    wide_pieces = all_groups(wide_all)
    mine = place.f % place.shards // place.blocks
    choose_all = jnp.concatenate(
        [
            jnp.where(mine == 0, choosers[0], choosers[1]),
            jnp.where(mine == 0, choosers[1], choosers[0]),
        ],
        1,
    )

    def pick(pieces, index):
        return jnp.concatenate([p[:, index * rank : (index + 1) * rank] for p in pieces], 1)

    whole_count, part_count = 10, 8
    lora_a, lora_b, lora_a_down, lora_b_up = [], [], [], []
    for layer in range(layers):
        base = layer * whole_count
        q_a, k_a, v_a, cq_a, ck_a, cv_a, up_a, o_b, co_b, down_b = range(base, base + whole_count)
        base = layers * whole_count + layer * part_count
        o_a, co_a, q_b, k_b, v_b, cq_b, ck_b, cv_b = range(base, base + part_count)
        a_order = (q_a, k_a, v_a, o_a, cq_a, ck_a, cv_a, co_a, up_a)
        b_order = (q_b, k_b, v_b, o_b, cq_b, ck_b, cv_b, co_b, down_b)
        lora_a.append(jnp.stack([dot_nt(pick(narrow_pieces, k), choose_all) for k in a_order]))
        lora_b.append(jnp.stack([dot_nt(choose_all, pick(narrow_pieces, k)) for k in b_order]))
        lora_a_down.append(dot_nt(pick(wide_pieces, 2 * layer), choose_all))
        lora_b_up.append(dot_nt(choose_all, pick(wide_pieces, 2 * layer + 1)))

    grad_text = place.swap(place.scatter(grad_text).astype(bf16)).astype(f32)
    return (
        place.swap(state.astype(bf16)),
        place.swap(grad.astype(bf16)).astype(f32),
        grad_text.reshape(context.shape),
        jnp.stack(lora_a),
        jnp.stack(lora_a_down),
        jnp.stack(lora_b),
        jnp.stack(lora_b_up),
    )


def solution(mesh):
    rep, fsdp = AXES
    in_specs = (
        P(AXES, None),
        P(rep, fsdp, None),
        P(AXES, None),
        P(None, AXES),
        P(rep),
        P(rep),
        P(rep),
        P(rep, None, None),
        P(),
        P(),
        P(None, None, fsdp, None),
        P(None, None, fsdp, None),
        P(None, fsdp, None),
        P(None, fsdp, None),
        P(None, None, fsdp, None),
        P(None, fsdp, None),
        P(None, None, None, fsdp),
        P(None, None, fsdp),
    )
    out_specs = (
        P(AXES, None),
        P(AXES, None),
        P(rep, fsdp, None),
        P(None, None, fsdp, None),
        P(None, fsdp, None),
        P(None, None, None, fsdp),
        P(None, None, fsdp),
    )
    return jax.shard_map(
        on_device, mesh=mesh, in_specs=in_specs, out_specs=out_specs, check_vma=False
    )
```

```python
import functools
import math

import jax
import jax.numpy as jnp
from jax import lax
from jax.experimental import pallas as pl
from jax.experimental.pallas import tpu as pltpu
from jax.sharding import PartitionSpec as P

HD = 128
ADAPTER_RANK = 16
TENSOR = 4

AXES = ("o", "c", "z", "y")
epsilon = 1e-06
masked_score = -1e30
f32 = jnp.float32
bf16 = jnp.bfloat16
CHUNK = 256
SUBLANES = 8
BLOCK = 512
VMEM_BYTES = 32 << 20

NEAR = ((0, 0), (0, 1), (0, 2), (0, 4), (0, 5), (0, 6), (0, 8), (1, 3), (1, 7), (1, 8))
HEADS = ((0, 3), (0, 7), (1, 0), (1, 1), (1, 2), (1, 4), (1, 5), (1, 6))


def dot(left, right):
    return jnp.dot(left, right, preferred_element_type=f32)


def dot_nt(left, right):
    return lax.dot_general(left, right, (((1,), (1,)), ((), ())), preferred_element_type=f32)


def dot_tn(left, right):
    return lax.dot_general(left, right, (((0,), (0,)), ((), ())), preferred_element_type=f32)


class Place:
    def __init__(self):
        self.rep = lax.axis_size(AXES[0]) * lax.axis_size(AXES[1])
        self.planes = lax.axis_size(AXES[2])
        self.size = 2 * self.planes
        self.blocks = self.planes // self.rep
        self.shards = self.size // TENSOR
        self.o, self.c, self.z, self.y = [lax.axis_index(axis) for axis in AXES]
        self.g, self.b = self.z // self.blocks, self.z % self.blocks
        self.p = 2 * self.o + self.y

    def send(self, values, move):
        pairs = []
        for index in range(self.rep * self.size):
            rest, y = divmod(index, 2)
            rest, z = divmod(rest, self.planes)
            to = move(*divmod(rest, 2), *divmod(z, self.blocks), y)
            if to is not None:
                o, c, g, b, y = to
                target = ((2 * o + c) * self.planes + g * self.blocks + b) * 2 + y
                pairs.append((index, target))
        return lax.ppermute(values, AXES, pairs)

    def swap(self, values):
        return self.send(values, lambda o, c, g, b, y: (g // 2, g % 2, 2 * o + c, b, y))

    def part(self, values, k):
        return self.send(values, lambda o, c, g, b, y: (o ^ (k // 2), c, g, b, y ^ (k % 2)))

    def other_group(self, values, k):
        return self.send(values, lambda o, c, g, b, y: (o, c, g ^ k, b, y))

    def other_block(self, values, k):
        return self.send(values, lambda o, c, g, b, y: (o, c, g, b ^ k, y))

    def other_core(self, values):
        return self.send(values, lambda o, c, g, b, y: (o, 1 - c, g, b, y))

    def other_outer(self, values):
        return self.send(values, lambda o, c, g, b, y: (1 - o, c, g, b, y))

    def first_index(self, core, block, part):
        plane = (2 * (part // 2) + core) * self.blocks + block
        return 2 * plane + part % 2

    def gather(self, rows):
        cut = rows.shape[1] // 2
        one = self.part(rows, 1)
        two = self.part(rows, 2)
        return (rows, one, two, self.part(one[:, :cut], 2), self.part(two[:, cut:], 1))

    def scatter(self, parts):
        left_near, left_far, right_near, right_far = parts
        count = left_near.shape[0] // 2
        from_one = self.part(left_far, 1)
        from_two = self.part(right_far, 2)
        left = (left_near[count:].astype(f32) + from_one[count:].astype(f32)).astype(bf16)
        right = (right_near[count:].astype(f32) + from_two[count:].astype(f32)).astype(bf16)
        return (
            left_near, from_one, self.part(left, 2), right_near, from_two, self.part(right, 1)
        )

    def arrivals(self, stats):
        return [stats] + [self.part(stats, k) for k in range(1, TENSOR)]

    def spread(self, rows):
        own = [rows] + [self.other_block(rows, k) for k in range(1, self.blocks)]
        return own + [self.other_core(piece) for piece in own]

    def collect(self, pieces):
        total = [(piece,) for piece in pieces[: self.blocks]]
        total = [
            own + (self.other_core(piece.astype(bf16)),)
            for own, piece in zip(total, pieces[self.blocks :])
        ]
        if self.blocks == 1:
            return total[0]
        total = [sum(term.astype(f32) for term in terms) for terms in total]
        result = total[0]
        for k in range(1, self.blocks):
            result = result + self.other_block(total[k].astype(bf16), k).astype(f32)
        return (result,)

    def gather_planes(self, rows):
        return lax.all_gather(rows, (AXES[2], AXES[1]), axis=0, tiled=True)

    def fetch_columns(self, mine, there):
        arrived = self.send(
            there, lambda o, c, g, b, y: (o, c, g, b, 1 - y) if y == c else None
        )
        return jnp.where(self.y == self.c, mine, arrived)

    def fetch_heads(self, whole, first, matrices):
        count, wide = whole.shape[0] // TENSOR, whole.shape[1] - first
        pieces = []
        for k in range(TENSOR):
            piece = lax.dynamic_slice(whole, ((self.p ^ k) * count, first), (count, wide))
            pieces.append(self.part(piece, k) if k else piece)
        planes = self.planes // TENSOR
        rows = count // (planes * 2 * TENSOR)
        if rows % (2 * SUBLANES) == 0:
            return assemble(self.p, pieces, planes, matrices)
        result = jnp.zeros((planes, 2, 2, 2, rows, matrices, TENSOR, wide // matrices), bf16)
        for k, piece in enumerate(pieces):
            piece = piece.reshape(planes, 2, TENSOR, rows, matrices, wide // matrices)
            piece = piece.transpose(0, 1, 3, 4, 2, 5)[:, None, None]
            at = (0, self.y ^ (k % 2), self.o ^ (k // 2)) + (0,) * 5
            result = lax.dynamic_update_slice(result, piece, at)
        return result.reshape(count, TENSOR * wide)

    def in_order(self, pieces):
        whole = jnp.stack(pieces)
        if len(pieces) > 1:
            for k, piece in enumerate(pieces):
                whole = lax.dynamic_update_index_in_dim(whole, piece, self.b ^ k, 0)
        return whole

    def all_blocks(self, piece):
        return self.in_order([piece] + [self.other_block(piece, k) for k in range(1, self.blocks)])


def heads_share(matrices, share, shares):
    number, rows, width = matrices.shape
    piece = lax.dynamic_slice_in_dim(matrices, share * (rows // shares), rows // shares, 1)
    piece = piece.reshape(number, rows // shares, TENSOR, width // TENSOR).transpose(2, 1, 0, 3)
    return piece.reshape(TENSOR * (rows // shares), number * (width // TENSOR))


def assemble_kernel(planes, matrices, part, *refs):
    pieces, out = refs[:TENSOR], refs[TENSOR]
    count, wide = pieces[0].shape
    rows, one = count // (planes * 2 * TENSOR), wide // matrices
    for k, piece in enumerate(pieces):
        owner = part[0] ^ k
        place = (owner % 2) * 2 + owner // 2
        for plane in range(planes):
            for core in range(2):
                start = (plane * TENSOR + place) * 2 + core
                at = pl.ds(pl.multiple_of(start * rows, rows), rows)
                for group in range(TENSOR):
                    source = ((plane * 2 + core) * TENSOR + group) * rows
                    for m in range(matrices):
                        to = (m * TENSOR + group) * one
                        out[at, to : to + one] = piece[
                            source : source + rows, m * one : (m + 1) * one
                        ]


def assemble(part, pieces, planes, matrices):
    count, wide = pieces[0].shape
    return pl.pallas_call(
        functools.partial(assemble_kernel, planes, matrices),
        out_shape=jax.ShapeDtypeStruct((count, TENSOR * wide), bf16),
        in_specs=[pl.BlockSpec(memory_space=m) for m in [pltpu.SMEM] + [pltpu.VMEM] * TENSOR],
        out_specs=pl.BlockSpec(memory_space=pltpu.VMEM),
        compiler_params=pltpu.CompilerParams(vmem_limit_bytes=VMEM_BYTES),
        cost_estimate=pl.CostEstimate(
            flops=0, bytes_accessed=16 * count * wide, transcendentals=0
        ),
    )(part.astype(jnp.int32)[None], *pieces)


def rotary_tables(positions):
    pair_count = HD // 2
    third_part = pair_count // 3
    first_part = pair_count - 2 * third_part
    pieces = []
    for column, amount in ((0, first_part), (1, third_part), (2, third_part)):
        frequency = jnp.power(10000.0, -jnp.arange(amount, dtype=f32) / amount)
        pieces.append(positions[column].astype(f32)[:, None] * frequency[None, :])
    angles = jnp.repeat(jnp.concatenate(pieces, 1), 2, 1)
    sign = jnp.where(jnp.arange(HD) % 2 == 0, -1.0, 1.0)
    return jnp.cos(angles), jnp.sin(angles) * sign


def call(kernel, outs, args, scratch=(), flops=0, anywhere=()):
    outs = [jax.ShapeDtypeStruct(shape, dtype) for shape, dtype in outs]
    moved = sum(v.size * v.dtype.itemsize for v in list(args) + outs)
    space = [pl.ANY if k in anywhere else pltpu.VMEM for k in range(len(args))]
    return pl.pallas_call(
        kernel,
        out_shape=outs,
        in_specs=[pl.BlockSpec(memory_space=m) for m in space],
        out_specs=[pl.BlockSpec(memory_space=pltpu.VMEM) for _ in outs],
        scratch_shapes=list(scratch),
        compiler_params=pltpu.CompilerParams(vmem_limit_bytes=VMEM_BYTES),
        cost_estimate=pl.CostEstimate(flops=flops, bytes_accessed=moved, transcendentals=0),
    )(*args)


def part_shapes(rows, width):
    return [((rows // 2, width // 2), bf16)] * 4


def put_parts(parts, raw, inner, factors):
    count, half = raw.shape[0] // TENSOR, raw.shape[1] // 2
    for at in chunks(raw.shape[1]):
        values = (raw[:, at] + dot(inner, factors[:, at])).astype(bf16)
        right = at.start // half
        to = slice(at.start - right * half, at.stop - right * half)
        order = ((0, 1), (2, 3)) if right else ((0, 2), (1, 3))
        for ref, slots in zip(parts[2:] if right else parts[:2], order):
            for row, slot in enumerate(slots):
                ref[row * count : (row + 1) * count, to] = values[
                    slot * count : (slot + 1) * count
                ]


def join(pieces, full):
    own, one, two, left, right = pieces
    count, width = own.shape
    full[:count] = own[...]
    full[count : 2 * count] = one[...]
    full[2 * count : 3 * count] = two[...]
    full[3 * count :, : width // 2] = left[...]
    full[3 * count :, width // 2 :] = right[...]


def chunks(width):
    return [slice(start, start + CHUNK) for start in range(0, width, CHUNK)]


def turned(values):
    return values.astype(f32).T.astype(bf16)


def narrow(values, mask):
    return (values * mask).astype(bf16)


def row_sums(values):
    ones = jnp.ones((SUBLANES, values.shape[1]), bf16)
    high = values.astype(bf16)
    return dot_nt(ones, high) + dot_nt(ones, (values - high.astype(f32)).astype(bf16))


def as_columns(row, width):
    column = jnp.broadcast_to(row, (HD, row.shape[1])).T
    return jnp.concatenate([column] * (width // HD), 1)


def total_stats(refs):
    total = refs[0][...]
    count = total.shape[1] // TENSOR
    for k, ref in enumerate(refs):
        if k:
            order = [ref[:, (j ^ k) * count : ((j ^ k) + 1) * count] for j in range(TENSOR)]
            total = total + jnp.concatenate(order, 1)
    return total


def stat_rows(total, index):
    return total[index * SUBLANES : index * SUBLANES + 1]


def swap_pairs(values):
    lane = lax.broadcasted_iota(jnp.int32, values.shape, 1)
    return jnp.where(lane % 2 == 0, pltpu.roll(values, HD - 1, 1), pltpu.roll(values, 1, 1))


def rotate(values, cosine, sine):
    heads = [values[:, k : k + HD] for k in range(0, values.shape[1], HD)]
    return jnp.concatenate([v * cosine + swap_pairs(v) * sine for v in heads], 1)


def rotate_back(grad, cosine, sine):
    heads = [grad[:, k : k + HD] for k in range(0, grad.shape[1], HD)]
    return jnp.concatenate([v * cosine + swap_pairs(v * sine) for v in heads], 1)


def gelu_terms(x):
    slope = math.sqrt(2.0 / math.pi)
    square = x * x
    t = jnp.tanh(slope * x * (1.0 + 0.044715 * square))
    value = 0.5 * x * (1.0 + t)
    inner = slope * (1.0 + 3.0 * 0.044715 * square)
    return value, 0.5 * (1.0 + t) + 0.5 * x * (1.0 - t * t) * inner


def sum_terms(terms, count):
    sides = []
    for near, first, far in (terms[:3], terms[3:]):
        total = near[:count].astype(f32) + first[:count].astype(f32) + far[...].astype(f32)
        sides.append(total)
    return jnp.concatenate(sides, 1)


def advance_kernel(*refs):
    terms, (state, factor, scale, shift, new, normed) = refs[:6], refs[6:]
    value = state[...] + factor[...] * sum_terms(terms, state.shape[0])
    new[...] = value
    centred = value - jnp.mean(value, -1, keepdims=True)
    hat = centred * lax.rsqrt(jnp.mean(centred * centred, -1, keepdims=True) + epsilon)
    normed[...] = (hat * scale[...] + shift[...]).astype(bf16)


def advance(terms, state, factor, scale, shift):
    return call(
        advance_kernel, [(state.shape, f32), (state.shape, bf16)],
        (*terms, state, factor, scale, shift), flops=30 * state.size,
    )


def retreat_kernel(*refs):
    terms, (state, grad, scale, factor, new, out) = refs[:6], refs[6:]
    value = state[...]
    centred = value - jnp.mean(value, -1, keepdims=True)
    spread = lax.rsqrt(jnp.mean(centred * centred, -1, keepdims=True) + epsilon)
    hat = centred * spread
    inner = sum_terms(terms, value.shape[0]) * scale[...]
    along = jnp.mean(inner * hat, -1, keepdims=True)
    result = grad[...] + spread * (inner - jnp.mean(inner, -1, keepdims=True) - hat * along)
    new[...] = result
    out[...] = (result * factor[...]).astype(bf16)


def retreat(terms, state, grad, scale, factor):
    return call(
        retreat_kernel, [(state.shape, f32), (state.shape, bf16)],
        (*terms, state, grad, scale, factor), flops=40 * state.size,
    )


def pack_kernel(layer, squares, planes, *refs):
    part, square, wide = refs[:3]
    mine, there, held, sems = refs[3:]
    own = square.shape[3] // TENSOR
    copies = []
    if planes:
        whole = pltpu.make_async_copy(wide.at[layer], held, sems.at[2 * len(squares)])
        whole.start()
    for k, column in enumerate(squares):
        for side, out in enumerate((mine, there)):
            at = pl.ds(pl.multiple_of((part[0] ^ side) * own, own), own)
            copies.append(
                pltpu.make_async_copy(
                    square.at[layer, squares[column], :, at],
                    out.at[:, pl.ds(column, own)],
                    sems.at[2 * k + side],
                )
            )
            copies[-1].start()
    if planes:
        base, stop, count = planes
        one = held.shape[1] // (8 * count)
        step = (stop - base) // (2 * count)
        whole.wait()
        for out in (mine, there) if step > one else ():
            out[:, base:stop] = jnp.zeros((held.shape[0], stop - base), bf16)
        for k in range(TENSOR):

            @pl.when(part[0] == k)
            def _(k=k):
                for side, out in enumerate((mine, there)):
                    o, y = divmod(k ^ side, 2)
                    for z in range(2 * count):
                        at = (((z // 2) * 2 + y) * 4 + o * 2 + z % 2) * one
                        to = base + z * step
                        out[:, to : to + one] = held[:, at : at + one]

    for copy in copies:
        copy.wait()


def pack(part, square, wide, layer, width, squares, planes=None):
    rows = square.shape[2]
    scratch = [
        pltpu.VMEM(wide.shape[1:] if planes else (SUBLANES, HD), bf16),
        pltpu.SemaphoreType.DMA((2 * len(squares) + 1,)),
    ]
    return pl.pallas_call(
        functools.partial(pack_kernel, layer, squares, planes),
        out_shape=[jax.ShapeDtypeStruct((rows, width), bf16)] * 2,
        in_specs=[pl.BlockSpec(memory_space=m) for m in (pltpu.SMEM, pl.ANY, pl.ANY)],
        out_specs=[pl.BlockSpec(memory_space=pltpu.VMEM)] * 2,
        scratch_shapes=scratch,
        compiler_params=pltpu.CompilerParams(vmem_limit_bytes=VMEM_BYTES),
        cost_estimate=pl.CostEstimate(flops=0, bytes_accessed=8 * rows * width, transcendentals=0),
    )(part, square, wide)


def pick_kernel(seqs, near_list, heads_list, *refs):
    adapters, groups, firsts, seconds, wide_firsts, wide_seconds = refs[:6]
    near, heads, cat = refs[6:]
    rank = seqs * ADAPTER_RANK
    per = HD // rank
    layers, _, rows, _ = firsts.shape
    row = lax.broadcasted_iota(jnp.int32, (per * HD, HD), 0)
    column = lax.broadcasted_iota(jnp.int32, (per * HD, HD), 1)

    def one_hot(group):
        wanted = jnp.zeros_like(column)
        for s in range(seqs):
            here = (column // ADAPTER_RANK) % seqs == s
            wanted = jnp.where(here, adapters[group * seqs + s] * ADAPTER_RANK, wanted)
        wanted = wanted + column % ADAPTER_RANK + (column // rank) * HD
        return (row == wanted).astype(f32).astype(bf16)

    hots = [one_hot(groups[k]) for k in range(TENSOR + 2)]

    def blocks(items, count):
        for block in range(-(-len(items) // per)):
            here = items[block * per : (block + 1) * per]
            for k in range(per):
                at = slice(k * HD, (k + 1) * HD)
                if k < len(here):
                    ref, index = here[k]
                    cat[:count, at] = ref[index]
                else:
                    cat[:count, at] = jnp.zeros((count, HD), bf16)
            yield block, cat[:count]

    refs_of = (firsts, seconds)
    items = [(refs_of[w], (layer, i)) for layer in range(layers) for w, i in near_list]
    for block, values in blocks(items, rows):
        for k in range(TENSOR):
            near[k, block * rows : (block + 1) * rows] = dot(values, hots[k]).astype(bf16)
    base = -(-len(items) // per) * rows
    items = [(refs_of[w], (layer, i)) for layer in range(layers) for w, i in heads_list]
    for block, values in blocks(items, rows):
        for k in range(2):
            heads[k, block * rows : (block + 1) * rows] = dot(values, hots[TENSOR + k]).astype(bf16)
    units = wide_firsts.shape[1]
    items = [(ref, (layer,)) for layer in range(layers) for ref in (wide_firsts, wide_seconds)]
    for block, values in blocks(items, units):
        at = base + block * units
        for k in range(TENSOR):
            near[k, at : at + units] = dot(values, hots[k]).astype(bf16)


def pick(adapters, groups, firsts, seconds, wide_firsts, wide_seconds, seqs):
    layers, _, rows, _ = firsts.shape
    units = wide_firsts.shape[1]
    per = HD // (seqs * ADAPTER_RANK)
    near_rows = -(-layers * len(NEAR) // per) * rows + -(-layers * 2 // per) * units
    heads_rows = -(-layers * len(HEADS) // per) * rows
    space = [pltpu.SMEM] * 2 + [pltpu.VMEM] * 4
    return pl.pallas_call(
        functools.partial(pick_kernel, seqs, NEAR, HEADS),
        out_shape=[
            jax.ShapeDtypeStruct((TENSOR, near_rows, HD), bf16),
            jax.ShapeDtypeStruct((2, heads_rows, HD), bf16),
        ],
        in_specs=[pl.BlockSpec(memory_space=m) for m in space],
        out_specs=[pl.BlockSpec(memory_space=pltpu.VMEM)] * 2,
        scratch_shapes=[pltpu.VMEM((max(rows, units), per * HD), bf16)],
        compiler_params=pltpu.CompilerParams(vmem_limit_bytes=VMEM_BYTES),
        cost_estimate=pl.CostEstimate(flops=0, bytes_accessed=8 * near_rows * HD, transcendentals=0),
    )(adapters, groups, firsts, seconds, wide_firsts, wide_seconds)


def picked(ref, place, rank, count=1):
    return ref[place * rank : (place + count) * rank]


def ffn_kernel(places, *refs):
    pieces, (mask, near, far, w_in, w_out), refs = refs[:5], refs[5:10], refs[10:]
    parts, (up_raw, up_inner, down_inner), (full, raw, hidden) = refs[:4], refs[4:7], refs[7:]
    rank = mask.shape[1]
    width = full.shape[1]
    up_a, down_b, down_a, up_b = places
    join(pieces, full)
    raw[:, : w_in.shape[1]] = dot(full[...], w_in[...])
    inner = narrow(dot_nt(full[...], picked(near, up_a, rank)), mask[...])
    up_inner[...] = inner
    factors = picked(far, up_b, rank)
    for at in chunks(w_in.shape[1]):
        values = raw[:, at] + dot(inner, factors[:, at])
        up_raw[:, at] = values.astype(bf16)
        hidden[:, at] = gelu_terms(values)[0].astype(bf16)
    raw[:, :width] = dot(hidden[...], w_out[...])
    inner = narrow(dot_nt(hidden[...], picked(far, down_a, rank)), mask[...])
    down_inner[...] = inner
    put_parts(parts, raw.at[:, :width], inner, picked(near, down_b, rank))


def ffn(pieces, mask, near, far, w_in, w_out, places):
    count, width = pieces[0].shape
    rows, rank = mask.shape
    wide = w_in.shape[1]
    outs = part_shapes(rows, width) + [((rows, wide), bf16), ((rows, rank), bf16)]
    scratch = [
        pltpu.VMEM((rows, width), bf16),
        pltpu.VMEM((rows, max(wide, width)), f32),
        pltpu.VMEM((rows, wide), bf16),
    ]
    outs = call(
        functools.partial(ffn_kernel, places), outs + [((rows, rank), bf16)],
        (*pieces, mask, near, far, w_in, w_out), scratch, 4 * rows * width * wide,
    )
    return outs[:4], tuple(outs[4:])


def ffn_back_kernel(places, *refs):
    grads, inputs, refs = refs[:5], refs[5:10], refs[10:]
    up_raw, up_inner, down_inner, mask, near, far, w_in, w_out = refs[:8]
    parts, (a_down, b_up, a_up, b_down) = refs[8:12], refs[12:16]
    grad, full, raw, grad_up = refs[16:]
    rank = mask.shape[1]
    width = full.shape[1]
    at_up_a, at_down_b, at_down_a, at_up_b = places
    join(grads, grad)
    join(inputs, full)
    raw[:, : w_out.shape[0]] = dot_nt(grad[...], w_out[...])
    down_back = narrow(dot_nt(grad[...], picked(near, at_down_b, rank)), mask[...])
    down_turned = turned(down_back)
    up_turned = turned(up_inner[...])
    factors = picked(far, at_down_a, rank)
    for at in chunks(up_raw.shape[1]):
        hidden_grad = raw[:, at] + dot(down_back, factors[:, at])
        value, slope = gelu_terms(up_raw[:, at].astype(f32))
        raw_grad = (hidden_grad * slope).astype(bf16)
        grad_up[:, at] = raw_grad
        a_down[:, at] = dot(down_turned, value.astype(bf16)).astype(bf16)
        b_up[:, at] = dot(up_turned, raw_grad).astype(bf16)
    up_back = narrow(dot_nt(grad_up[...], picked(far, at_up_b, rank)), mask[...])
    raw[:, :width] = dot_nt(grad_up[...], w_in[...])
    put_parts(parts, raw.at[:, :width], up_back, picked(near, at_up_a, rank))
    a_up[...] = dot(turned(up_back), full[...]).astype(bf16)
    b_down[...] = dot(turned(down_inner[...]), grad[...]).astype(bf16)


def ffn_back(grads, inputs, saved, mask, near, far, w_in, w_out, places):
    count, width = grads[0].shape
    rows, rank = mask.shape
    wide = w_in.shape[1]
    outs = part_shapes(rows, width) + [((rank, n), bf16) for n in (wide, wide, width, width)]
    scratch = [
        pltpu.VMEM((rows, width), bf16),
        pltpu.VMEM((rows, width), bf16),
        pltpu.VMEM((rows, max(wide, width)), f32),
        pltpu.VMEM((rows, wide), bf16),
    ]
    outs = call(
        functools.partial(ffn_back_kernel, places), outs,
        (*grads, *inputs, *saved, mask, near, far, w_in, w_out), scratch,
        4 * rows * width * wide,
    )
    return outs[:4], outs[4:]


def project_kernel(start, count, normed, *refs):
    pieces, (mask, weights, near, heads), refs = refs[:5], refs[5:9], refs[9:]
    raws, (inner, stats, full, together) = refs[:count], refs[count:]
    own = raws[0].shape[1]
    rank = mask.shape[1]
    base, near_at, heads_at = start
    join(pieces, full)
    together[...] = dot(full[...], weights[:, base : base + count * own])
    inner[...] = narrow(
        dot_nt(full[...], picked(near, near_at, rank, count)),
        jnp.concatenate([mask[...]] * count, 1),
    )
    for k, raw in enumerate(raws):
        values = together[:, k * own : (k + 1) * own] + dot(
            inner[:, k * rank : (k + 1) * rank], picked(heads, heads_at + k, rank)
        )
        raw[...] = values.astype(raw.dtype)
        if k < normed:
            stats[k * SUBLANES : (k + 1) * SUBLANES] = row_sums(values * values)


def project(pieces, mask, weights, near, heads, start, count, normed):
    rows, rank = mask.shape
    own = heads.shape[1]
    outs = [((rows, own), f32 if k < normed else bf16) for k in range(count)]
    outs += [((rows, count * rank), bf16), ((normed * SUBLANES, rows), f32)]
    outs = call(
        functools.partial(project_kernel, start, count, normed), outs,
        (*pieces, mask, weights, near, heads),
        [pltpu.VMEM((rows, pieces[0].shape[1]), bf16), pltpu.VMEM((rows, count * own), f32)],
        2 * rows * weights.shape[0] * own * count,
    )
    return outs[:count], outs[count], outs[count + 1]


def scales_of(total, index, width, own):
    return as_columns(lax.rsqrt(stat_rows(total, index) / width + epsilon), own)


def normalize_kernel(count, turning, valued, width, *refs):
    raws, gains, refs = refs[:count], refs[count : 2 * count], refs[2 * count :]
    tables, refs = refs[: 2 * turning], refs[2 * turning :]
    value, refs = refs[:valued], refs[valued:]
    stats, outs, total = refs[: -count - 1], refs[-count - 1 : -1], refs[-1]
    total[...] = total_stats(stats)
    own = raws[0].shape[1]
    for k in range(count):
        values = raws[k][...] * scales_of(total, k, width, own) * gains[k][...]
        if turning:
            values = rotate(values, tables[0][...], tables[1][...])
        outs[k][:, :own] = values.astype(bf16)
    if valued:
        outs[-1][:, own:] = value[0][...]


def normalize(raws, gains, stats, width, tables=(), value=()):
    shape = raws[0].shape
    outs = [(shape, bf16) for _ in raws]
    if value:
        outs[-1] = ((shape[0], 2 * shape[1]), bf16)
    outs.append((stats[0].shape, f32))
    outs = call(
        functools.partial(normalize_kernel, len(raws), len(tables) // 2, len(value), width), outs,
        (*raws, *gains, *tables, *value, *stats), flops=20 * len(raws) * raws[0].size,
    )
    return outs[:-1], outs[-1]


def attend_kernel(count, start, *refs):
    query, marks, refs = refs[0], refs[1], refs[2:]
    pairs, key_marks, refs = refs[:count], refs[count : 2 * count], refs[2 * count :]
    mask, weights, near, heads = refs[:4]
    parts, result, inner, raw = refs[4:8], refs[8], refs[9], refs[10]
    rows, own = query.shape
    width, rank = near.shape[1], mask.shape[1]
    base, near_at, heads_at = start
    scale = 1.0 / math.sqrt(HD)
    block = min(BLOCK, rows)

    @pl.loop(0, rows // block)
    def _(index):
        at = pl.ds(pl.multiple_of(index * block, block), block)
        allowed = [marks[at] == key_mark[...] for key_mark in key_marks]
        for head in range(0, own, HD):
            scores = [
                jnp.where(
                    ok, dot_nt(query[at, head : head + HD], pair[:, head : head + HD]) * scale,
                    masked_score,
                )
                for ok, pair in zip(allowed, pairs)
            ]
            peak = functools.reduce(
                jnp.maximum, [jnp.max(s, -1, keepdims=True) for s in scores]
            )
            weighed = [jnp.exp(s - peak) for s in scores]
            total = sum(jnp.sum(w, -1, keepdims=True) for w in weighed)
            summed = sum(
                dot(w.astype(bf16), pair[:, own + head : own + head + HD])
                for w, pair in zip(weighed, pairs)
            )
            result[at, head : head + HD] = (summed / total).astype(bf16)

    raw[...] = dot(result[...], weights[:, base : base + width])
    inner[...] = narrow(dot_nt(result[...], picked(heads, heads_at, rank)), mask[...])
    put_parts(parts, raw, inner[...], picked(near, near_at, rank))


def attend(query, marks, pairs, key_marks, mask, weights, near, heads, start):
    rows, own = query.shape
    width, rank = near.shape[1], mask.shape[1]
    outs = part_shapes(rows, width) + [((rows, own), bf16), ((rows, rank), bf16)]
    keys = sum(pair.shape[0] for pair in pairs)
    outs = call(
        functools.partial(attend_kernel, len(pairs), start), outs,
        (query, marks, *pairs, *key_marks, mask, weights, near, heads),
        [pltpu.VMEM((rows, width), f32)], 4 * rows * keys * own + 2 * rows * own * width,
    )
    return outs[:4], outs[4], outs[5]


def attend_back_kernel(count, start, *refs):
    grads, (query, marks), refs = refs[:5], refs[5:7], refs[7:]
    pairs, key_marks, refs = refs[:count], refs[count : 2 * count], refs[2 * count :]
    (result, inner, mask, weights, near, heads), refs = refs[:6], refs[6:]
    base, near_at, heads_at = start
    grad_query, pair_grads, refs = refs[0], refs[1 : 1 + count], refs[1 + count :]
    a_grad, b_grad, grad, grad_out, raw = refs
    rows, own = query.shape
    rank = mask.shape[1]
    scale = 1.0 / math.sqrt(HD)
    block = min(BLOCK, rows)
    join(grads, grad)
    back = narrow(dot_nt(grad[...], picked(near, near_at, rank)), mask[...])
    raw[...] = dot_nt(grad[...], weights[:, base : base + grad.shape[1]])
    grad_out[...] = (raw[...] + dot(back, picked(heads, heads_at, rank))).astype(bf16)
    a_grad[...] = dot(turned(back), result[...]).astype(bf16)
    b_grad[...] = dot(turned(inner[...]), grad[...]).astype(bf16)
    for head in range(0, own, HD):
        here, there = slice(head, head + HD), slice(own + head, own + head + HD)
        keys_turned = [turned(pair[:, here]) for pair in pairs]
        for start in range(0, rows, block):
            at = slice(start, start + block)
            q, g = query[at, here], grad_out[at, here]
            scores = [
                jnp.where(
                    key_mark[...] == marks[:, at], dot_nt(pair[:, here], q) * scale, masked_score
                )
                for key_mark, pair in zip(key_marks, pairs)
            ]
            peak = functools.reduce(jnp.maximum, [jnp.max(s, 0, keepdims=True) for s in scores])
            weighed = [jnp.exp(s - peak) for s in scores]
            inverse = 1.0 / sum(jnp.sum(w, 0, keepdims=True) for w in weighed)
            probs = [w * inverse for w in weighed]
            along = [dot_nt(pair[:, there], g) for pair in pairs]
            delta = sum(jnp.sum(p * d, 0, keepdims=True) for p, d in zip(probs, along))
            turned_grad = 0.0
            for k in range(count):
                score_grad = (probs[k] * (along[k] - delta)).astype(bf16)
                key_grad = dot(score_grad, q) * scale
                value_grad = dot(probs[k].astype(bf16), g)
                if start:
                    key_grad = key_grad + pair_grads[k][:, here]
                    value_grad = value_grad + pair_grads[k][:, there]
                pair_grads[k][:, here] = key_grad
                pair_grads[k][:, there] = value_grad
                turned_grad = turned_grad + dot(keys_turned[k], score_grad)
            grad_query[at, here] = (turned_grad * scale).T


def attend_back(
    grads, query, marks, pairs, key_marks, result, inner, mask, weights, near, heads, start
):
    rows, own = query.shape
    width, rank = near.shape[1], mask.shape[1]
    outs = [((rows, own), f32)] + [(pair.shape, f32) for pair in pairs]
    outs += [((rank, own), bf16), ((rank, width), bf16)]
    keys = sum(pair.shape[0] for pair in pairs)
    outs = call(
        functools.partial(attend_back_kernel, len(pairs), start), outs,
        (*grads, query, marks, *pairs, *key_marks, result, inner, mask, weights, near, heads),
        [
            pltpu.VMEM((rows, width), bf16), pltpu.VMEM((rows, own), bf16),
            pltpu.VMEM((rows, own), f32),
        ],
        10 * rows * keys * own + 2 * rows * own * width,
    )
    return outs[0], outs[1:-2], outs[-2], outs[-1]


def back_stats_kernel(counts, turning, valued, width, *refs):
    number = len(counts)
    terms = []
    for count in counts:
        terms.append(refs[:count])
        refs = refs[count:]
    raws, gains, refs = refs[:number], refs[number : 2 * number], refs[2 * number :]
    tables, refs = refs[: 2 * turning], refs[2 * turning :]
    total, outs, stats = refs[0], refs[1:-1], refs[-1]
    own = raws[0].shape[1]
    for k in range(number):
        grad = sum(term[:, :own].astype(f32) for term in terms[k])
        if turning:
            grad = rotate_back(grad, tables[0][...], tables[1][...])
        grad = grad * gains[k][...]
        outs[k][...] = grad
        hat = raws[k][...] * scales_of(total, k, width, own)
        stats[k * SUBLANES : (k + 1) * SUBLANES] = row_sums(hat * grad)
    if valued:
        outs[-1][...] = sum(term[:, own:].astype(f32) for term in terms[-1]).astype(bf16)


def back_stats(terms, raws, gains, total, width, tables=(), valued=False):
    shape = raws[0].shape
    outs = [(shape, f32) for _ in raws] + [(shape, bf16)] * valued + [(total.shape, f32)]
    outs = call(
        functools.partial(
            back_stats_kernel, tuple(len(t) for t in terms), len(tables) // 2, int(valued), width
        ),
        outs, (*[term for t in terms for term in t], *raws, *gains, *tables, total),
        flops=30 * len(raws) * raws[0].size,
    )
    return outs[:-1], outs[-1]


def project_back_kernel(start, count, normed, parted, *refs):
    scaled, raws, refs = refs[:count], refs[count : count + normed], refs[count + normed :]
    total, (inner, mask, weights, near, heads), refs = refs[0], refs[1:6], refs[6:]
    inputs, refs = refs[:5], refs[5:]
    split = 4 if parted else 1
    stats, refs = refs[: -6 - split], refs[-6 - split :]
    outs, (a_grad, b_grad, full, grads, back, raw) = refs[:split], refs[split:]
    own = scaled[0].shape[1]
    width = full.shape[1]
    rank = mask.shape[1]
    base, near_at, heads_at = start
    join(inputs, full)
    along = total_stats(stats)
    for k in range(count):
        if k < normed:
            scale = scales_of(total, k, width, own)
            hat = raws[k][...] * scale
            mean = as_columns(stat_rows(along, k) / width, own)
            grads[:, k * own : (k + 1) * own] = (scale * (scaled[k][...] - hat * mean)).astype(bf16)
        else:
            grads[:, k * own : (k + 1) * own] = scaled[k][...]
    inner_turned = turned(inner[...])
    for k in range(count):
        at = slice(k * rank, (k + 1) * rank)
        grad = grads[:, k * own : (k + 1) * own]
        back[:, at] = narrow(dot_nt(grad, picked(heads, heads_at + k, rank)), mask[...])
        b_grad[at] = dot(inner_turned[at], grad).astype(bf16)
    a_grad[...] = dot(turned(back[...]), full[...]).astype(bf16)
    raw[...] = dot_nt(grads[...], weights[:, base : base + count * own])
    factors = picked(near, near_at, rank, count)
    if parted:
        put_parts(outs, raw, back[...], factors)
    else:
        for at in chunks(width):
            outs[0][:, at] = raw[:, at] + dot(back[...], factors[:, at])


def project_back(
    scaled, raws, total, stats, inner, mask, weights, near, heads, inputs, start, parted=True
):
    count, normed = len(scaled), len(raws)
    rows, own = scaled[0].shape
    width, rank = weights.shape[0], mask.shape[1]
    outs = part_shapes(rows, width) if parted else [((rows, width), f32)]
    split = len(outs)
    outs = outs + [((count * rank, width), bf16), ((count * rank, own), bf16)]
    scratch = [
        pltpu.VMEM((rows, width), bf16),
        pltpu.VMEM((rows, count * own), bf16),
        pltpu.VMEM((rows, count * rank), bf16),
        pltpu.VMEM((rows, width), f32),
    ]
    outs = call(
        functools.partial(project_back_kernel, start, count, normed, parted), outs,
        (*scaled, *raws, total, inner, mask, weights, near, heads, *inputs, *stats), scratch,
        2 * rows * width * own * count,
    )
    return outs[:split], outs[split], outs[split + 1]


def on_device(
    tokens,
    context,
    cotangent,
    positions,
    sequence_lengths,
    sequence_adapter,
    text_token_count,
    timestep_modulation,
    modulation,
    gains,
    query_key_value_weight,
    output_weight,
    up_weight,
    down_weight,
    first_factors,
    down_first_factor,
    second_factors,
    up_second_factor,
):
    place = Place()
    rows, width = tokens.shape
    seq_count, text_local = context.shape[:2]
    layers = query_key_value_weight.shape[0]
    columns = first_factors.shape[3]
    rank = seq_count * ADAPTER_RANK
    own = width // TENSOR
    wide = up_weight.shape[2] // TENSOR
    padded = -(-wide // CHUNK) * CHUNK
    set_rows = TENSOR * rows

    numbers = jnp.concatenate([positions.reshape(-1), sequence_lengths, text_token_count])
    numbers = place.swap(numbers)
    state = place.swap(tokens).astype(f32)
    times = place.swap(timestep_modulation)
    positions = numbers[: 3 * rows].reshape(3, rows)
    lengths, counts = [
        numbers[3 * rows + k * seq_count : 3 * rows + (k + 1) * seq_count] for k in range(2)
    ]

    bounds = jnp.cumsum(lengths)

    def token_segments(index):
        packed = jnp.arange(rows, dtype=jnp.int32) * place.size + index
        return jnp.sum((packed[:, None] >= bounds[None, :]).astype(jnp.int32), 1)

    def text_marks(index):
        at = index * text_local + jnp.arange(text_local)
        marks = jnp.where(at[None, :] < counts[:, None], jnp.arange(seq_count)[:, None], -1)
        return marks.reshape(-1)

    def over_set(function, core, block):
        return jnp.concatenate(
            [function(place.first_index(core, block, place.p ^ k)) for k in range(TENSOR)]
        )

    def over_group(function):
        return [
            over_set(function, core, place.b ^ k)
            for core in (place.c, 1 - place.c)
            for k in range(place.blocks)
        ]

    segment = over_set(token_segments, place.c, place.b)
    sequence = jnp.minimum(segment, seq_count - 1)
    self_marks = over_group(token_segments)
    cross_marks = over_group(text_marks)
    column_sequence = jnp.arange(rank) // ADAPTER_RANK
    mask = (sequence[:, None] == column_sequence[None, :]) & (segment < seq_count)[:, None]
    mask = mask.astype(f32)
    text_sequence = jnp.tile(jnp.repeat(jnp.arange(seq_count), text_local), TENSOR)
    text_mask = (text_sequence[:, None] == column_sequence[None, :]).astype(f32)
    valid = (segment[:rows] < seq_count).astype(f32)[:, None]

    def mods_of(layer):
        table = modulation[layer][None] + times
        chosen = [table[0, k][None] for k in range(6)]
        for s in range(1, seq_count):
            here = (sequence[:rows] == s)[:, None]
            chosen = [jnp.where(here, table[s, k][None], chosen[k]) for k in range(6)]
        return chosen

    def own_gain(layer, index):
        return lax.dynamic_slice_in_dim(gains[layer, index], place.p * own, own, 0)[None]

    table = jnp.zeros((place.rep, seq_count), jnp.int32)
    for k in range(2):
        arrived = sequence_adapter if k == 0 else place.other_outer(sequence_adapter)
        for m, values in enumerate((arrived, place.other_core(arrived))):
            here = jnp.arange(place.rep) == 2 * (place.o ^ k) + (place.c ^ m)
            table = jnp.where(here[:, None], values[None], table)
    half_units = down_first_factor.shape[1] // 2
    wanted = [place.g ^ k for k in range(TENSOR)] + [place.p, place.p ^ 1]
    near_share, heads_pick = pick(
        table.reshape(-1),
        jnp.stack(wanted).astype(jnp.int32),
        first_factors,
        second_factors.transpose(0, 1, 3, 2),
        lax.dynamic_slice_in_dim(down_first_factor, place.o * half_units, half_units, 1),
        lax.dynamic_slice_in_dim(
            up_second_factor.transpose(0, 2, 1), place.o * half_units, half_units, 1
        ),
        seq_count,
    )
    shard_rows = first_factors.shape[2]
    wide_blocks = -(-layers * 2 * rank // HD)
    near_rows = near_share.shape[1] - wide_blocks * half_units
    from_groups = [near_share[0]]
    from_groups += [place.other_group(near_share[k], k) for k in range(1, TENSOR)]
    from_groups = [place.all_blocks(piece) for piece in from_groups]
    own_rows = jnp.stack([piece[:, :near_rows] for piece in from_groups])
    other_rows = place.part(own_rows, 1)
    near = jnp.zeros((place.rep, 2) + own_rows.shape[1:], bf16)
    far = jnp.zeros((place.rep, place.blocks, wide_blocks * half_units, HD), bf16)
    for k in range(TENSOR):
        for rows_of, y in ((own_rows, place.y), (other_rows, 1 - place.y)):
            near = lax.dynamic_update_slice(
                near, rows_of[k][None, None], (place.g ^ k, y, 0, 0, 0)
            )
        far = lax.dynamic_update_slice(
            far, from_groups[k][None, :, near_rows:], (place.g ^ k, 0, 0, 0)
        )
    near = near.reshape(place.rep, 2, place.blocks, -1, shard_rows, HD)
    near = near.transpose(0, 2, 1, 4, 3, 5).reshape(width, -1).T
    far = far.reshape(place.planes, wide_blocks, half_units, HD).transpose(0, 2, 1, 3)
    far = far.reshape(wide, wide_blocks * HD)
    far = far.reshape(place.size, -1, wide_blocks * HD)
    far = jnp.pad(far, ((0, 0), (0, (padded - wide) // place.size), (0, 0))).reshape(padded, -1).T
    arrived = place.part(heads_pick[1], 1)
    heads_pick = jnp.where(
        place.y == 0, jnp.stack([heads_pick[0], arrived]), jnp.stack([arrived, heads_pick[0]])
    )
    heads_pick = place.send(
        heads_pick, lambda o, c, g, b, y: (g // 2, c, 2 * o + y, b, g % 2)
    )
    heads_pick = place.all_blocks(heads_pick).reshape(place.blocks, 2, -1, shard_rows, HD)
    far_heads = heads_pick.transpose(0, 1, 3, 2, 4).reshape(own, -1).T

    up_at = 6 * own
    part = place.p.astype(jnp.int32)[None]
    share = 2 * place.o + place.c

    def tied(value, after):
        return value if after is None else lax.optimization_barrier((value, after))[0]

    def fetch_self(layer, after, ready=None):
        mine, there = pack(
            tied(part, after), query_key_value_weight, up_weight, layer, 3 * own,
            {k * own: k for k in range(3)},
        )
        rows = place.fetch_columns(mine, there)
        piece = heads_share(output_weight[layer], share, place.rep)
        whole = place.gather_planes(tied(jnp.concatenate([rows, piece], 1), ready))
        return whole, place.fetch_heads(whole, 3 * own, 2)

    def fetch_others(layer, after):
        mine, there = pack(
            tied(part, after), query_key_value_weight, up_weight, layer, 3 * own + padded,
            {k * own: 3 + k for k in range(3)}, (3 * own, 3 * own + padded, place.planes),
        )
        rows = place.fetch_columns(mine, there)
        cross = place.gather_planes(rows[:, : 3 * own])
        up = place.gather_planes(rows[:, 3 * own :])
        count = down_weight.shape[1] // place.rep
        piece = lax.dynamic_slice(
            down_weight, (layer, share * count, 0), (1, count, width)
        )[0]
        piece = jnp.pad(piece, ((0, padded // place.size - count), (0, 0)))
        return cross, up, place.gather_planes(tied(piece, rows))

    positions = jnp.stack([positions] + [place.part(positions, k) for k in range(1, TENSOR)], 1)
    tables = rotary_tables(positions.reshape(3, set_rows))

    def arrivals(stats):
        arrived = place.arrivals(stats)
        count = stats.shape[1] // TENSOR
        if count % HD == 0:
            return arrived
        pieces = [v.reshape(-1, TENSOR, count) for v in arrived]
        total = sum(
            jnp.stack([v[:, j ^ k] for j in range(TENSOR)], 1) for k, v in enumerate(pieces)
        )
        return [total.reshape(stats.shape)]

    columns_of = [v.reshape(-1, 1) for v in (segment, sequence)]
    rows_of = [v.reshape(1, -1) for v in (segment, sequence)]
    self_rows, cross_rows = [[v.reshape(1, -1) for v in m] for m in (self_marks, cross_marks)]
    self_columns, cross_columns = [
        [v.reshape(-1, 1) for v in m] for m in (self_marks, cross_marks)
    ]
    zero_row = jnp.zeros((1, width), f32)
    starts = []
    for layer in range(layers):
        one, two, three = layer * len(NEAR), layer * len(HEADS), 2 * layer
        starts.append(
            (
                (0, one, two + 2), (0, one + 7, two), (0, one + 3, two + 5), (own, one + 4, two + 6),
                (width, one + 8, two + 1), (one + 6, one + 9, three, three + 1),
            )
        )

    saved = []
    factors = []
    for layer in range(layers):
        shift_one, scale_one, gate_one, shift_two, scale_two, gate_two = mods_of(layer)
        factors.append((valid * gate_one, valid * gate_two, 1.0 + scale_one, 1.0 + scale_two))
        factors[-1] += (shift_one, shift_two)
    valid_rows = jnp.broadcast_to(valid, (rows, width))
    centred = state - jnp.mean(state, -1, keepdims=True)
    hat = centred * lax.rsqrt(jnp.mean(centred * centred, -1, keepdims=True) + epsilon)
    normed = (hat * factors[0][2] + factors[0][4]).astype(bf16)
    fetched = []
    coming = fetch_self(0, None, (state, numbers, times, from_groups))
    others = None
    for layer in range(layers):
        gate_one, gate_two, scale_one, scale_two, shift_one, shift_two = factors[layer]
        in_at, out_at, cross_at, text_at, crossed_at, ffn_at = starts[layer]
        self_in, heads = coming
        self_pieces = place.gather(normed)
        if layer == 0:
            others = fetch_others(layer, self_pieces[3])
            text = tied(context.reshape(seq_count * text_local, width), self_pieces[3])
            text = place.gather(place.swap(text))
        cross_in, ffn_in, ffn_out = others
        raws, self_inner, stats = project(self_pieces, mask, self_in, near, far_heads, in_at, 3, 2)
        gain = [own_gain(layer, k) for k in range(4)]
        (query, pair), self_total = normalize(
            raws[:2], gain[:2], arrivals(stats), width, tables, raws[2:]
        )
        pairs = place.spread(pair)
        if layer + 1 < layers:
            coming = fetch_self(layer + 1, query)
        parts, attended, out_inner = attend(
            query, columns_of[0], pairs, self_rows, mask, heads, near, far_heads, out_at
        )
        self_saved = (self_pieces, raws, self_inner, self_total, query, pairs, attended, out_inner)
        state_one, normed = advance(
            place.scatter(parts), state, gate_one, gains[layer, 4][None], zero_row
        )

        text_raws, text_inner, stats = project(
            text, text_mask, cross_in, near, far_heads, text_at, 2, 1
        )
        (pair,), text_total = normalize(
            text_raws[:1], gain[3:], arrivals(stats), width, (), text_raws[1:]
        )
        pairs = place.spread(pair)
        cross_pieces = place.gather(normed)
        if layer + 1 < layers:
            others = fetch_others(layer + 1, cross_pieces[3])
        else:
            cotangent = place.swap(tied(cotangent, cross_pieces[3]))
        raws, cross_inner, stats = project(
            cross_pieces, mask, cross_in, near, far_heads, cross_at, 1, 1
        )
        (query,), cross_total = normalize(raws, gain[2:3], arrivals(stats), width)
        parts, crossed, crossed_inner = attend(
            query, columns_of[1], pairs, cross_rows, mask, heads, near, far_heads, crossed_at
        )
        cross_saved = (
            cross_pieces, raws, cross_inner, cross_total, query, pairs, crossed, crossed_inner
        )
        state_two, normed = advance(
            place.scatter(parts), state_one, valid_rows, scale_two, shift_two
        )

        ffn_pieces = place.gather(normed)
        parts, ffn_saved = ffn(ffn_pieces, mask, near, far, ffn_in, ffn_out, ffn_at)
        fetched.append((self_in, heads, cross_in, ffn_in, ffn_out))
        saved.append(
            (
                (state, state_one, state_two), self_saved, cross_saved,
                (text_raws, text_inner, text_total), (ffn_pieces, ffn_saved), gain,
            )
        )
        following = factors[min(layer + 1, layers - 1)]
        state, normed = advance(
            place.scatter(parts), state_two, gate_two, following[2], following[4]
        )

    grad = cotangent.astype(f32)
    out = (grad * factors[-1][1]).astype(bf16)
    grad_text = 0.0
    whole_grads, part_grads, wide_grads = [], [], []
    for layer in reversed(range(layers)):
        self_in, heads, cross_in, ffn_in, ffn_out = fetched[layer]
        gate_one, gate_two, scale_one, scale_two, shift_one, shift_two = factors[layer]
        (
            (state_zero, state_one, state_two), self_saved, cross_saved,
            (text_raws, text_inner, text_total), (ffn_pieces, ffn_saved), gain,
        ) = saved[layer]
        in_at, out_at, cross_at, text_at, crossed_at, ffn_at = starts[layer]
        parts, (down_a, up_b, up_a, down_b) = ffn_back(
            place.gather(out), ffn_pieces, ffn_saved, mask, near, far, ffn_in, ffn_out, ffn_at
        )
        grad, out = retreat(place.scatter(parts), state_two, grad, scale_two, valid_rows)

        pieces, raws, inner, total, query, pairs, result, result_inner = cross_saved
        grad_query, pair_grads, cross_out_a, cross_out_b = attend_back(
            place.gather(out), query, rows_of[1], pairs, cross_columns, result, result_inner,
            mask, heads, near, far_heads, crossed_at,
        )
        scaled, stats = back_stats([(grad_query,)], raws, gain[2:3], total, width)
        parts, cross_a, cross_b = project_back(
            scaled, raws, total, arrivals(stats), inner, mask, cross_in, near, far_heads, pieces,
            cross_at,
        )
        terms = place.collect(pair_grads)
        scaled, stats = back_stats([terms], text_raws[:1], gain[3:], text_total, width, (), True)
        (text_grad,), text_a, text_b = project_back(
            scaled, text_raws[:1], text_total, arrivals(stats), text_inner, text_mask, cross_in,
            near, far_heads, text, text_at, False,
        )
        grad_text = grad_text + text_grad
        grad, out = retreat(
            place.scatter(parts), state_one, grad, gains[layer, 4][None], gate_one
        )

        pieces, raws, inner, total, query, pairs, result, result_inner = self_saved
        grad_query, pair_grads, self_out_a, self_out_b = attend_back(
            place.gather(out), query, rows_of[0], pairs, self_columns, result, result_inner,
            mask, heads, near, far_heads, out_at,
        )
        terms = place.collect(pair_grads)
        scaled, stats = back_stats(
            [(grad_query,), terms], raws[:2], gain[:2], total, width, tables, True
        )
        parts, self_a, self_b = project_back(
            scaled, raws[:2], total, arrivals(stats), inner, mask, self_in, near, far_heads, pieces,
            in_at,
        )
        gate = factors[max(layer - 1, 0)][1]
        grad, out = retreat(place.scatter(parts), state_zero, grad, scale_one, gate)

        whole_grads.append(
            jnp.concatenate([self_a, cross_a, text_a, up_a, self_out_b, cross_out_b, down_b], 0)
        )
        part_grads.append(
            jnp.concatenate([self_out_a, cross_out_a, self_b, cross_b, text_b], 0)
        )
        wide_grad = jnp.concatenate([down_a, up_b], 0).reshape(2 * rank, place.size, -1)
        wide_grads.append(wide_grad[:, :, : wide // place.size].reshape(2 * rank, wide))

    def flat(lists):
        return jnp.concatenate(lists[::-1], 0).T

    grad_text = grad_text.astype(bf16)
    count, half = grad_text.shape[0] // TENSOR, width // 2
    slots = [grad_text[k * count : (k + 1) * count] for k in range(TENSOR)]
    text_parts = [
        jnp.concatenate([v[:, at] for v in pair], 0)
        for at, pair in (
            (slice(0, half), (slots[0], slots[2])),
            (slice(0, half), (slots[1], slots[3])),
            (slice(half, width), (slots[0], slots[1])),
            (slice(half, width), (slots[2], slots[3])),
        )
    ]

    def added(terms):
        left, one, two, right, three, four = [v.astype(f32) for v in terms]
        count = two.shape[0]
        return jnp.concatenate(
            [left[:count] + one[:count] + two, right[:count] + three[:count] + four], 1
        )

    whole_all = flat(whole_grads)
    whole_wide = whole_all.shape[1]
    whole_all = whole_all.reshape(place.planes, 2, 2, -1, whole_wide)
    slots = [
        lax.dynamic_slice(
            whole_all,
            (0, (place.p ^ k) % 2, (place.p ^ k) // 2, 0, 0),
            (place.planes, 1, 1) + whole_all.shape[3:],
        ).reshape(-1, whole_wide)
        for k in range(TENSOR)
    ]
    count, half = slots[0].shape[0], whole_wide // 2
    from_parts = added(
        place.scatter(
            [
                jnp.concatenate([v[:, at] for v in pair], 0)
                for at, pair in (
                    (slice(0, half), (slots[0], slots[2])),
                    (slice(0, half), (slots[1], slots[3])),
                    (slice(half, whole_wide), (slots[0], slots[1])),
                    (slice(half, whole_wide), (slots[2], slots[3])),
                )
            ]
        )
    )

    def sum_set(values):
        values = values.astype(f32) + place.other_core(values.astype(bf16)).astype(f32)
        result = values
        for k in range(1, place.blocks):
            result = result + place.other_block(values.astype(bf16), k).astype(f32)
        return result.astype(bf16)

    def to_owner(values):
        planes = values.reshape(place.planes, -1, values.shape[1])
        pieces = []
        for k in range(place.rep):
            plane = (place.g ^ k) * place.blocks + place.b
            piece = lax.dynamic_index_in_dim(planes, plane, 0, False)
            pieces.append(place.other_group(piece, k) if k else piece)
        near = jnp.concatenate(pieces, 1)
        other = place.other_outer(near)
        low = jnp.where(place.o == 0, near, other)
        high = jnp.where(place.o == 0, other, near)
        return jnp.split(jnp.concatenate([low, high], 0), place.rep, 1)

    def heads_to_owner(values):
        planes = values.reshape(place.blocks, -1, values.shape[1])
        mine = lax.dynamic_index_in_dim(planes, place.b, 0, False)
        mine = place.send(mine, lambda o, c, g, b, y: (g // 2, c, 2 * o + y, b, g % 2))
        mine = mine.reshape(2, -1, values.shape[1])
        pieces = []
        for k in range(TENSOR):
            piece = lax.dynamic_index_in_dim(mine, (place.y ^ k) % 2, 0, False)
            pieces.append(place.part(piece, k) if k else piece)
        return pieces

    whole_pieces = to_owner(sum_set(from_parts))
    part_pieces = heads_to_owner(sum_set(flat(part_grads)))
    wide_pieces = to_owner(sum_set(flat(wide_grads)))

    def chooser(adapters):
        column = (adapters[:, None] * ADAPTER_RANK + jnp.arange(ADAPTER_RANK)[None, :]).reshape(-1)
        return (jnp.arange(columns)[:, None] == column[None, :]).astype(bf16)

    def choosers(first):
        return jnp.concatenate(
            [
                chooser(lax.dynamic_index_in_dim(table, first ^ k, 0, False))
                for k in range(place.rep)
            ],
            1,
        )

    choose_near = choosers(place.g)
    choose_heads = choosers(place.p)

    def of_index(pieces, index):
        return jnp.concatenate([p[:, index * rank : (index + 1) * rank] for p in pieces], 1)

    whole_count, part_count = 10, 8
    lora_a, lora_b, lora_a_down, lora_b_up = [], [], [], []
    for layer in range(layers):
        near = [of_index(whole_pieces, layer * whole_count + k) for k in range(whole_count)]
        far = [of_index(part_pieces, layer * part_count + k) for k in range(part_count)]
        q_a, k_a, v_a, cq_a, ck_a, cv_a, up_a, o_b, co_b, down_b = near
        o_a, co_a, q_b, k_b, v_b, cq_b, ck_b, cv_b = far
        a_all = [(v, choose_near) for v in (q_a, k_a, v_a, cq_a, ck_a, cv_a, up_a)]
        a_all = a_all[:3] + [(o_a, choose_heads)] + a_all[3:6] + [(co_a, choose_heads)] + a_all[6:]
        b_all = [(v, choose_heads) for v in (q_b, k_b, v_b, cq_b, ck_b, cv_b)]
        b_all = b_all[:3] + [(o_b, choose_near)] + b_all[3:]
        b_all = b_all + [(co_b, choose_near), (down_b, choose_near)]
        lora_a.append(jnp.stack([dot_nt(v, chosen) for v, chosen in a_all]))
        lora_b.append(jnp.stack([dot_nt(chosen, v) for v, chosen in b_all]))
        lora_a_down.append(dot_nt(of_index(wide_pieces, 2 * layer), choose_near))
        lora_b_up.append(dot_nt(choose_near, of_index(wide_pieces, 2 * layer + 1)))

    grad_text = added(place.scatter(text_parts))
    grad_text = place.swap(grad_text.astype(bf16)).astype(f32)
    return (
        place.swap(state.astype(bf16)),
        place.swap(grad.astype(bf16)).astype(f32),
        grad_text.reshape(context.shape),
        jnp.stack(lora_a),
        jnp.stack(lora_a_down),
        jnp.stack(lora_b),
        jnp.stack(lora_b_up),
    )


def solution(mesh):
    rep, fsdp = AXES[:2], AXES[2:]
    sizes = (mesh.shape["rep"] // 2, 2, mesh.shape["fsdp"] // 2, 2)
    mesh = jax.sharding.Mesh(mesh.devices.reshape(sizes), AXES)
    in_specs = (
        P(AXES, None),
        P(rep, fsdp, None),
        P(AXES, None),
        P(None, AXES),
        P(rep),
        P(rep),
        P(rep),
        P(rep, None, None),
        P(),
        P(),
        P(None, None, fsdp, None),
        P(None, None, fsdp, None),
        P(None, fsdp, None),
        P(None, fsdp, None),
        P(None, None, fsdp, None),
        P(None, fsdp, None),
        P(None, None, None, fsdp),
        P(None, None, fsdp),
    )
    out_specs = (
        P(AXES, None),
        P(AXES, None),
        P(rep, fsdp, None),
        P(None, None, fsdp, None),
        P(None, fsdp, None),
        P(None, None, None, fsdp),
        P(None, None, fsdp),
    )
    return jax.shard_map(
        on_device, mesh=mesh, in_specs=in_specs, out_specs=out_specs, check_vma=False
    )
```

```python
import functools
import math

import jax
import jax.numpy as jnp
from jax import lax
from jax.experimental import pallas as pl
from jax.experimental.pallas import tpu as pltpu
from jax.sharding import PartitionSpec as P

HD = 128
ADAPTER_RANK = 16
TENSOR = 4

AXES = ("o", "c", "z", "y")
epsilon = 1e-06
masked_score = -1e30
f32 = jnp.float32
bf16 = jnp.bfloat16
CHUNK = 256
SUBLANES = 8
BLOCK = 512
VMEM_BYTES = 56 << 20

NEAR = ((0, 0), (0, 1), (0, 2), (0, 4), (0, 5), (0, 6), (0, 8), (1, 3), (1, 7), (1, 8))
HEADS = ((0, 3), (0, 7), (1, 0), (1, 1), (1, 2), (1, 4), (1, 5), (1, 6))


def dot(left, right):
    return jnp.dot(left, right, preferred_element_type=f32)


def dot_nt(left, right):
    return lax.dot_general(left, right, (((1,), (1,)), ((), ())), preferred_element_type=f32)


def dot_tn(left, right):
    return lax.dot_general(left, right, (((0,), (0,)), ((), ())), preferred_element_type=f32)


class Place:
    def __init__(self):
        self.rep = lax.axis_size(AXES[0]) * lax.axis_size(AXES[1])
        self.planes = lax.axis_size(AXES[2])
        self.size = 2 * self.planes
        self.blocks = self.planes // self.rep
        self.shards = self.size // TENSOR
        self.o, self.c, self.z, self.y = [lax.axis_index(axis) for axis in AXES]
        self.g, self.b = self.z // self.blocks, self.z % self.blocks
        self.p = 2 * self.o + self.y

    def send(self, values, move):
        pairs = []
        for index in range(self.rep * self.size):
            rest, y = divmod(index, 2)
            rest, z = divmod(rest, self.planes)
            to = move(*divmod(rest, 2), *divmod(z, self.blocks), y)
            if to is not None:
                o, c, g, b, y = to
                target = ((2 * o + c) * self.planes + g * self.blocks + b) * 2 + y
                pairs.append((index, target))
        return lax.ppermute(values, AXES, pairs)

    def swap(self, values):
        return self.send(values, lambda o, c, g, b, y: (g % 2, g // 2, 2 * o + c, b, y))

    def swap_back(self, values):
        return self.send(values, lambda o, c, g, b, y: (g // 2, g % 2, 2 * c + o, b, y))

    def part(self, values, k):
        return self.send(values, lambda o, c, g, b, y: (o ^ (k // 2), c, g, b, y ^ (k % 2)))

    def other_group(self, values, k):
        return self.send(values, lambda o, c, g, b, y: (o, c, g ^ k, b, y))

    def other_block(self, values, k):
        return self.send(values, lambda o, c, g, b, y: (o, c, g, b ^ k, y))

    def other_core(self, values):
        return self.send(values, lambda o, c, g, b, y: (o, 1 - c, g, b, y))

    def other_outer(self, values):
        return self.send(values, lambda o, c, g, b, y: (1 - o, c, g, b, y))

    def first_index(self, core, block, part):
        plane = (2 * core + part // 2) * self.blocks + block
        return 2 * plane + part % 2

    def gather(self, rows):
        cut = rows.shape[1] // 2
        one = self.part(rows, 1)
        two = self.part(rows, 2)
        return (rows, one, two, self.part(one[:, :cut], 2), self.part(two[:, cut:], 1))

    def scatter(self, parts):
        left_near, left_far, right_near, right_far = parts
        count = left_near.shape[0] // 2
        from_one = self.part(left_far, 1)
        from_two = self.part(right_far, 2)
        left = (left_near[count:].astype(f32) + from_one[count:].astype(f32)).astype(bf16)
        right = (right_near[count:].astype(f32) + from_two[count:].astype(f32)).astype(bf16)
        return (
            left_near, from_one, self.part(left, 2), right_near, from_two, self.part(right, 1)
        )

    def arrivals(self, stats):
        return [stats] + [self.part(stats, k) for k in range(1, TENSOR)]

    def spread(self, rows):
        own = [rows] + [self.other_block(rows, k) for k in range(1, self.blocks)]
        return own + [self.other_core(piece) for piece in own]

    def collect(self, pieces):
        total = [(piece,) for piece in pieces[: self.blocks]]
        total = [
            own + (self.other_core(piece.astype(bf16)),)
            for own, piece in zip(total, pieces[self.blocks :])
        ]
        if self.blocks == 1:
            return total[0]
        total = [sum(term.astype(f32) for term in terms) for terms in total]
        result = total[0]
        for k in range(1, self.blocks):
            result = result + self.other_block(total[k].astype(bf16), k).astype(f32)
        return (result,)

    def gather_planes(self, rows):
        return lax.all_gather(rows, (AXES[2], AXES[1]), axis=0, tiled=True)

    def fetch_columns(self, mine, there):
        arrived = self.send(
            there, lambda o, c, g, b, y: (o, c, g, b, 1 - y) if y == c else None
        )
        return jnp.where(self.y == self.c, mine, arrived)

    def fetch_heads(self, whole, first, widths):
        count, wide = whole.shape[0] // TENSOR, whole.shape[1] - first
        planes = self.planes // TENSOR
        half = count // (2 * planes)

        def rows_of(part):
            return lax.dynamic_slice(whole, (part * count, first), (count, wide))

        def core_rows(part):
            piece = rows_of(part).reshape(planes, 2, half, wide)
            return lax.dynamic_index_in_dim(piece, self.c, 1, False).reshape(planes * half, wide)

        halves = [self.part(core_rows(self.p ^ k), k) for k in range(1, TENSOR)]
        mine = jnp.stack(halves)
        other = self.other_core(mine)
        both = jnp.where(
            self.c == 0, jnp.stack([mine, other], 1), jnp.stack([other, mine], 1)
        ).reshape(TENSOR - 1, 2, planes, half, wide)
        pieces = [rows_of(self.p)]
        pieces += [both[k].transpose(1, 0, 2, 3).reshape(count, wide) for k in range(TENSOR - 1)]
        rows = count // (planes * 2 * TENSOR)
        if rows % (2 * SUBLANES) == 0:
            return assemble(self.p, pieces, planes, widths)
        parts, start = [], 0
        for one in widths:
            result = jnp.zeros((planes, 2, 2, 2, rows, TENSOR, one), bf16)
            for k, piece in enumerate(pieces):
                piece = piece[:, start : start + one].reshape(planes, 2, TENSOR, rows, one)
                piece = piece.transpose(0, 1, 3, 2, 4)[:, None, None]
                at = (0, self.y ^ (k % 2), self.o ^ (k // 2)) + (0,) * 4
                result = lax.dynamic_update_slice(result, piece, at)
            parts.append(result.reshape(count, TENSOR * one))
            start += one
        return jnp.concatenate(parts, 1)


def heads_share(matrices, share, shares):
    pieces = []
    for matrix in matrices:
        rows, width = matrix.shape[0] // shares, matrix.shape[1] // TENSOR
        piece = lax.dynamic_slice_in_dim(matrix, share * rows, rows, 0)
        piece = piece.reshape(rows, TENSOR, width).transpose(1, 0, 2)
        pieces.append(piece.reshape(TENSOR * rows, width))
    return jnp.concatenate(pieces, 1)


def assemble_kernel(planes, widths, part, *refs):
    pieces, out = refs[:TENSOR], refs[TENSOR]
    count = pieces[0].shape[0]
    rows = count // (planes * 2 * TENSOR)
    for k, piece in enumerate(pieces):
        owner = part[0] ^ k
        place = (owner % 2) * 2 + owner // 2
        for plane in range(planes):
            for core in range(2):
                start = (plane * TENSOR + place) * 2 + core
                at = pl.ds(pl.multiple_of(start * rows, rows), rows)
                for group in range(TENSOR):
                    source = ((plane * 2 + core) * TENSOR + group) * rows
                    first = 0
                    for one in widths:
                        to = first * TENSOR + group * one
                        out[at, to : to + one] = piece[
                            source : source + rows, first : first + one
                        ]
                        first += one


def assemble(part, pieces, planes, widths):
    count, wide = pieces[0].shape
    return pl.pallas_call(
        functools.partial(assemble_kernel, planes, widths),
        out_shape=jax.ShapeDtypeStruct((count, TENSOR * wide), bf16),
        in_specs=[pl.BlockSpec(memory_space=m) for m in [pltpu.SMEM] + [pltpu.VMEM] * TENSOR],
        out_specs=pl.BlockSpec(memory_space=pltpu.VMEM),
        compiler_params=pltpu.CompilerParams(vmem_limit_bytes=VMEM_BYTES),
        cost_estimate=pl.CostEstimate(
            flops=0, bytes_accessed=16 * count * wide, transcendentals=0
        ),
    )(part.astype(jnp.int32)[None], *pieces)


def rotary_tables(positions):
    pair_count = HD // 2
    third_part = pair_count // 3
    first_part = pair_count - 2 * third_part
    pieces = []
    for column, amount in ((0, first_part), (1, third_part), (2, third_part)):
        frequency = jnp.power(10000.0, -jnp.arange(amount, dtype=f32) / amount)
        pieces.append(positions[column].astype(f32)[:, None] * frequency[None, :])
    angles = jnp.repeat(jnp.concatenate(pieces, 1), 2, 1)
    sign = jnp.where(jnp.arange(HD) % 2 == 0, -1.0, 1.0)
    return jnp.cos(angles), jnp.sin(angles) * sign


def call(kernel, outs, args, scratch=(), flops=0, anywhere=()):
    outs = [jax.ShapeDtypeStruct(shape, dtype) for shape, dtype in outs]
    moved = sum(v.size * v.dtype.itemsize for v in list(args) + outs)
    space = [pl.ANY if k in anywhere else pltpu.VMEM for k in range(len(args))]
    return pl.pallas_call(
        kernel,
        out_shape=outs,
        in_specs=[pl.BlockSpec(memory_space=m) for m in space],
        out_specs=[pl.BlockSpec(memory_space=pltpu.VMEM) for _ in outs],
        scratch_shapes=list(scratch),
        compiler_params=pltpu.CompilerParams(vmem_limit_bytes=VMEM_BYTES),
        cost_estimate=pl.CostEstimate(flops=flops, bytes_accessed=moved, transcendentals=0),
    )(*args)


def part_shapes(rows, width):
    return [((rows // 2, width // 2), bf16)] * 4


def put_parts(parts, raw, inner, factors):
    count, half = raw.shape[0] // TENSOR, raw.shape[1] // 2
    for at in chunks(raw.shape[1]):
        values = (raw[:, at] + dot(inner, factors[:, at])).astype(bf16)
        right = at.start // half
        to = slice(at.start - right * half, at.stop - right * half)
        order = ((0, 1), (2, 3)) if right else ((0, 2), (1, 3))
        for ref, slots in zip(parts[2:] if right else parts[:2], order):
            for row, slot in enumerate(slots):
                ref[row * count : (row + 1) * count, to] = values[
                    slot * count : (slot + 1) * count
                ]


def start_copy(source, held, sem):
    copy = pltpu.make_async_copy(source, held, sem)
    copy.start()
    return copy


def join(pieces, full):
    own, one, two, left, right = pieces
    count, width = own.shape
    full[:count] = own[...]
    full[count : 2 * count] = one[...]
    full[2 * count : 3 * count] = two[...]
    full[3 * count :, : width // 2] = left[...]
    full[3 * count :, width // 2 :] = right[...]


def chunks(width):
    return [slice(start, start + CHUNK) for start in range(0, width, CHUNK)]


def turned(values):
    return values.astype(f32).T.astype(bf16)


def narrow(values, mask):
    return (values * mask).astype(bf16)


def row_sums(values):
    ones = jnp.ones((SUBLANES, values.shape[1]), bf16)
    high = values.astype(bf16)
    return dot_nt(ones, high) + dot_nt(ones, (values - high.astype(f32)).astype(bf16))


def as_columns(row, width):
    column = jnp.broadcast_to(row, (HD, row.shape[1])).T
    return jnp.concatenate([column] * (width // HD), 1)


def total_stats(refs):
    total = refs[0][...]
    count = total.shape[1] // TENSOR
    for k, ref in enumerate(refs):
        if k:
            order = [ref[:, (j ^ k) * count : ((j ^ k) + 1) * count] for j in range(TENSOR)]
            total = total + jnp.concatenate(order, 1)
    return total


def stat_rows(total, index):
    return total[index * SUBLANES : index * SUBLANES + 1]


def swap_pairs(values):
    lane = lax.broadcasted_iota(jnp.int32, values.shape, 1)
    return jnp.where(lane % 2 == 0, pltpu.roll(values, HD - 1, 1), pltpu.roll(values, 1, 1))


def rotate(values, cosine, sine):
    heads = [values[:, k : k + HD] for k in range(0, values.shape[1], HD)]
    return jnp.concatenate([v * cosine + swap_pairs(v) * sine for v in heads], 1)


def rotate_back(grad, cosine, sine):
    heads = [grad[:, k : k + HD] for k in range(0, grad.shape[1], HD)]
    return jnp.concatenate([v * cosine + swap_pairs(v * sine) for v in heads], 1)


def gelu_terms(x):
    slope = math.sqrt(2.0 / math.pi)
    square = x * x
    t = jnp.tanh(slope * x * (1.0 + 0.044715 * square))
    value = 0.5 * x * (1.0 + t)
    inner = slope * (1.0 + 3.0 * 0.044715 * square)
    return value, 0.5 * (1.0 + t) + 0.5 * x * (1.0 - t * t) * inner


def sum_terms(terms, count):
    sides = []
    for near, first, far in (terms[:3], terms[3:]):
        total = near[:count].astype(f32) + first[:count].astype(f32) + far[...].astype(f32)
        sides.append(total)
    return jnp.concatenate(sides, 1)


def advance_kernel(*refs):
    terms, (state, factor, scale, shift, new, normed) = refs[:6], refs[6:]
    value = state[...] + factor[...] * sum_terms(terms, state.shape[0])
    new[...] = value
    centred = value - jnp.mean(value, -1, keepdims=True)
    hat = centred * lax.rsqrt(jnp.mean(centred * centred, -1, keepdims=True) + epsilon)
    normed[...] = (hat * scale[...] + shift[...]).astype(bf16)


def advance(terms, state, factor, scale, shift):
    return call(
        advance_kernel, [(state.shape, f32), (state.shape, bf16)],
        (*terms, state, factor, scale, shift), flops=30 * state.size,
    )


def retreat_kernel(*refs):
    terms, (state, grad, scale, factor, new, out) = refs[:6], refs[6:]
    value = state[...]
    centred = value - jnp.mean(value, -1, keepdims=True)
    spread = lax.rsqrt(jnp.mean(centred * centred, -1, keepdims=True) + epsilon)
    hat = centred * spread
    inner = sum_terms(terms, value.shape[0]) * scale[...]
    along = jnp.mean(inner * hat, -1, keepdims=True)
    result = grad[...] + spread * (inner - jnp.mean(inner, -1, keepdims=True) - hat * along)
    new[...] = result
    out[...] = (result * factor[...]).astype(bf16)


def retreat(terms, state, grad, scale, factor):
    return call(
        retreat_kernel, [(state.shape, f32), (state.shape, bf16)],
        (*terms, state, grad, scale, factor), flops=40 * state.size,
    )


def pack_kernel(layer, squares, planes, *refs):
    part, square, wide = refs[:3]
    mine, there, held, sems = refs[3:]
    own = square.shape[3] // TENSOR
    copies = []
    if planes:
        whole = pltpu.make_async_copy(wide.at[layer], held, sems.at[2 * len(squares)])
        whole.start()
    for k, column in enumerate(squares):
        for side, out in enumerate((mine, there)):
            at = pl.ds(pl.multiple_of((part[0] ^ side) * own, own), own)
            copies.append(
                pltpu.make_async_copy(
                    square.at[layer, squares[column], :, at],
                    out.at[:, pl.ds(column, own)],
                    sems.at[2 * k + side],
                )
            )
            copies[-1].start()
    if planes:
        base, stop, count = planes
        one = held.shape[1] // (8 * count)
        step = (stop - base) // (2 * count)
        whole.wait()
        for out in (mine, there) if step > one else ():
            out[:, base:stop] = jnp.zeros((held.shape[0], stop - base), bf16)
        for k in range(TENSOR):

            @pl.when(part[0] == k)
            def _(k=k):
                for side, out in enumerate((mine, there)):
                    o, y = divmod(k ^ side, 2)
                    for z in range(2 * count):
                        at = (((z // 2) * 2 + y) * 4 + o * 2 + z % 2) * one
                        to = base + z * step
                        out[:, to : to + one] = held[:, at : at + one]

    for copy in copies:
        copy.wait()


def pack(part, square, wide, layer, width, squares, planes=None):
    rows = square.shape[2]
    scratch = [
        pltpu.VMEM(wide.shape[1:] if planes else (SUBLANES, HD), bf16),
        pltpu.SemaphoreType.DMA((2 * len(squares) + 1,)),
    ]
    return pl.pallas_call(
        functools.partial(pack_kernel, layer, squares, planes),
        out_shape=[jax.ShapeDtypeStruct((rows, width), bf16)] * 2,
        in_specs=[pl.BlockSpec(memory_space=m) for m in (pltpu.SMEM, pl.ANY, pl.ANY)],
        out_specs=[pl.BlockSpec(memory_space=pltpu.VMEM)] * 2,
        scratch_shapes=scratch,
        compiler_params=pltpu.CompilerParams(vmem_limit_bytes=VMEM_BYTES),
        cost_estimate=pl.CostEstimate(flops=0, bytes_accessed=8 * rows * width, transcendentals=0),
    )(part, square, wide)


def picked(ref, place, rank, count=1):
    return ref[place * rank : (place + count) * rank]


def ffn_kernel(places, *refs):
    pieces, (mask, near, far, w_in, w_out), refs = refs[:5], refs[5:10], refs[10:]
    parts, (up_raw, up_inner, down_inner), refs = refs[:4], refs[4:7], refs[7:]
    full, raw, hidden, held_in, held_out, sems = refs
    rank = mask.shape[1]
    width = full.shape[1]
    up_a, down_b, down_a, up_b = places
    first = start_copy(w_in, held_in, sems.at[0])
    second = start_copy(w_out.at[:, pl.ds(0, full.shape[1])], held_out, sems.at[1])
    join(pieces, full)
    inner = narrow(dot_nt(full[...], picked(near, up_a, rank)), mask[...])
    up_inner[...] = inner
    first.wait()
    raw[:, : held_in.shape[1]] = dot(full[...], held_in[...])
    factors = picked(far, up_b, rank)
    for at in chunks(held_in.shape[1]):
        values = raw[:, at] + dot(inner, factors[:, at])
        up_raw[:, at] = values.astype(bf16)
        hidden[:, at] = gelu_terms(values)[0].astype(bf16)
    second.wait()
    raw[:, :width] = dot(hidden[...], held_out[...])
    inner = narrow(dot_nt(hidden[...], picked(far, down_a, rank)), mask[...])
    down_inner[...] = inner
    put_parts(parts, raw.at[:, :width], inner, picked(near, down_b, rank))


def ffn(pieces, mask, near, far, w_in, w_out, places):
    count, width = pieces[0].shape
    rows, rank = mask.shape
    wide = w_in.shape[1]
    outs = part_shapes(rows, width) + [((rows, wide), bf16), ((rows, rank), bf16)]
    scratch = [
        pltpu.VMEM((rows, width), bf16),
        pltpu.VMEM((rows, max(wide, width)), f32),
        pltpu.VMEM((rows, wide), bf16),
        pltpu.VMEM(w_in.shape, bf16),
        pltpu.VMEM((w_out.shape[0], width), bf16),
        pltpu.SemaphoreType.DMA((2,)),
    ]
    outs = call(
        functools.partial(ffn_kernel, places), outs + [((rows, rank), bf16)],
        (*pieces, mask, near, far, w_in, w_out), scratch, 4 * rows * width * wide, (8, 9),
    )
    return outs[:4], tuple(outs[4:])


def ffn_back_kernel(places, *refs):
    grads, inputs, refs = refs[:5], refs[5:10], refs[10:]
    up_raw, up_inner, down_inner, mask, near, far, w_in, w_out = refs[:8]
    parts, (a_down, b_up, a_up, b_down) = refs[8:12], refs[12:16]
    grad, full, raw, grad_up, held_in, held_out, sems = refs[16:]
    rank = mask.shape[1]
    width = full.shape[1]
    at_up_a, at_down_b, at_down_a, at_up_b = places
    second = start_copy(w_out.at[:, pl.ds(0, full.shape[1])], held_out, sems.at[1])
    first = start_copy(w_in, held_in, sems.at[0])
    join(grads, grad)
    join(inputs, full)
    down_back = narrow(dot_nt(grad[...], picked(near, at_down_b, rank)), mask[...])
    down_turned = turned(down_back)
    up_turned = turned(up_inner[...])
    factors = picked(far, at_down_a, rank)
    second.wait()
    raw[:, : held_out.shape[0]] = dot_nt(grad[...], held_out[...])
    for at in chunks(up_raw.shape[1]):
        hidden_grad = raw[:, at] + dot(down_back, factors[:, at])
        value, slope = gelu_terms(up_raw[:, at].astype(f32))
        raw_grad = (hidden_grad * slope).astype(bf16)
        grad_up[:, at] = raw_grad
        a_down[:, at] = dot(down_turned, value.astype(bf16)).astype(bf16)
        b_up[:, at] = dot(up_turned, raw_grad).astype(bf16)
    up_back = narrow(dot_nt(grad_up[...], picked(far, at_up_b, rank)), mask[...])
    first.wait()
    raw[:, :width] = dot_nt(grad_up[...], held_in[...])
    put_parts(parts, raw.at[:, :width], up_back, picked(near, at_up_a, rank))
    a_up[...] = dot(turned(up_back), full[...]).astype(bf16)
    b_down[...] = dot(turned(down_inner[...]), grad[...]).astype(bf16)


def ffn_back(grads, inputs, saved, mask, near, far, w_in, w_out, places):
    count, width = grads[0].shape
    rows, rank = mask.shape
    wide = w_in.shape[1]
    outs = part_shapes(rows, width) + [((rank, n), bf16) for n in (wide, wide, width, width)]
    scratch = [
        pltpu.VMEM((rows, width), bf16),
        pltpu.VMEM((rows, width), bf16),
        pltpu.VMEM((rows, max(wide, width)), f32),
        pltpu.VMEM((rows, wide), bf16),
        pltpu.VMEM(w_in.shape, bf16),
        pltpu.VMEM((w_out.shape[0], width), bf16),
        pltpu.SemaphoreType.DMA((2,)),
    ]
    outs = call(
        functools.partial(ffn_back_kernel, places), outs,
        (*grads, *inputs, *saved, mask, near, far, w_in, w_out), scratch,
        4 * rows * width * wide, (16, 17),
    )
    return outs[:4], outs[4:]


def project_kernel(start, count, normed, *refs):
    pieces, (mask, weights, near, heads), refs = refs[:5], refs[5:9], refs[9:]
    raws, (inner, stats, full, together, held, sems) = refs[:count], refs[count:]
    own = raws[0].shape[1]
    rank = mask.shape[1]
    base, near_at, heads_at = start
    copy = start_copy(weights.at[:, pl.ds(base, count * own)], held, sems.at[0])
    join(pieces, full)
    inner[...] = narrow(
        dot_nt(full[...], picked(near, near_at, rank, count)),
        jnp.concatenate([mask[...]] * count, 1),
    )
    copy.wait()
    together[...] = dot(full[...], held[...])
    for k, raw in enumerate(raws):
        values = together[:, k * own : (k + 1) * own] + dot(
            inner[:, k * rank : (k + 1) * rank], picked(heads, heads_at + k, rank)
        )
        raw[...] = values.astype(raw.dtype)
        if k < normed:
            stats[k * SUBLANES : (k + 1) * SUBLANES] = row_sums(values * values)


def project(pieces, mask, weights, near, heads, start, count, normed):
    rows, rank = mask.shape
    own = heads.shape[1]
    outs = [((rows, own), f32 if k < normed else bf16) for k in range(count)]
    outs += [((rows, count * rank), bf16), ((normed * SUBLANES, rows), f32)]
    outs = call(
        functools.partial(project_kernel, start, count, normed), outs,
        (*pieces, mask, weights, near, heads),
        [
            pltpu.VMEM((rows, pieces[0].shape[1]), bf16), pltpu.VMEM((rows, count * own), f32),
            pltpu.VMEM((weights.shape[0], count * own), bf16), pltpu.SemaphoreType.DMA((1,)),
        ],
        2 * rows * weights.shape[0] * own * count, (6,),
    )
    return outs[:count], outs[count], outs[count + 1]


def scales_of(total, index, width, own):
    return as_columns(lax.rsqrt(stat_rows(total, index) / width + epsilon), own)


def normalize_kernel(count, turning, valued, width, *refs):
    raws, gains, refs = refs[:count], refs[count : 2 * count], refs[2 * count :]
    tables, refs = refs[: 2 * turning], refs[2 * turning :]
    value, refs = refs[:valued], refs[valued:]
    stats, outs, total = refs[: -count - 1], refs[-count - 1 : -1], refs[-1]
    total[...] = total_stats(stats)
    own = raws[0].shape[1]
    for k in range(count):
        values = raws[k][...] * scales_of(total, k, width, own) * gains[k][...]
        if turning:
            values = rotate(values, tables[0][...], tables[1][...])
        outs[k][:, :own] = values.astype(bf16)
    if valued:
        outs[-1][:, own:] = value[0][...]


def normalize(raws, gains, stats, width, tables=(), value=()):
    shape = raws[0].shape
    outs = [(shape, bf16) for _ in raws]
    if value:
        outs[-1] = ((shape[0], 2 * shape[1]), bf16)
    outs.append((stats[0].shape, f32))
    outs = call(
        functools.partial(normalize_kernel, len(raws), len(tables) // 2, len(value), width), outs,
        (*raws, *gains, *tables, *value, *stats), flops=20 * len(raws) * raws[0].size,
    )
    return outs[:-1], outs[-1]


def attend_kernel(count, start, *refs):
    query, marks, refs = refs[0], refs[1], refs[2:]
    pairs, key_marks, refs = refs[:count], refs[count : 2 * count], refs[2 * count :]
    mask, weights, near, heads = refs[:4]
    parts, (result, inner, raw, held, sems) = refs[4:8], refs[8:]
    rows, own = query.shape
    width, rank = near.shape[1], mask.shape[1]
    base, near_at, heads_at = start
    copy = start_copy(weights.at[:, pl.ds(base, width)], held, sems.at[0])
    scale = 1.0 / math.sqrt(HD)
    block = min(BLOCK, rows)

    @pl.loop(0, rows // block)
    def _(index):
        at = pl.ds(pl.multiple_of(index * block, block), block)
        allowed = [marks[at] == key_mark[...] for key_mark in key_marks]
        for head in range(0, own, HD):
            scores = [
                jnp.where(
                    ok, dot_nt(query[at, head : head + HD], pair[:, head : head + HD]) * scale,
                    masked_score,
                )
                for ok, pair in zip(allowed, pairs)
            ]
            peak = functools.reduce(
                jnp.maximum, [jnp.max(s, -1, keepdims=True) for s in scores]
            )
            weighed = [jnp.exp(s - peak) for s in scores]
            total = sum(jnp.sum(w, -1, keepdims=True) for w in weighed)
            summed = sum(
                dot(w.astype(bf16), pair[:, own + head : own + head + HD])
                for w, pair in zip(weighed, pairs)
            )
            result[at, head : head + HD] = (summed / total).astype(bf16)

    copy.wait()
    raw[...] = dot(result[...], held[...])
    inner[...] = narrow(dot_nt(result[...], picked(heads, heads_at, rank)), mask[...])
    put_parts(parts, raw, inner[...], picked(near, near_at, rank))


def attend(query, marks, pairs, key_marks, mask, weights, near, heads, start):
    rows, own = query.shape
    width, rank = near.shape[1], mask.shape[1]
    outs = part_shapes(rows, width) + [((rows, own), bf16), ((rows, rank), bf16)]
    keys = sum(pair.shape[0] for pair in pairs)
    outs = call(
        functools.partial(attend_kernel, len(pairs), start), outs,
        (query, marks, *pairs, *key_marks, mask, weights, near, heads),
        [
            pltpu.VMEM((rows, width), f32), pltpu.VMEM((own, width), bf16),
            pltpu.SemaphoreType.DMA((1,)),
        ],
        4 * rows * keys * own + 2 * rows * own * width, (3 + 2 * len(pairs),),
    )
    return outs[:4], outs[4], outs[5]


def attend_back_kernel(count, start, *refs):
    grads, (query, marks), refs = refs[:5], refs[5:7], refs[7:]
    pairs, key_marks, refs = refs[:count], refs[count : 2 * count], refs[2 * count :]
    (result, inner, mask, weights, near, heads), refs = refs[:6], refs[6:]
    base, near_at, heads_at = start
    grad_query, pair_grads, refs = refs[0], refs[1 : 1 + count], refs[1 + count :]
    a_grad, b_grad, grad, grad_out, raw, held, sems = refs
    rows, own = query.shape
    rank = mask.shape[1]
    scale = 1.0 / math.sqrt(HD)
    block = min(BLOCK, rows)
    copy = start_copy(weights.at[:, pl.ds(base, grad.shape[1])], held, sems.at[0])
    join(grads, grad)
    back = narrow(dot_nt(grad[...], picked(near, near_at, rank)), mask[...])
    b_grad[...] = dot(turned(inner[...]), grad[...]).astype(bf16)
    copy.wait()
    raw[...] = dot_nt(grad[...], held[...])
    grad_out[...] = (raw[...] + dot(back, picked(heads, heads_at, rank))).astype(bf16)
    a_grad[...] = dot(turned(back), result[...]).astype(bf16)
    for head in range(0, own, HD):
        here, there = slice(head, head + HD), slice(own + head, own + head + HD)
        keys_turned = [turned(pair[:, here]) for pair in pairs]
        for start in range(0, rows, block):
            at = slice(start, start + block)
            q, g = query[at, here], grad_out[at, here]
            scores = [
                jnp.where(
                    key_mark[...] == marks[:, at], dot_nt(pair[:, here], q) * scale, masked_score
                )
                for key_mark, pair in zip(key_marks, pairs)
            ]
            peak = functools.reduce(jnp.maximum, [jnp.max(s, 0, keepdims=True) for s in scores])
            weighed = [jnp.exp(s - peak) for s in scores]
            inverse = 1.0 / sum(jnp.sum(w, 0, keepdims=True) for w in weighed)
            probs = [w * inverse for w in weighed]
            along = [dot_nt(pair[:, there], g) for pair in pairs]
            delta = sum(jnp.sum(p * d, 0, keepdims=True) for p, d in zip(probs, along))
            turned_grad = 0.0
            for k in range(count):
                score_grad = (probs[k] * (along[k] - delta)).astype(bf16)
                key_grad = dot(score_grad, q) * scale
                value_grad = dot(probs[k].astype(bf16), g)
                if start:
                    key_grad = key_grad + pair_grads[k][:, here]
                    value_grad = value_grad + pair_grads[k][:, there]
                pair_grads[k][:, here] = key_grad
                pair_grads[k][:, there] = value_grad
                turned_grad = turned_grad + dot(keys_turned[k], score_grad)
            grad_query[at, here] = (turned_grad * scale).T


def attend_back(
    grads, query, marks, pairs, key_marks, result, inner, mask, weights, near, heads, start
):
    rows, own = query.shape
    width, rank = near.shape[1], mask.shape[1]
    outs = [((rows, own), f32)] + [(pair.shape, f32) for pair in pairs]
    outs += [((rank, own), bf16), ((rank, width), bf16)]
    keys = sum(pair.shape[0] for pair in pairs)
    outs = call(
        functools.partial(attend_back_kernel, len(pairs), start), outs,
        (*grads, query, marks, *pairs, *key_marks, result, inner, mask, weights, near, heads),
        [
            pltpu.VMEM((rows, width), bf16), pltpu.VMEM((rows, own), bf16),
            pltpu.VMEM((rows, own), f32), pltpu.VMEM((own, width), bf16),
            pltpu.SemaphoreType.DMA((1,)),
        ],
        10 * rows * keys * own + 2 * rows * own * width, (10 + 2 * len(pairs),),
    )
    return outs[0], outs[1:-2], outs[-2], outs[-1]


def back_stats_kernel(counts, turning, valued, width, *refs):
    number = len(counts)
    terms = []
    for count in counts:
        terms.append(refs[:count])
        refs = refs[count:]
    raws, gains, refs = refs[:number], refs[number : 2 * number], refs[2 * number :]
    tables, refs = refs[: 2 * turning], refs[2 * turning :]
    total, outs, stats = refs[0], refs[1:-1], refs[-1]
    own = raws[0].shape[1]
    for k in range(number):
        grad = sum(term[:, :own].astype(f32) for term in terms[k])
        if turning:
            grad = rotate_back(grad, tables[0][...], tables[1][...])
        grad = grad * gains[k][...]
        outs[k][...] = grad
        hat = raws[k][...] * scales_of(total, k, width, own)
        stats[k * SUBLANES : (k + 1) * SUBLANES] = row_sums(hat * grad)
    if valued:
        outs[-1][...] = sum(term[:, own:].astype(f32) for term in terms[-1]).astype(bf16)


def back_stats(terms, raws, gains, total, width, tables=(), valued=False):
    shape = raws[0].shape
    outs = [(shape, f32) for _ in raws] + [(shape, bf16)] * valued + [(total.shape, f32)]
    outs = call(
        functools.partial(
            back_stats_kernel, tuple(len(t) for t in terms), len(tables) // 2, int(valued), width
        ),
        outs, (*[term for t in terms for term in t], *raws, *gains, *tables, total),
        flops=30 * len(raws) * raws[0].size,
    )
    return outs[:-1], outs[-1]


def project_back_kernel(start, count, normed, parted, *refs):
    scaled, raws, refs = refs[:count], refs[count : count + normed], refs[count + normed :]
    total, (inner, mask, weights, near, heads), refs = refs[0], refs[1:6], refs[6:]
    inputs, refs = refs[:5], refs[5:]
    split = 4 if parted else 1
    stats, refs = refs[: -8 - split], refs[-8 - split :]
    outs, (a_grad, b_grad, full, grads, back, raw, held, sems) = refs[:split], refs[split:]
    own = scaled[0].shape[1]
    width = full.shape[1]
    rank = mask.shape[1]
    base, near_at, heads_at = start
    copy = start_copy(weights.at[:, pl.ds(base, count * own)], held, sems.at[0])
    join(inputs, full)
    along = total_stats(stats)
    for k in range(count):
        if k < normed:
            scale = scales_of(total, k, width, own)
            hat = raws[k][...] * scale
            mean = as_columns(stat_rows(along, k) / width, own)
            grads[:, k * own : (k + 1) * own] = (scale * (scaled[k][...] - hat * mean)).astype(bf16)
        else:
            grads[:, k * own : (k + 1) * own] = scaled[k][...]
    inner_turned = turned(inner[...])
    for k in range(count):
        at = slice(k * rank, (k + 1) * rank)
        grad = grads[:, k * own : (k + 1) * own]
        back[:, at] = narrow(dot_nt(grad, picked(heads, heads_at + k, rank)), mask[...])
        b_grad[at] = dot(inner_turned[at], grad).astype(bf16)
    a_grad[...] = dot(turned(back[...]), full[...]).astype(bf16)
    copy.wait()
    raw[...] = dot_nt(grads[...], held[...])
    factors = picked(near, near_at, rank, count)
    if parted:
        put_parts(outs, raw, back[...], factors)
    else:
        for at in chunks(width):
            outs[0][:, at] = raw[:, at] + dot(back[...], factors[:, at])


def project_back(
    scaled, raws, total, stats, inner, mask, weights, near, heads, inputs, start, parted=True
):
    count, normed = len(scaled), len(raws)
    rows, own = scaled[0].shape
    width, rank = weights.shape[0], mask.shape[1]
    outs = part_shapes(rows, width) if parted else [((rows, width), f32)]
    split = len(outs)
    outs = outs + [((count * rank, width), bf16), ((count * rank, own), bf16)]
    scratch = [
        pltpu.VMEM((rows, width), bf16),
        pltpu.VMEM((rows, count * own), bf16),
        pltpu.VMEM((rows, count * rank), bf16),
        pltpu.VMEM((rows, width), f32),
        pltpu.VMEM((width, count * own), bf16),
        pltpu.SemaphoreType.DMA((1,)),
    ]
    outs = call(
        functools.partial(project_back_kernel, start, count, normed, parted), outs,
        (*scaled, *raws, total, inner, mask, weights, near, heads, *inputs, *stats), scratch,
        2 * rows * width * own * count, (count + normed + 3,),
    )
    return outs[:split], outs[split], outs[split + 1]


def on_device(
    tokens,
    context,
    cotangent,
    positions,
    sequence_lengths,
    sequence_adapter,
    text_token_count,
    timestep_modulation,
    modulation,
    gains,
    query_key_value_weight,
    output_weight,
    up_weight,
    down_weight,
    first_factors,
    down_first_factor,
    second_factors,
    up_second_factor,
):
    place = Place()
    rows, width = tokens.shape
    seq_count, text_local = context.shape[:2]
    layers = query_key_value_weight.shape[0]
    columns = first_factors.shape[3]
    rank = seq_count * ADAPTER_RANK
    own = width // TENSOR
    wide = up_weight.shape[2] // TENSOR
    padded = -(-wide // CHUNK) * CHUNK
    set_rows = TENSOR * rows

    numbers = jnp.concatenate([positions.reshape(-1), sequence_lengths, text_token_count])
    numbers = place.swap(numbers)
    moved = place.swap(
        jnp.concatenate([tokens, context.reshape(seq_count * text_local, width)], 0)
    )
    state = moved[:rows].astype(f32)
    times = place.swap(timestep_modulation)
    positions = numbers[: 3 * rows].reshape(3, rows)
    lengths, counts = [
        numbers[3 * rows + k * seq_count : 3 * rows + (k + 1) * seq_count] for k in range(2)
    ]

    bounds = jnp.cumsum(lengths)

    def token_segments(index):
        packed = jnp.arange(rows, dtype=jnp.int32) * place.size + index
        return jnp.sum((packed[:, None] >= bounds[None, :]).astype(jnp.int32), 1)

    def text_marks(index):
        at = index * text_local + jnp.arange(text_local)
        marks = jnp.where(at[None, :] < counts[:, None], jnp.arange(seq_count)[:, None], -1)
        return marks.reshape(-1)

    def over_set(function, core, block):
        return jnp.concatenate(
            [function(place.first_index(core, block, place.p ^ k)) for k in range(TENSOR)]
        )

    def over_group(function):
        return [
            over_set(function, core, place.b ^ k)
            for core in (place.c, 1 - place.c)
            for k in range(place.blocks)
        ]

    segment = over_set(token_segments, place.c, place.b)
    sequence = jnp.minimum(segment, seq_count - 1)
    self_marks = over_group(token_segments)
    cross_marks = over_group(text_marks)
    column_sequence = jnp.arange(rank) // ADAPTER_RANK
    mask = (sequence[:, None] == column_sequence[None, :]) & (segment < seq_count)[:, None]
    mask = mask.astype(f32)
    text_sequence = jnp.tile(jnp.repeat(jnp.arange(seq_count), text_local), TENSOR)
    text_mask = (text_sequence[:, None] == column_sequence[None, :]).astype(f32)
    valid = (segment[:rows] < seq_count).astype(f32)[:, None]

    def mods_of(layer):
        table = modulation[layer][None] + times
        chosen = [table[0, k][None] for k in range(6)]
        for s in range(1, seq_count):
            here = (sequence[:rows] == s)[:, None]
            chosen = [jnp.where(here, table[s, k][None], chosen[k]) for k in range(6)]
        return chosen

    def own_gain(layer, index):
        return lax.dynamic_slice_in_dim(gains[layer, index], place.p * own, own, 0)[None]

    table = jnp.zeros((place.rep, seq_count), jnp.int32)
    for k in range(2):
        arrived = sequence_adapter if k == 0 else place.other_outer(sequence_adapter)
        for m, values in enumerate((arrived, place.other_core(arrived))):
            here = jnp.arange(place.rep) == 2 * (place.o ^ k) + (place.c ^ m)
            table = jnp.where(here[:, None], values[None], table)
    def tied(value, after):
        return value if after is None else lax.optimization_barrier((value, after))[0]

    wanted = (table[:, :, None] * ADAPTER_RANK + jnp.arange(ADAPTER_RANK)).reshape(-1)
    choose = (jnp.arange(columns)[:, None] == wanted[None, :]).astype(bf16)
    firsts = jnp.einsum("lkdj,jr->lkdr", first_factors, choose).astype(bf16)
    seconds = jnp.einsum("lkjd,jr->lkdr", second_factors, choose).astype(bf16)

    def own_columns(values, count):
        column = jnp.arange(count * rank * place.rep)
        kept = jnp.arange(count * rank)
        here = (column // (rank * place.rep))[:, None] == (kept // rank)[None, :]
        here &= (column % (rank * place.rep))[:, None] == (place.g * rank + kept % rank)[None, :]
        return lax.dot_general(
            here.astype(bf16), values, (((0,), (1,)), ((), ())), preferred_element_type=f32
        ).astype(bf16)

    factor_rows = [
        jnp.concatenate([(firsts, seconds)[w][layer, k] for w, k in NEAR], 1)
        for layer in range(layers)
    ]
    factor_rows = jnp.concatenate(factor_rows, 1)
    factor_rows = place.fetch_columns(factor_rows, factor_rows)
    factor_width = factor_rows.shape[1] // layers

    def fetch_factors(layer, after):
        whole = factor_rows[:, layer * factor_width : (layer + 1) * factor_width]
        return own_columns(place.gather_planes(tied(whole, after)), len(NEAR))

    up_at = 6 * own
    part = place.p.astype(jnp.int32)[None]
    share = 2 * place.o + place.c

    def self_rows_of(layer, after):
        mine, there = pack(
            tied(part, after), query_key_value_weight, up_weight, layer, 3 * own,
            {k * own: k for k in range(3)},
        )
        factors = [(firsts, seconds)[w][layer, k] for w, k in HEADS]
        piece = heads_share(
            [output_weight[layer, 0], output_weight[layer, 1], jnp.concatenate(factors, 1)],
            share, place.rep,
        )
        return jnp.concatenate([place.fetch_columns(mine, there), piece], 1)

    def fetch_self(rows, after):
        whole = place.gather_planes(tied(rows, after))
        widths = (own, own, len(HEADS) * rank * place.rep // TENSOR)
        heads = place.fetch_heads(whole, 3 * own, widths)
        return whole, heads, own_columns(heads[:, 2 * width :], len(HEADS))

    def other_rows_of(layer, after):
        mine, there = pack(
            tied(part, after), query_key_value_weight, up_weight, layer, 3 * own + padded,
            {k * own: 3 + k for k in range(3)}, (3 * own, 3 * own + padded, place.planes),
        )
        return place.fetch_columns(mine, there)

    def fetch_others(layer, rows, after):
        rows = tied(rows, after)
        cross = place.gather_planes(rows[:, : 3 * own])
        up = place.gather_planes(rows[:, 3 * own :])
        count = down_weight.shape[1] // place.rep
        piece = lax.dynamic_slice(
            down_weight, (layer, share * count, 0), (1, count, width)
        )[0]
        factors = [
            dot(lax.dynamic_slice_in_dim(down_first_factor[layer], share * count, count, 0), choose),
            dot_tn(
                lax.dynamic_slice_in_dim(up_second_factor[layer], share * count, count, 1), choose
            ),
        ]
        piece = jnp.concatenate([piece] + [v.astype(bf16) for v in factors], 1)
        piece = jnp.pad(piece, ((0, padded // place.size - count), (0, 0)))
        down = place.gather_planes(tied(piece, rows))
        return cross, up, down, own_columns(down[:, width:], 2)

    positions = jnp.stack([positions] + [place.part(positions, k) for k in range(1, TENSOR)], 1)
    tables = rotary_tables(positions.reshape(3, set_rows))

    def arrivals(stats):
        arrived = place.arrivals(stats)
        count = stats.shape[1] // TENSOR
        if count % HD == 0:
            return arrived
        pieces = [v.reshape(-1, TENSOR, count) for v in arrived]
        total = sum(
            jnp.stack([v[:, j ^ k] for j in range(TENSOR)], 1) for k, v in enumerate(pieces)
        )
        return [total.reshape(stats.shape)]

    columns_of = [v.reshape(-1, 1) for v in (segment, sequence)]
    rows_of = [v.reshape(1, -1) for v in (segment, sequence)]
    self_rows, cross_rows = [[v.reshape(1, -1) for v in m] for m in (self_marks, cross_marks)]
    self_columns, cross_columns = [
        [v.reshape(-1, 1) for v in m] for m in (self_marks, cross_marks)
    ]
    zero_row = jnp.zeros((1, width), f32)
    in_at, out_at, cross_at, text_at = (0, 0, 2), (0, 7, 0), (0, 3, 5), (own, 4, 6)
    crossed_at, ffn_at = (width, 8, 1), (6, 9, 0, 1)

    saved = []
    factors = []
    for layer in range(layers):
        shift_one, scale_one, gate_one, shift_two, scale_two, gate_two = mods_of(layer)
        factors.append((valid * gate_one, valid * gate_two, 1.0 + scale_one, 1.0 + scale_two))
        factors[-1] += (shift_one, shift_two)
    valid_rows = jnp.broadcast_to(valid, (rows, width))
    centred = state - jnp.mean(state, -1, keepdims=True)
    hat = centred * lax.rsqrt(jnp.mean(centred * centred, -1, keepdims=True) + epsilon)
    normed = (hat * factors[0][2] + factors[0][4]).astype(bf16)
    fetched = []
    coming = fetch_self(self_rows_of(0, None), (moved, numbers, times))
    picked_now = fetch_factors(0, None)
    others = None
    for layer in range(layers):
        gate_one, gate_two, scale_one, scale_two, shift_one, shift_two = factors[layer]
        self_in, heads, far_heads = coming
        near = picked_now
        self_pieces = place.gather(normed)
        if layer == 0:
            first_rows = other_rows_of(layer, self_pieces[3])
            others = fetch_others(layer, first_rows, None)
            prepared = [
                (self_rows_of(k, first_rows), other_rows_of(k, first_rows))
                for k in range(1, layers)
            ]
            text = place.gather(tied(moved[rows:], self_pieces[3]))
        cross_in, ffn_in, ffn_out, far = others
        raws, self_inner, stats = project(self_pieces, mask, self_in, near, far_heads, in_at, 3, 2)
        gain = [own_gain(layer, k) for k in range(4)]
        (query, pair), self_total = normalize(
            raws[:2], gain[:2], arrivals(stats), width, tables, raws[2:]
        )
        pairs = place.spread(pair)
        if layer + 1 < layers:
            coming = fetch_self(prepared[layer][0], query)
            picked_now = fetch_factors(layer + 1, query)
        parts, attended, out_inner = attend(
            query, columns_of[0], pairs, self_rows, mask, heads, near, far_heads, out_at
        )
        self_saved = (self_pieces, raws, self_inner, self_total, query, pairs, attended, out_inner)
        state_one, normed = advance(
            place.scatter(parts), state, gate_one, gains[layer, 4][None], zero_row
        )

        text_raws, text_inner, stats = project(
            text, text_mask, cross_in, near, far_heads, text_at, 2, 1
        )
        (pair,), text_total = normalize(
            text_raws[:1], gain[3:], arrivals(stats), width, (), text_raws[1:]
        )
        pairs = place.spread(pair)
        cross_pieces = place.gather(normed)
        if layer + 1 < layers:
            others = fetch_others(layer + 1, prepared[layer][1], cross_pieces[3])
        else:
            cotangent = place.swap(tied(cotangent, ffn_out[:SUBLANES]))
        raws, cross_inner, stats = project(
            cross_pieces, mask, cross_in, near, far_heads, cross_at, 1, 1
        )
        (query,), cross_total = normalize(raws, gain[2:3], arrivals(stats), width)
        parts, crossed, crossed_inner = attend(
            query, columns_of[1], pairs, cross_rows, mask, heads, near, far_heads, crossed_at
        )
        cross_saved = (
            cross_pieces, raws, cross_inner, cross_total, query, pairs, crossed, crossed_inner
        )
        state_two, normed = advance(
            place.scatter(parts), state_one, valid_rows, scale_two, shift_two
        )

        ffn_pieces = place.gather(normed)
        ready = mask if layer + 1 == layers else tied(mask, coming[1])
        parts, ffn_saved = ffn(ffn_pieces, ready, near, far, ffn_in, ffn_out, ffn_at)
        fetched.append((self_in, heads, cross_in, ffn_in, ffn_out, near, far, far_heads))
        saved.append(
            (
                (state, state_one, state_two), self_saved, cross_saved,
                (text_raws, text_inner, text_total), (ffn_pieces, ffn_saved), gain,
            )
        )
        following = factors[min(layer + 1, layers - 1)]
        state, normed = advance(
            place.scatter(parts), state_two, gate_two, following[2], following[4]
        )

    grad = cotangent.astype(f32)
    out = (grad * factors[-1][1]).astype(bf16)
    grad_text = 0.0
    whole_grads, part_grads, wide_grads = [], [], []
    for layer in reversed(range(layers)):
        self_in, heads, cross_in, ffn_in, ffn_out, near, far, far_heads = fetched[layer]
        gate_one, gate_two, scale_one, scale_two, shift_one, shift_two = factors[layer]
        (
            (state_zero, state_one, state_two), self_saved, cross_saved,
            (text_raws, text_inner, text_total), (ffn_pieces, ffn_saved), gain,
        ) = saved[layer]
        parts, (down_a, up_b, up_a, down_b) = ffn_back(
            place.gather(out), ffn_pieces, ffn_saved, mask, near, far, ffn_in, ffn_out, ffn_at
        )
        grad, out = retreat(place.scatter(parts), state_two, grad, scale_two, valid_rows)

        pieces, raws, inner, total, query, pairs, result, result_inner = cross_saved
        grad_query, pair_grads, cross_out_a, cross_out_b = attend_back(
            place.gather(out), query, rows_of[1], pairs, cross_columns, result, result_inner,
            mask, heads, near, far_heads, crossed_at,
        )
        scaled, stats = back_stats([(grad_query,)], raws, gain[2:3], total, width)
        parts, cross_a, cross_b = project_back(
            scaled, raws, total, arrivals(stats), inner, mask, cross_in, near, far_heads, pieces,
            cross_at,
        )
        terms = place.collect(pair_grads)
        scaled, stats = back_stats([terms], text_raws[:1], gain[3:], text_total, width, (), True)
        (text_grad,), text_a, text_b = project_back(
            scaled, text_raws[:1], text_total, arrivals(stats), text_inner, text_mask, cross_in,
            near, far_heads, text, text_at, False,
        )
        grad_text = grad_text + text_grad
        grad, out = retreat(
            place.scatter(parts), state_one, grad, gains[layer, 4][None], gate_one
        )

        pieces, raws, inner, total, query, pairs, result, result_inner = self_saved
        grad_query, pair_grads, self_out_a, self_out_b = attend_back(
            place.gather(out), query, rows_of[0], pairs, self_columns, result, result_inner,
            mask, heads, near, far_heads, out_at,
        )
        terms = place.collect(pair_grads)
        scaled, stats = back_stats(
            [(grad_query,), terms], raws[:2], gain[:2], total, width, tables, True
        )
        parts, self_a, self_b = project_back(
            scaled, raws[:2], total, arrivals(stats), inner, mask, self_in, near, far_heads, pieces,
            in_at,
        )
        gate = factors[max(layer - 1, 0)][1]
        grad, out = retreat(place.scatter(parts), state_zero, grad, scale_one, gate)

        whole_grads.append(
            jnp.concatenate([self_a, cross_a, text_a, up_a, self_out_b, cross_out_b, down_b], 0)
        )
        part_grads.append(
            jnp.concatenate([self_out_a, cross_out_a, self_b, cross_b, text_b], 0)
        )
        wide_grad = jnp.concatenate([down_a, up_b], 0).reshape(2 * rank, place.size, -1)
        wide_grads.append(wide_grad[:, :, : wide // place.size].reshape(2 * rank, wide))

    def flat(lists):
        return jnp.concatenate(lists[::-1], 0).T

    grad_text = grad_text.astype(bf16)
    count, half = grad_text.shape[0] // TENSOR, width // 2
    slots = [grad_text[k * count : (k + 1) * count] for k in range(TENSOR)]
    text_parts = [
        jnp.concatenate([v[:, at] for v in pair], 0)
        for at, pair in (
            (slice(0, half), (slots[0], slots[2])),
            (slice(0, half), (slots[1], slots[3])),
            (slice(half, width), (slots[0], slots[1])),
            (slice(half, width), (slots[2], slots[3])),
        )
    ]

    def added(terms):
        left, one, two, right, three, four = [v.astype(f32) for v in terms]
        count = two.shape[0]
        return jnp.concatenate(
            [left[:count] + one[:count] + two, right[:count] + three[:count] + four], 1
        )

    whole_all = flat(whole_grads)
    whole_wide = whole_all.shape[1]
    whole_all = whole_all.reshape(place.planes, 2, 2, -1, whole_wide)
    slots = [
        lax.dynamic_slice(
            whole_all,
            (0, (place.p ^ k) % 2, (place.p ^ k) // 2, 0, 0),
            (place.planes, 1, 1) + whole_all.shape[3:],
        ).reshape(-1, whole_wide)
        for k in range(TENSOR)
    ]
    count, half = slots[0].shape[0], whole_wide // 2
    from_parts = added(
        place.scatter(
            [
                jnp.concatenate([v[:, at] for v in pair], 0)
                for at, pair in (
                    (slice(0, half), (slots[0], slots[2])),
                    (slice(0, half), (slots[1], slots[3])),
                    (slice(half, whole_wide), (slots[0], slots[1])),
                    (slice(half, whole_wide), (slots[2], slots[3])),
                )
            ]
        )
    )

    def sum_set(values):
        values = values.astype(f32) + place.other_core(values.astype(bf16)).astype(f32)
        result = values
        for k in range(1, place.blocks):
            result = result + place.other_block(values.astype(bf16), k).astype(f32)
        return result.astype(bf16)

    def to_owner(values):
        planes = values.reshape(place.planes, -1, values.shape[1])
        pieces = []
        for k in range(place.rep):
            plane = (place.g ^ k) * place.blocks + place.b
            piece = lax.dynamic_index_in_dim(planes, plane, 0, False)
            pieces.append(place.other_group(piece, k) if k else piece)
        near = jnp.concatenate(pieces, 1)
        other = place.other_outer(near)
        low = jnp.where(place.o == 0, near, other)
        high = jnp.where(place.o == 0, other, near)
        return jnp.split(jnp.concatenate([low, high], 0), place.rep, 1)

    def heads_to_owner(values):
        planes = values.reshape(place.blocks, -1, values.shape[1])
        mine = lax.dynamic_index_in_dim(planes, place.b, 0, False)
        mine = place.send(mine, lambda o, c, g, b, y: (g // 2, c, 2 * o + y, b, g % 2))
        mine = mine.reshape(2, -1, values.shape[1])
        pieces = []
        for k in range(TENSOR):
            piece = lax.dynamic_index_in_dim(mine, (place.y ^ k) % 2, 0, False)
            pieces.append(place.part(piece, k) if k else piece)
        return pieces

    whole_pieces = to_owner(sum_set(from_parts))
    part_pieces = heads_to_owner(sum_set(flat(part_grads)))
    wide_pieces = to_owner(sum_set(flat(wide_grads)))

    def chooser(adapters):
        column = (adapters[:, None] * ADAPTER_RANK + jnp.arange(ADAPTER_RANK)[None, :]).reshape(-1)
        return (jnp.arange(columns)[:, None] == column[None, :]).astype(bf16)

    def choosers(first):
        return jnp.concatenate(
            [
                chooser(lax.dynamic_index_in_dim(table, first ^ k, 0, False))
                for k in range(place.rep)
            ],
            1,
        )

    choose_near = choosers(place.g)
    choose_heads = choosers(place.p)

    def of_index(pieces, index):
        return jnp.concatenate([p[:, index * rank : (index + 1) * rank] for p in pieces], 1)

    whole_count, part_count = 10, 8
    lora_a, lora_b, lora_a_down, lora_b_up = [], [], [], []
    for layer in range(layers):
        near = [of_index(whole_pieces, layer * whole_count + k) for k in range(whole_count)]
        far = [of_index(part_pieces, layer * part_count + k) for k in range(part_count)]
        q_a, k_a, v_a, cq_a, ck_a, cv_a, up_a, o_b, co_b, down_b = near
        o_a, co_a, q_b, k_b, v_b, cq_b, ck_b, cv_b = far
        a_all = [(v, choose_near) for v in (q_a, k_a, v_a, cq_a, ck_a, cv_a, up_a)]
        a_all = a_all[:3] + [(o_a, choose_heads)] + a_all[3:6] + [(co_a, choose_heads)] + a_all[6:]
        b_all = [(v, choose_heads) for v in (q_b, k_b, v_b, cq_b, ck_b, cv_b)]
        b_all = b_all[:3] + [(o_b, choose_near)] + b_all[3:]
        b_all = b_all + [(co_b, choose_near), (down_b, choose_near)]
        lora_a.append(jnp.stack([dot_nt(v, chosen) for v, chosen in a_all]))
        lora_b.append(jnp.stack([dot_nt(chosen, v) for v, chosen in b_all]))
        lora_a_down.append(dot_nt(of_index(wide_pieces, 2 * layer), choose_near))
        lora_b_up.append(dot_nt(choose_near, of_index(wide_pieces, 2 * layer + 1)))

    grad_text = added(place.scatter(text_parts))
    grad_text = place.swap_back(grad_text.astype(bf16)).astype(f32)
    return (
        place.swap_back(state.astype(bf16)),
        place.swap_back(grad.astype(bf16)).astype(f32),
        grad_text.reshape(context.shape),
        jnp.stack(lora_a),
        jnp.stack(lora_a_down),
        jnp.stack(lora_b),
        jnp.stack(lora_b_up),
    )


def solution(mesh):
    rep, fsdp = AXES[:2], AXES[2:]
    sizes = (mesh.shape["rep"] // 2, 2, mesh.shape["fsdp"] // 2, 2)
    mesh = jax.sharding.Mesh(mesh.devices.reshape(sizes), AXES)
    in_specs = (
        P(AXES, None),
        P(rep, fsdp, None),
        P(AXES, None),
        P(None, AXES),
        P(rep),
        P(rep),
        P(rep),
        P(rep, None, None),
        P(),
        P(),
        P(None, None, fsdp, None),
        P(None, None, fsdp, None),
        P(None, fsdp, None),
        P(None, fsdp, None),
        P(None, None, fsdp, None),
        P(None, fsdp, None),
        P(None, None, None, fsdp),
        P(None, None, fsdp),
    )
    out_specs = (
        P(AXES, None),
        P(AXES, None),
        P(rep, fsdp, None),
        P(None, None, fsdp, None),
        P(None, fsdp, None),
        P(None, None, None, fsdp),
        P(None, None, fsdp),
    )
    return jax.shard_map(
        on_device, mesh=mesh, in_specs=in_specs, out_specs=out_specs, check_vma=False
    )
```

```python
import functools
import math

import jax
import jax.numpy as jnp
from jax import lax
from jax.experimental import pallas as pl
from jax.experimental.pallas import tpu as pltpu
from jax.sharding import PartitionSpec as P

HD = 128
ADAPTER_RANK = 16
TENSOR = 4

AXES = ("o", "c", "z", "y")
epsilon = 1e-06
masked_score = -1e30
f32 = jnp.float32
bf16 = jnp.bfloat16
CHUNK = 256
SUBLANES = 8
BLOCK = 512
VMEM_BYTES = 56 << 20

NEAR = ((0, 0), (0, 1), (0, 2), (0, 4), (0, 5), (0, 6), (0, 8), (1, 3), (1, 7), (1, 8))
HEADS = ((0, 3), (0, 7), (1, 0), (1, 1), (1, 2), (1, 4), (1, 5), (1, 6))


def dot(left, right):
    return jnp.dot(left, right, preferred_element_type=f32)


def dot_nt(left, right):
    return lax.dot_general(left, right, (((1,), (1,)), ((), ())), preferred_element_type=f32)


def dot_tn(left, right):
    return lax.dot_general(left, right, (((0,), (0,)), ((), ())), preferred_element_type=f32)


class Place:
    def __init__(self):
        self.rep = lax.axis_size(AXES[0]) * lax.axis_size(AXES[1])
        self.planes = lax.axis_size(AXES[2])
        self.size = 2 * self.planes
        self.blocks = self.planes // self.rep
        self.shards = self.size // TENSOR
        self.o, self.c, self.z, self.y = [lax.axis_index(axis) for axis in AXES]
        self.g, self.b = self.z // self.blocks, self.z % self.blocks
        self.p = 2 * self.o + self.y

    def send(self, values, move):
        pairs = []
        for index in range(self.rep * self.size):
            rest, y = divmod(index, 2)
            rest, z = divmod(rest, self.planes)
            to = move(*divmod(rest, 2), *divmod(z, self.blocks), y)
            if to is not None:
                o, c, g, b, y = to
                target = ((2 * o + c) * self.planes + g * self.blocks + b) * 2 + y
                pairs.append((index, target))
        return lax.ppermute(values, AXES, pairs)

    def swap(self, values):
        return self.send(values, lambda o, c, g, b, y: (g % 2, g // 2, 2 * o + c, b, y))

    def swap_back(self, values):
        return self.send(values, lambda o, c, g, b, y: (g // 2, g % 2, 2 * c + o, b, y))

    def part(self, values, k):
        return self.send(values, lambda o, c, g, b, y: (o ^ (k // 2), c, g, b, y ^ (k % 2)))

    def other_group(self, values, k):
        return self.send(values, lambda o, c, g, b, y: (o, c, g ^ k, b, y))

    def other_block(self, values, k):
        return self.send(values, lambda o, c, g, b, y: (o, c, g, b ^ k, y))

    def other_core(self, values):
        return self.send(values, lambda o, c, g, b, y: (o, 1 - c, g, b, y))

    def other_outer(self, values):
        return self.send(values, lambda o, c, g, b, y: (1 - o, c, g, b, y))

    def first_index(self, core, block, part):
        plane = (2 * core + part // 2) * self.blocks + block
        return 2 * plane + part % 2

    def gather(self, rows):
        cut = rows.shape[1] // 2
        one = self.part(rows, 1)
        two = self.part(rows, 2)
        return (rows, one, two, self.part(one[:, :cut], 2), self.part(two[:, cut:], 1))

    def scatter(self, parts):
        left_near, left_far, right_near, right_far = parts
        count = left_near.shape[0] // 2
        from_one = self.part(left_far, 1)
        from_two = self.part(right_far, 2)
        left = (left_near[count:].astype(f32) + from_one[count:].astype(f32)).astype(bf16)
        right = (right_near[count:].astype(f32) + from_two[count:].astype(f32)).astype(bf16)
        return (
            left_near, from_one, self.part(left, 2), right_near, from_two, self.part(right, 1)
        )

    def arrivals(self, stats):
        return [stats] + [self.part(stats, k) for k in range(1, TENSOR)]

    def spread(self, rows):
        own = [rows] + [self.other_block(rows, k) for k in range(1, self.blocks)]
        return own + [self.other_core(piece) for piece in own]

    def collect(self, pieces):
        total = [(piece,) for piece in pieces[: self.blocks]]
        total = [
            own + (self.other_core(piece.astype(bf16)),)
            for own, piece in zip(total, pieces[self.blocks :])
        ]
        if self.blocks == 1:
            return total[0]
        total = [sum(term.astype(f32) for term in terms) for terms in total]
        result = total[0]
        for k in range(1, self.blocks):
            result = result + self.other_block(total[k].astype(bf16), k).astype(f32)
        return (result,)

    def gather_planes(self, rows):
        return lax.all_gather(rows, (AXES[2], AXES[1]), axis=0, tiled=True)

    def fetch_columns(self, mine, there):
        arrived = self.send(
            there, lambda o, c, g, b, y: (o, c, g, b, 1 - y) if y == c else None
        )
        return jnp.where(self.y == self.c, mine, arrived)

    def fetch_heads(self, whole, first, widths):
        count, wide = whole.shape[0] // TENSOR, sum(widths)
        planes = self.planes // TENSOR
        half = count // (2 * planes)

        def rows_of(part):
            return lax.dynamic_slice(whole, (part * count, first), (count, wide))

        def core_rows(part):
            piece = rows_of(part).reshape(planes, 2, half, wide)
            return lax.dynamic_index_in_dim(piece, self.c, 1, False).reshape(planes * half, wide)

        halves = [self.part(core_rows(self.p ^ k), k) for k in range(1, TENSOR)]
        mine = jnp.stack(halves)
        other = self.other_core(mine)
        both = jnp.where(
            self.c == 0, jnp.stack([mine, other], 1), jnp.stack([other, mine], 1)
        ).reshape(TENSOR - 1, 2, planes, half, wide)
        pieces = [rows_of(self.p)]
        pieces += [both[k].transpose(1, 0, 2, 3).reshape(count, wide) for k in range(TENSOR - 1)]
        rows = count // (planes * 2 * TENSOR)
        if rows % (2 * SUBLANES) == 0:
            return assemble(self.p, pieces, planes, widths)
        parts, start = [], 0
        for one in widths:
            result = jnp.zeros((planes, 2, 2, 2, rows, TENSOR, one), bf16)
            for k, piece in enumerate(pieces):
                piece = piece[:, start : start + one].reshape(planes, 2, TENSOR, rows, one)
                piece = piece.transpose(0, 1, 3, 2, 4)[:, None, None]
                at = (0, self.y ^ (k % 2), self.o ^ (k // 2)) + (0,) * 4
                result = lax.dynamic_update_slice(result, piece, at)
            parts.append(result.reshape(count, TENSOR * one))
            start += one
        return jnp.concatenate(parts, 1)


def heads_share(matrices, share, shares):
    pieces = []
    for matrix in matrices:
        rows, width = matrix.shape[0] // shares, matrix.shape[1] // TENSOR
        piece = lax.dynamic_slice_in_dim(matrix, share * rows, rows, 0)
        piece = piece.reshape(rows, TENSOR, width).transpose(1, 0, 2)
        pieces.append(piece.reshape(TENSOR * rows, width))
    return jnp.concatenate(pieces, 1)


def assemble_kernel(planes, widths, part, *refs):
    pieces, out = refs[:TENSOR], refs[TENSOR]
    count = pieces[0].shape[0]
    rows = count // (planes * 2 * TENSOR)
    for k, piece in enumerate(pieces):
        owner = part[0] ^ k
        place = (owner % 2) * 2 + owner // 2
        for plane in range(planes):
            for core in range(2):
                start = (plane * TENSOR + place) * 2 + core
                at = pl.ds(pl.multiple_of(start * rows, rows), rows)
                for group in range(TENSOR):
                    source = ((plane * 2 + core) * TENSOR + group) * rows
                    first = 0
                    for one in widths:
                        to = first * TENSOR + group * one
                        out[at, to : to + one] = piece[
                            source : source + rows, first : first + one
                        ]
                        first += one


def assemble(part, pieces, planes, widths):
    count, wide = pieces[0].shape
    return pl.pallas_call(
        functools.partial(assemble_kernel, planes, widths),
        out_shape=jax.ShapeDtypeStruct((count, TENSOR * wide), bf16),
        in_specs=[pl.BlockSpec(memory_space=m) for m in [pltpu.SMEM] + [pltpu.VMEM] * TENSOR],
        out_specs=pl.BlockSpec(memory_space=pltpu.VMEM),
        compiler_params=pltpu.CompilerParams(vmem_limit_bytes=VMEM_BYTES),
        cost_estimate=pl.CostEstimate(
            flops=0, bytes_accessed=16 * count * wide, transcendentals=0
        ),
    )(part.astype(jnp.int32)[None], *pieces)


def rotary_tables(positions):
    pair_count = HD // 2
    third_part = pair_count // 3
    first_part = pair_count - 2 * third_part
    pieces = []
    for column, amount in ((0, first_part), (1, third_part), (2, third_part)):
        frequency = jnp.power(10000.0, -jnp.arange(amount, dtype=f32) / amount)
        pieces.append(positions[column].astype(f32)[:, None] * frequency[None, :])
    angles = jnp.repeat(jnp.concatenate(pieces, 1), 2, 1)
    sign = jnp.where(jnp.arange(HD) % 2 == 0, -1.0, 1.0)
    return jnp.cos(angles), jnp.sin(angles) * sign


def call(kernel, outs, args, scratch=(), flops=0, anywhere=()):
    outs = [jax.ShapeDtypeStruct(shape, dtype) for shape, dtype in outs]
    moved = sum(v.size * v.dtype.itemsize for v in list(args) + outs)
    space = [pl.ANY if k in anywhere else pltpu.VMEM for k in range(len(args))]
    return pl.pallas_call(
        kernel,
        out_shape=outs,
        in_specs=[pl.BlockSpec(memory_space=m) for m in space],
        out_specs=[pl.BlockSpec(memory_space=pltpu.VMEM) for _ in outs],
        scratch_shapes=list(scratch),
        compiler_params=pltpu.CompilerParams(vmem_limit_bytes=VMEM_BYTES),
        cost_estimate=pl.CostEstimate(flops=flops, bytes_accessed=moved, transcendentals=0),
    )(*args)


def part_shapes(rows, width):
    return [((rows // 2, width // 2), bf16)] * 4


def put_parts(parts, raw, inner, factors):
    count, half = raw.shape[0] // TENSOR, raw.shape[1] // 2
    for at in chunks(raw.shape[1]):
        values = (raw[:, at] + dot(inner, factors[:, at])).astype(bf16)
        right = at.start // half
        to = slice(at.start - right * half, at.stop - right * half)
        order = ((0, 1), (2, 3)) if right else ((0, 2), (1, 3))
        for ref, slots in zip(parts[2:] if right else parts[:2], order):
            for row, slot in enumerate(slots):
                ref[row * count : (row + 1) * count, to] = values[
                    slot * count : (slot + 1) * count
                ]


def start_copy(source, held, sem):
    copy = pltpu.make_async_copy(source, held, sem)
    copy.start()
    return copy


def join(pieces, full):
    own, one, two, left, right = pieces
    count, width = own.shape
    full[:count] = own[...]
    full[count : 2 * count] = one[...]
    full[2 * count : 3 * count] = two[...]
    full[3 * count :, : width // 2] = left[...]
    full[3 * count :, width // 2 :] = right[...]


def chunks(width):
    return [slice(start, start + CHUNK) for start in range(0, width, CHUNK)]


def turned(values):
    return values.astype(f32).T.astype(bf16)


def narrow(values, mask):
    return (values * mask).astype(bf16)


def row_sums(values):
    ones = jnp.ones((SUBLANES, values.shape[1]), bf16)
    high = values.astype(bf16)
    return dot_nt(ones, high) + dot_nt(ones, (values - high.astype(f32)).astype(bf16))


def as_columns(row, width):
    column = jnp.broadcast_to(row, (HD, row.shape[1])).T
    return jnp.concatenate([column] * (width // HD), 1)


def total_stats(refs):
    total = refs[0][...]
    count = total.shape[1] // TENSOR
    for k, ref in enumerate(refs):
        if k:
            order = [ref[:, (j ^ k) * count : ((j ^ k) + 1) * count] for j in range(TENSOR)]
            total = total + jnp.concatenate(order, 1)
    return total


def stat_rows(total, index):
    return total[index * SUBLANES : index * SUBLANES + 1]


def swap_pairs(values):
    lane = lax.broadcasted_iota(jnp.int32, values.shape, 1)
    return jnp.where(lane % 2 == 0, pltpu.roll(values, HD - 1, 1), pltpu.roll(values, 1, 1))


def rotate(values, cosine, sine):
    heads = [values[:, k : k + HD] for k in range(0, values.shape[1], HD)]
    return jnp.concatenate([v * cosine + swap_pairs(v) * sine for v in heads], 1)


def rotate_back(grad, cosine, sine):
    heads = [grad[:, k : k + HD] for k in range(0, grad.shape[1], HD)]
    return jnp.concatenate([v * cosine + swap_pairs(v * sine) for v in heads], 1)


def gelu_terms(x):
    slope = math.sqrt(2.0 / math.pi)
    square = x * x
    t = jnp.tanh(slope * x * (1.0 + 0.044715 * square))
    value = 0.5 * x * (1.0 + t)
    inner = slope * (1.0 + 3.0 * 0.044715 * square)
    return value, 0.5 * (1.0 + t) + 0.5 * x * (1.0 - t * t) * inner


def sum_terms(terms, count):
    sides = []
    for near, first, far in (terms[:3], terms[3:]):
        total = near[:count].astype(f32) + first[:count].astype(f32) + far[...].astype(f32)
        sides.append(total)
    return jnp.concatenate(sides, 1)


def advance_kernel(*refs):
    terms, (state, factor, scale, shift, new, normed) = refs[:6], refs[6:]
    value = state[...] + factor[...] * sum_terms(terms, state.shape[0])
    new[...] = value
    centred = value - jnp.mean(value, -1, keepdims=True)
    hat = centred * lax.rsqrt(jnp.mean(centred * centred, -1, keepdims=True) + epsilon)
    normed[...] = (hat * scale[...] + shift[...]).astype(bf16)


def advance(terms, state, factor, scale, shift):
    return call(
        advance_kernel, [(state.shape, f32), (state.shape, bf16)],
        (*terms, state, factor, scale, shift), flops=30 * state.size,
    )


def retreat_kernel(*refs):
    terms, (state, grad, scale, factor, new, out) = refs[:6], refs[6:]
    value = state[...]
    centred = value - jnp.mean(value, -1, keepdims=True)
    spread = lax.rsqrt(jnp.mean(centred * centred, -1, keepdims=True) + epsilon)
    hat = centred * spread
    inner = sum_terms(terms, value.shape[0]) * scale[...]
    along = jnp.mean(inner * hat, -1, keepdims=True)
    result = grad[...] + spread * (inner - jnp.mean(inner, -1, keepdims=True) - hat * along)
    new[...] = result
    out[...] = (result * factor[...]).astype(bf16)


def retreat(terms, state, grad, scale, factor):
    return call(
        retreat_kernel, [(state.shape, f32), (state.shape, bf16)],
        (*terms, state, grad, scale, factor), flops=40 * state.size,
    )


def pack_kernel(layer, squares, planes, *refs):
    part, square, wide = refs[:3]
    mine, there, held, sems = refs[3:]
    own = square.shape[3] // TENSOR
    copies = []
    if planes:
        whole = pltpu.make_async_copy(wide.at[layer], held, sems.at[2 * len(squares)])
        whole.start()
    for k, column in enumerate(squares):
        for side, out in enumerate((mine, there)):
            at = pl.ds(pl.multiple_of((part[0] ^ side) * own, own), own)
            copies.append(
                pltpu.make_async_copy(
                    square.at[layer, squares[column], :, at],
                    out.at[:, pl.ds(column, own)],
                    sems.at[2 * k + side],
                )
            )
            copies[-1].start()
    if planes:
        base, stop, count = planes
        one = held.shape[1] // (8 * count)
        step = (stop - base) // (2 * count)
        whole.wait()
        for out in (mine, there) if step > one else ():
            out[:, base:stop] = jnp.zeros((held.shape[0], stop - base), bf16)
        for k in range(TENSOR):

            @pl.when(part[0] == k)
            def _(k=k):
                for side, out in enumerate((mine, there)):
                    o, y = divmod(k ^ side, 2)
                    for z in range(2 * count):
                        at = (((z // 2) * 2 + y) * 4 + o * 2 + z % 2) * one
                        to = base + z * step
                        out[:, to : to + one] = held[:, at : at + one]

    for copy in copies:
        copy.wait()


def pack(part, square, wide, layer, width, squares, planes=None):
    rows = square.shape[2]
    scratch = [
        pltpu.VMEM(wide.shape[1:] if planes else (SUBLANES, HD), bf16),
        pltpu.SemaphoreType.DMA((2 * len(squares) + 1,)),
    ]
    return pl.pallas_call(
        functools.partial(pack_kernel, layer, squares, planes),
        out_shape=[jax.ShapeDtypeStruct((rows, width), bf16)] * 2,
        in_specs=[pl.BlockSpec(memory_space=m) for m in (pltpu.SMEM, pl.ANY, pl.ANY)],
        out_specs=[pl.BlockSpec(memory_space=pltpu.VMEM)] * 2,
        scratch_shapes=scratch,
        compiler_params=pltpu.CompilerParams(vmem_limit_bytes=VMEM_BYTES),
        cost_estimate=pl.CostEstimate(flops=0, bytes_accessed=8 * rows * width, transcendentals=0),
    )(part, square, wide)


def picked(ref, place, rank, count=1):
    return ref[place * rank : (place + count) * rank]


def last_columns(ref, held):
    return ref.at[:, pl.ds(ref.shape[1] - held.shape[1], held.shape[1])]


def ffn_kernel(places, *refs):
    pieces, (mask, near, far, w_in, w_out), refs = refs[:5], refs[5:10], refs[10:]
    parts, (up_raw, up_inner, down_inner), refs = refs[:4], refs[4:7], refs[7:]
    full, raw, hidden, held_in, held_out, sems = refs
    rank = mask.shape[1]
    width = full.shape[1]
    up_a, down_b, down_a, up_b = places
    first = start_copy(last_columns(w_in, held_in), held_in, sems.at[0])
    second = start_copy(w_out.at[:, pl.ds(0, full.shape[1])], held_out, sems.at[1])
    join(pieces, full)
    inner = narrow(dot_nt(full[...], picked(near, up_a, rank)), mask[...])
    up_inner[...] = inner
    first.wait()
    raw[:, : held_in.shape[1]] = dot(full[...], held_in[...])
    factors = picked(far, up_b, rank)
    for at in chunks(held_in.shape[1]):
        values = raw[:, at] + dot(inner, factors[:, at])
        up_raw[:, at] = values.astype(bf16)
        hidden[:, at] = gelu_terms(values)[0].astype(bf16)
    second.wait()
    raw[:, :width] = dot(hidden[...], held_out[...])
    inner = narrow(dot_nt(hidden[...], picked(far, down_a, rank)), mask[...])
    down_inner[...] = inner
    put_parts(parts, raw.at[:, :width], inner, picked(near, down_b, rank))


def ffn(pieces, mask, near, far, w_in, w_out, places):
    count, width = pieces[0].shape
    rows, rank = mask.shape
    wide = w_out.shape[0]
    outs = part_shapes(rows, width) + [((rows, wide), bf16), ((rows, rank), bf16)]
    scratch = [
        pltpu.VMEM((rows, width), bf16),
        pltpu.VMEM((rows, max(wide, width)), f32),
        pltpu.VMEM((rows, wide), bf16),
        pltpu.VMEM((width, wide), bf16),
        pltpu.VMEM((w_out.shape[0], width), bf16),
        pltpu.SemaphoreType.DMA((2,)),
    ]
    outs = call(
        functools.partial(ffn_kernel, places), outs + [((rows, rank), bf16)],
        (*pieces, mask, near, far, w_in, w_out), scratch, 4 * rows * width * wide, (8, 9),
    )
    return outs[:4], tuple(outs[4:])


def ffn_back_kernel(places, *refs):
    grads, inputs, refs = refs[:5], refs[5:10], refs[10:]
    up_raw, up_inner, down_inner, mask, near, far, w_in, w_out = refs[:8]
    parts, (a_down, b_up, a_up, b_down) = refs[8:12], refs[12:16]
    grad, full, raw, grad_up, held_in, held_out, sems = refs[16:]
    rank = mask.shape[1]
    width = full.shape[1]
    at_up_a, at_down_b, at_down_a, at_up_b = places
    second = start_copy(w_out.at[:, pl.ds(0, full.shape[1])], held_out, sems.at[1])
    first = start_copy(last_columns(w_in, held_in), held_in, sems.at[0])
    join(grads, grad)
    join(inputs, full)
    down_back = narrow(dot_nt(grad[...], picked(near, at_down_b, rank)), mask[...])
    down_turned = turned(down_back)
    up_turned = turned(up_inner[...])
    factors = picked(far, at_down_a, rank)
    second.wait()
    raw[:, : held_out.shape[0]] = dot_nt(grad[...], held_out[...])
    for at in chunks(up_raw.shape[1]):
        hidden_grad = raw[:, at] + dot(down_back, factors[:, at])
        value, slope = gelu_terms(up_raw[:, at].astype(f32))
        raw_grad = (hidden_grad * slope).astype(bf16)
        grad_up[:, at] = raw_grad
        a_down[:, at] = dot(down_turned, value.astype(bf16)).astype(bf16)
        b_up[:, at] = dot(up_turned, raw_grad).astype(bf16)
    up_back = narrow(dot_nt(grad_up[...], picked(far, at_up_b, rank)), mask[...])
    first.wait()
    raw[:, :width] = dot_nt(grad_up[...], held_in[...])
    put_parts(parts, raw.at[:, :width], up_back, picked(near, at_up_a, rank))
    a_up[...] = dot(turned(up_back), full[...]).astype(bf16)
    b_down[...] = dot(turned(down_inner[...]), grad[...]).astype(bf16)


def ffn_back(grads, inputs, saved, mask, near, far, w_in, w_out, places):
    count, width = grads[0].shape
    rows, rank = mask.shape
    wide = w_out.shape[0]
    outs = part_shapes(rows, width) + [((rank, n), bf16) for n in (wide, wide, width, width)]
    scratch = [
        pltpu.VMEM((rows, width), bf16),
        pltpu.VMEM((rows, width), bf16),
        pltpu.VMEM((rows, max(wide, width)), f32),
        pltpu.VMEM((rows, wide), bf16),
        pltpu.VMEM((width, wide), bf16),
        pltpu.VMEM((w_out.shape[0], width), bf16),
        pltpu.SemaphoreType.DMA((2,)),
    ]
    outs = call(
        functools.partial(ffn_back_kernel, places), outs,
        (*grads, *inputs, *saved, mask, near, far, w_in, w_out), scratch,
        4 * rows * width * wide, (16, 17),
    )
    return outs[:4], outs[4:]


def project_kernel(start, count, normed, *refs):
    pieces, (mask, weights, near, heads), refs = refs[:5], refs[5:9], refs[9:]
    raws, (inner, stats, full, together, held, sems) = refs[:count], refs[count:]
    own = raws[0].shape[1]
    rank = mask.shape[1]
    base, near_at, heads_at = start
    copy = start_copy(weights.at[:, pl.ds(base, count * own)], held, sems.at[0])
    join(pieces, full)
    inner[...] = narrow(
        dot_nt(full[...], picked(near, near_at, rank, count)),
        jnp.concatenate([mask[...]] * count, 1),
    )
    copy.wait()
    together[...] = dot(full[...], held[...])
    for k, raw in enumerate(raws):
        values = together[:, k * own : (k + 1) * own] + dot(
            inner[:, k * rank : (k + 1) * rank], picked(heads, heads_at + k, rank)
        )
        raw[...] = values.astype(raw.dtype)
        if k < normed:
            stats[k * SUBLANES : (k + 1) * SUBLANES] = row_sums(values * values)


def project(pieces, mask, weights, near, heads, start, count, normed):
    rows, rank = mask.shape
    own = heads.shape[1]
    outs = [((rows, own), f32 if k < normed else bf16) for k in range(count)]
    outs += [((rows, count * rank), bf16), ((normed * SUBLANES, rows), f32)]
    outs = call(
        functools.partial(project_kernel, start, count, normed), outs,
        (*pieces, mask, weights, near, heads),
        [
            pltpu.VMEM((rows, pieces[0].shape[1]), bf16), pltpu.VMEM((rows, count * own), f32),
            pltpu.VMEM((weights.shape[0], count * own), bf16), pltpu.SemaphoreType.DMA((1,)),
        ],
        2 * rows * weights.shape[0] * own * count, (6,),
    )
    return outs[:count], outs[count], outs[count + 1]


def scales_of(total, index, width, own):
    return as_columns(lax.rsqrt(stat_rows(total, index) / width + epsilon), own)


def normalize_kernel(count, turning, valued, width, *refs):
    raws, gains, refs = refs[:count], refs[count : 2 * count], refs[2 * count :]
    tables, refs = refs[: 2 * turning], refs[2 * turning :]
    value, refs = refs[:valued], refs[valued:]
    stats, outs, total = refs[: -count - 1], refs[-count - 1 : -1], refs[-1]
    total[...] = total_stats(stats)
    own = raws[0].shape[1]
    for k in range(count):
        values = raws[k][...] * scales_of(total, k, width, own) * gains[k][...]
        if turning:
            values = rotate(values, tables[0][...], tables[1][...])
        outs[k][:, :own] = values.astype(bf16)
    if valued:
        outs[-1][:, own:] = value[0][...]


def normalize(raws, gains, stats, width, tables=(), value=()):
    shape = raws[0].shape
    outs = [(shape, bf16) for _ in raws]
    if value:
        outs[-1] = ((shape[0], 2 * shape[1]), bf16)
    outs.append((stats[0].shape, f32))
    outs = call(
        functools.partial(normalize_kernel, len(raws), len(tables) // 2, len(value), width), outs,
        (*raws, *gains, *tables, *value, *stats), flops=20 * len(raws) * raws[0].size,
    )
    return outs[:-1], outs[-1]


def attend_kernel(count, start, *refs):
    query, marks, refs = refs[0], refs[1], refs[2:]
    pairs, key_marks, refs = refs[:count], refs[count : 2 * count], refs[2 * count :]
    mask, weights, near, heads = refs[:4]
    parts, (result, inner, raw, held, sems) = refs[4:8], refs[8:]
    rows, own = query.shape
    width, rank = near.shape[1], mask.shape[1]
    base, near_at, heads_at = start
    copy = start_copy(weights.at[:, pl.ds(base, width)], held, sems.at[0])
    scale = 1.0 / math.sqrt(HD)
    block = min(BLOCK, rows)

    @pl.loop(0, rows // block)
    def _(index):
        at = pl.ds(pl.multiple_of(index * block, block), block)
        allowed = [marks[at] == key_mark[...] for key_mark in key_marks]
        for head in range(0, own, HD):
            scores = [
                jnp.where(
                    ok, dot_nt(query[at, head : head + HD], pair[:, head : head + HD]) * scale,
                    masked_score,
                )
                for ok, pair in zip(allowed, pairs)
            ]
            peak = functools.reduce(
                jnp.maximum, [jnp.max(s, -1, keepdims=True) for s in scores]
            )
            weighed = [jnp.exp(s - peak) for s in scores]
            total = sum(jnp.sum(w, -1, keepdims=True) for w in weighed)
            summed = sum(
                dot(w.astype(bf16), pair[:, own + head : own + head + HD])
                for w, pair in zip(weighed, pairs)
            )
            result[at, head : head + HD] = (summed / total).astype(bf16)

    copy.wait()
    raw[...] = dot(result[...], held[...])
    inner[...] = narrow(dot_nt(result[...], picked(heads, heads_at, rank)), mask[...])
    put_parts(parts, raw, inner[...], picked(near, near_at, rank))


def attend(query, marks, pairs, key_marks, mask, weights, near, heads, start):
    rows, own = query.shape
    width, rank = near.shape[1], mask.shape[1]
    outs = part_shapes(rows, width) + [((rows, own), bf16), ((rows, rank), bf16)]
    keys = sum(pair.shape[0] for pair in pairs)
    outs = call(
        functools.partial(attend_kernel, len(pairs), start), outs,
        (query, marks, *pairs, *key_marks, mask, weights, near, heads),
        [
            pltpu.VMEM((rows, width), f32), pltpu.VMEM((own, width), bf16),
            pltpu.SemaphoreType.DMA((1,)),
        ],
        4 * rows * keys * own + 2 * rows * own * width, (3 + 2 * len(pairs),),
    )
    return outs[:4], outs[4], outs[5]


def attend_back_kernel(count, start, *refs):
    grads, (query, marks), refs = refs[:5], refs[5:7], refs[7:]
    pairs, key_marks, refs = refs[:count], refs[count : 2 * count], refs[2 * count :]
    (result, inner, mask, weights, near, heads), refs = refs[:6], refs[6:]
    base, near_at, heads_at = start
    grad_query, pair_grads, refs = refs[0], refs[1 : 1 + count], refs[1 + count :]
    a_grad, b_grad, grad, grad_out, raw, held, sems = refs
    rows, own = query.shape
    rank = mask.shape[1]
    scale = 1.0 / math.sqrt(HD)
    block = min(BLOCK, rows)
    copy = start_copy(weights.at[:, pl.ds(base, grad.shape[1])], held, sems.at[0])
    join(grads, grad)
    back = narrow(dot_nt(grad[...], picked(near, near_at, rank)), mask[...])
    b_grad[...] = dot(turned(inner[...]), grad[...]).astype(bf16)
    copy.wait()
    raw[...] = dot_nt(grad[...], held[...])
    grad_out[...] = (raw[...] + dot(back, picked(heads, heads_at, rank))).astype(bf16)
    a_grad[...] = dot(turned(back), result[...]).astype(bf16)
    for head in range(0, own, HD):
        here, there = slice(head, head + HD), slice(own + head, own + head + HD)
        keys_turned = [turned(pair[:, here]) for pair in pairs]
        for start in range(0, rows, block):
            at = slice(start, start + block)
            q, g = query[at, here], grad_out[at, here]
            scores = [
                jnp.where(
                    key_mark[...] == marks[:, at], dot_nt(pair[:, here], q) * scale, masked_score
                )
                for key_mark, pair in zip(key_marks, pairs)
            ]
            peak = functools.reduce(jnp.maximum, [jnp.max(s, 0, keepdims=True) for s in scores])
            weighed = [jnp.exp(s - peak) for s in scores]
            inverse = 1.0 / sum(jnp.sum(w, 0, keepdims=True) for w in weighed)
            probs = [w * inverse for w in weighed]
            along = [dot_nt(pair[:, there], g) for pair in pairs]
            delta = sum(jnp.sum(p * d, 0, keepdims=True) for p, d in zip(probs, along))
            turned_grad = 0.0
            for k in range(count):
                score_grad = (probs[k] * (along[k] - delta)).astype(bf16)
                key_grad = dot(score_grad, q) * scale
                value_grad = dot(probs[k].astype(bf16), g)
                if start:
                    key_grad = key_grad + pair_grads[k][:, here]
                    value_grad = value_grad + pair_grads[k][:, there]
                pair_grads[k][:, here] = key_grad
                pair_grads[k][:, there] = value_grad
                turned_grad = turned_grad + dot(keys_turned[k], score_grad)
            grad_query[at, here] = (turned_grad * scale).T


def attend_back(
    grads, query, marks, pairs, key_marks, result, inner, mask, weights, near, heads, start
):
    rows, own = query.shape
    width, rank = near.shape[1], mask.shape[1]
    outs = [((rows, own), f32)] + [(pair.shape, f32) for pair in pairs]
    outs += [((rank, own), bf16), ((rank, width), bf16)]
    keys = sum(pair.shape[0] for pair in pairs)
    outs = call(
        functools.partial(attend_back_kernel, len(pairs), start), outs,
        (*grads, query, marks, *pairs, *key_marks, result, inner, mask, weights, near, heads),
        [
            pltpu.VMEM((rows, width), bf16), pltpu.VMEM((rows, own), bf16),
            pltpu.VMEM((rows, own), f32), pltpu.VMEM((own, width), bf16),
            pltpu.SemaphoreType.DMA((1,)),
        ],
        10 * rows * keys * own + 2 * rows * own * width, (10 + 2 * len(pairs),),
    )
    return outs[0], outs[1:-2], outs[-2], outs[-1]


def back_stats_kernel(counts, turning, valued, width, *refs):
    number = len(counts)
    terms = []
    for count in counts:
        terms.append(refs[:count])
        refs = refs[count:]
    raws, gains, refs = refs[:number], refs[number : 2 * number], refs[2 * number :]
    tables, refs = refs[: 2 * turning], refs[2 * turning :]
    total, outs, stats = refs[0], refs[1:-1], refs[-1]
    own = raws[0].shape[1]
    for k in range(number):
        grad = sum(term[:, :own].astype(f32) for term in terms[k])
        if turning:
            grad = rotate_back(grad, tables[0][...], tables[1][...])
        grad = grad * gains[k][...]
        outs[k][...] = grad
        hat = raws[k][...] * scales_of(total, k, width, own)
        stats[k * SUBLANES : (k + 1) * SUBLANES] = row_sums(hat * grad)
    if valued:
        outs[-1][...] = sum(term[:, own:].astype(f32) for term in terms[-1]).astype(bf16)


def back_stats(terms, raws, gains, total, width, tables=(), valued=False):
    shape = raws[0].shape
    outs = [(shape, f32) for _ in raws] + [(shape, bf16)] * valued + [(total.shape, f32)]
    outs = call(
        functools.partial(
            back_stats_kernel, tuple(len(t) for t in terms), len(tables) // 2, int(valued), width
        ),
        outs, (*[term for t in terms for term in t], *raws, *gains, *tables, total),
        flops=30 * len(raws) * raws[0].size,
    )
    return outs[:-1], outs[-1]


def project_back_kernel(start, count, normed, parted, *refs):
    scaled, raws, refs = refs[:count], refs[count : count + normed], refs[count + normed :]
    total, (inner, mask, weights, near, heads), refs = refs[0], refs[1:6], refs[6:]
    inputs, refs = refs[:5], refs[5:]
    split = 4 if parted else 1
    stats, refs = refs[: -8 - split], refs[-8 - split :]
    outs, (a_grad, b_grad, full, grads, back, raw, held, sems) = refs[:split], refs[split:]
    own = scaled[0].shape[1]
    width = full.shape[1]
    rank = mask.shape[1]
    base, near_at, heads_at = start
    copy = start_copy(weights.at[:, pl.ds(base, count * own)], held, sems.at[0])
    join(inputs, full)
    along = total_stats(stats)
    for k in range(count):
        if k < normed:
            scale = scales_of(total, k, width, own)
            hat = raws[k][...] * scale
            mean = as_columns(stat_rows(along, k) / width, own)
            grads[:, k * own : (k + 1) * own] = (scale * (scaled[k][...] - hat * mean)).astype(bf16)
        else:
            grads[:, k * own : (k + 1) * own] = scaled[k][...]
    inner_turned = turned(inner[...])
    for k in range(count):
        at = slice(k * rank, (k + 1) * rank)
        grad = grads[:, k * own : (k + 1) * own]
        back[:, at] = narrow(dot_nt(grad, picked(heads, heads_at + k, rank)), mask[...])
        b_grad[at] = dot(inner_turned[at], grad).astype(bf16)
    a_grad[...] = dot(turned(back[...]), full[...]).astype(bf16)
    copy.wait()
    raw[...] = dot_nt(grads[...], held[...])
    factors = picked(near, near_at, rank, count)
    if parted:
        put_parts(outs, raw, back[...], factors)
    else:
        for at in chunks(width):
            outs[0][:, at] = raw[:, at] + dot(back[...], factors[:, at])


def project_back(
    scaled, raws, total, stats, inner, mask, weights, near, heads, inputs, start, parted=True
):
    count, normed = len(scaled), len(raws)
    rows, own = scaled[0].shape
    width, rank = weights.shape[0], mask.shape[1]
    outs = part_shapes(rows, width) if parted else [((rows, width), f32)]
    split = len(outs)
    outs = outs + [((count * rank, width), bf16), ((count * rank, own), bf16)]
    scratch = [
        pltpu.VMEM((rows, width), bf16),
        pltpu.VMEM((rows, count * own), bf16),
        pltpu.VMEM((rows, count * rank), bf16),
        pltpu.VMEM((rows, width), f32),
        pltpu.VMEM((width, count * own), bf16),
        pltpu.SemaphoreType.DMA((1,)),
    ]
    outs = call(
        functools.partial(project_back_kernel, start, count, normed, parted), outs,
        (*scaled, *raws, total, inner, mask, weights, near, heads, *inputs, *stats), scratch,
        2 * rows * width * own * count, (count + normed + 3,),
    )
    return outs[:split], outs[split], outs[split + 1]


def on_device(
    tokens,
    context,
    cotangent,
    positions,
    sequence_lengths,
    sequence_adapter,
    text_token_count,
    timestep_modulation,
    modulation,
    gains,
    query_key_value_weight,
    output_weight,
    up_weight,
    down_weight,
    first_factors,
    down_first_factor,
    second_factors,
    up_second_factor,
):
    place = Place()
    rows, width = tokens.shape
    seq_count, text_local = context.shape[:2]
    layers = query_key_value_weight.shape[0]
    columns = first_factors.shape[3]
    rank = seq_count * ADAPTER_RANK
    own = width // TENSOR
    wide = up_weight.shape[2] // TENSOR
    padded = -(-wide // CHUNK) * CHUNK
    set_rows = TENSOR * rows

    numbers = jnp.concatenate([positions.reshape(-1), sequence_lengths, text_token_count])
    numbers = place.swap(numbers)
    moved = place.swap(
        jnp.concatenate([tokens, context.reshape(seq_count * text_local, width)], 0)
    )
    state = moved[:rows].astype(f32)
    times = place.swap(timestep_modulation)
    positions = numbers[: 3 * rows].reshape(3, rows)
    lengths, counts = [
        numbers[3 * rows + k * seq_count : 3 * rows + (k + 1) * seq_count] for k in range(2)
    ]

    bounds = jnp.cumsum(lengths)

    def token_segments(index):
        packed = jnp.arange(rows, dtype=jnp.int32) * place.size + index
        return jnp.sum((packed[:, None] >= bounds[None, :]).astype(jnp.int32), 1)

    def text_marks(index):
        at = index * text_local + jnp.arange(text_local)
        marks = jnp.where(at[None, :] < counts[:, None], jnp.arange(seq_count)[:, None], -1)
        return marks.reshape(-1)

    def over_set(function, core, block):
        return jnp.concatenate(
            [function(place.first_index(core, block, place.p ^ k)) for k in range(TENSOR)]
        )

    def over_group(function):
        return [
            over_set(function, core, place.b ^ k)
            for core in (place.c, 1 - place.c)
            for k in range(place.blocks)
        ]

    segment = over_set(token_segments, place.c, place.b)
    sequence = jnp.minimum(segment, seq_count - 1)
    self_marks = over_group(token_segments)
    cross_marks = over_group(text_marks)
    column_sequence = jnp.arange(rank) // ADAPTER_RANK
    mask = (sequence[:, None] == column_sequence[None, :]) & (segment < seq_count)[:, None]
    mask = mask.astype(f32)
    text_sequence = jnp.tile(jnp.repeat(jnp.arange(seq_count), text_local), TENSOR)
    text_mask = (text_sequence[:, None] == column_sequence[None, :]).astype(f32)
    valid = (segment[:rows] < seq_count).astype(f32)[:, None]

    def mods_of(layer):
        table = modulation[layer][None] + times
        chosen = [table[0, k][None] for k in range(6)]
        for s in range(1, seq_count):
            here = (sequence[:rows] == s)[:, None]
            chosen = [jnp.where(here, table[s, k][None], chosen[k]) for k in range(6)]
        return chosen

    def own_gain(layer, index):
        return lax.dynamic_slice_in_dim(gains[layer, index], place.p * own, own, 0)[None]

    table = jnp.zeros((place.rep, seq_count), jnp.int32)
    for k in range(2):
        arrived = sequence_adapter if k == 0 else place.other_outer(sequence_adapter)
        for m, values in enumerate((arrived, place.other_core(arrived))):
            here = jnp.arange(place.rep) == 2 * (place.o ^ k) + (place.c ^ m)
            table = jnp.where(here[:, None], values[None], table)
    def tied(value, after):
        return value if after is None else lax.optimization_barrier((value, after))[0]

    wanted = (table[:, :, None] * ADAPTER_RANK + jnp.arange(ADAPTER_RANK)).reshape(-1)
    choose = (jnp.arange(columns)[:, None] == wanted[None, :]).astype(bf16)
    firsts = jnp.einsum("lkdj,jr->lkdr", first_factors, choose).astype(bf16)
    seconds = jnp.einsum("lkjd,jr->lkdr", second_factors, choose).astype(bf16)

    def own_columns(values, count):
        column = jnp.arange(count * rank * place.rep)
        kept = jnp.arange(count * rank)
        here = (column // (rank * place.rep))[:, None] == (kept // rank)[None, :]
        here &= (column % (rank * place.rep))[:, None] == (place.g * rank + kept % rank)[None, :]
        return lax.dot_general(
            here.astype(bf16), values, (((0,), (1,)), ((), ())), preferred_element_type=f32
        ).astype(bf16)

    factor_rows = [
        jnp.concatenate([(firsts, seconds)[w][layer, k] for w, k in NEAR], 1)
        for layer in range(layers)
    ]
    factor_rows = jnp.concatenate(factor_rows, 1)
    factor_rows = place.fetch_columns(factor_rows, factor_rows)
    factor_width = factor_rows.shape[1] // layers

    def factors_of(layer):
        return factor_rows[:, layer * factor_width : (layer + 1) * factor_width]

    up_at = 6 * own
    part = place.p.astype(jnp.int32)[None]
    share = 2 * place.o + place.c

    def self_rows_of(layer, after):
        mine, there = pack(
            tied(part, after), query_key_value_weight, up_weight, layer, 3 * own,
            {k * own: k for k in range(3)},
        )
        factors = [(firsts, seconds)[w][layer, k] for w, k in HEADS]
        piece = heads_share(
            [output_weight[layer, 0], output_weight[layer, 1], jnp.concatenate(factors, 1)],
            share, place.rep,
        )
        return jnp.concatenate([place.fetch_columns(mine, there), piece], 1)

    def fetch_self(rows, after):
        whole = place.gather_planes(tied(rows, after))
        widths = (own, own, len(HEADS) * rank * place.rep // TENSOR)
        heads = place.fetch_heads(whole, 3 * own, widths)
        near = whole[:, 3 * own + sum(widths) :]
        near = own_columns(near, len(NEAR)) if near.shape[1] else None
        return whole, heads, own_columns(heads[:, 2 * width :], len(HEADS)), near

    def other_rows_of(layer, after):
        mine, there = pack(
            tied(part, after), query_key_value_weight, up_weight, layer, 3 * own + padded,
            {k * own: 3 + k for k in range(3)}, (3 * own, 3 * own + padded, place.planes),
        )
        return place.fetch_columns(mine, there)

    def fetch_others(layer, rows, after):
        rows = tied(rows, after)
        cross_up = place.gather_planes(rows)
        count = down_weight.shape[1] // place.rep
        piece = lax.dynamic_slice(
            down_weight, (layer, share * count, 0), (1, count, width)
        )[0]
        factors = [
            dot(lax.dynamic_slice_in_dim(down_first_factor[layer], share * count, count, 0), choose),
            dot_tn(
                lax.dynamic_slice_in_dim(up_second_factor[layer], share * count, count, 1), choose
            ),
        ]
        piece = jnp.concatenate([piece] + [v.astype(bf16) for v in factors], 1)
        piece = jnp.pad(piece, ((0, padded // place.size - count), (0, 0)))
        down = place.gather_planes(tied(piece, rows))
        return cross_up, down, own_columns(down[:, width:], 2), piece

    positions = jnp.stack([positions] + [place.part(positions, k) for k in range(1, TENSOR)], 1)
    tables = rotary_tables(positions.reshape(3, set_rows))

    def arrivals(stats):
        arrived = place.arrivals(stats)
        count = stats.shape[1] // TENSOR
        if count % HD == 0:
            return arrived
        pieces = [v.reshape(-1, TENSOR, count) for v in arrived]
        total = sum(
            jnp.stack([v[:, j ^ k] for j in range(TENSOR)], 1) for k, v in enumerate(pieces)
        )
        return [total.reshape(stats.shape)]

    columns_of = [v.reshape(-1, 1) for v in (segment, sequence)]
    rows_of = [v.reshape(1, -1) for v in (segment, sequence)]
    self_rows, cross_rows = [[v.reshape(1, -1) for v in m] for m in (self_marks, cross_marks)]
    self_columns, cross_columns = [
        [v.reshape(-1, 1) for v in m] for m in (self_marks, cross_marks)
    ]
    zero_row = jnp.zeros((1, width), f32)
    in_at, out_at, cross_at, text_at = (0, 0, 2), (0, 7, 0), (0, 3, 5), (own, 4, 6)
    crossed_at, ffn_at = (width, 8, 1), (6, 9, 0, 1)

    saved = []
    factors = []
    for layer in range(layers):
        shift_one, scale_one, gate_one, shift_two, scale_two, gate_two = mods_of(layer)
        factors.append((valid * gate_one, valid * gate_two, 1.0 + scale_one, 1.0 + scale_two))
        factors[-1] += (shift_one, shift_two)
    valid_rows = jnp.broadcast_to(valid, (rows, width))
    centred = state - jnp.mean(state, -1, keepdims=True)
    hat = centred * lax.rsqrt(jnp.mean(centred * centred, -1, keepdims=True) + epsilon)
    normed = (hat * factors[0][2] + factors[0][4]).astype(bf16)
    fetched = []
    coming = fetch_self(self_rows_of(0, None), (moved, numbers, times))
    first_near = own_columns(place.gather_planes(factors_of(0)), len(NEAR))
    others = None
    for layer in range(layers):
        gate_one, gate_two, scale_one, scale_two, shift_one, shift_two = factors[layer]
        self_in, heads, far_heads, near = coming
        near = first_near if near is None else near
        self_pieces = place.gather(normed)
        if layer == 0:
            first_rows = other_rows_of(layer, self_pieces[3])
            others = fetch_others(layer, first_rows, None)
            prepared = [
                (self_rows_of(k, first_rows), other_rows_of(k, first_rows))
                for k in range(1, layers)
            ]
            text = place.gather(tied(moved[rows:], self_pieces[3]))
        cross_in, ffn_out, far, down_piece = others
        raws, self_inner, stats = project(self_pieces, mask, self_in, near, far_heads, in_at, 3, 2)
        gain = [own_gain(layer, k) for k in range(4)]
        (query, pair), self_total = normalize(
            raws[:2], gain[:2], arrivals(stats), width, tables, raws[2:]
        )
        pairs = place.spread(pair)
        parts, attended, out_inner = attend(
            query, columns_of[0], pairs, self_rows, mask, heads, near, far_heads, out_at
        )
        self_saved = (self_pieces, raws, self_inner, self_total, query, pairs, attended, out_inner)
        state_one, normed = advance(
            place.scatter(parts), state, gate_one, gains[layer, 4][None], zero_row
        )
        if layer + 1 < layers:
            following = jnp.concatenate([prepared[layer][0], factors_of(layer + 1)], 1)
            following = tied(following, down_piece)
            coming = fetch_self(following, normed)

        text_raws, text_inner, stats = project(
            text, text_mask, cross_in, near, far_heads, text_at, 2, 1
        )
        (pair,), text_total = normalize(
            text_raws[:1], gain[3:], arrivals(stats), width, (), text_raws[1:]
        )
        pairs = place.spread(pair)
        cross_pieces = place.gather(normed)
        if layer + 1 < layers:
            others = fetch_others(layer + 1, prepared[layer][1], cross_pieces[3])
        else:
            cotangent = place.swap(tied(cotangent, ffn_out[:SUBLANES]))
        raws, cross_inner, stats = project(
            cross_pieces, mask, cross_in, near, far_heads, cross_at, 1, 1
        )
        (query,), cross_total = normalize(raws, gain[2:3], arrivals(stats), width)
        parts, crossed, crossed_inner = attend(
            query, columns_of[1], pairs, cross_rows, mask, heads, near, far_heads, crossed_at
        )
        cross_saved = (
            cross_pieces, raws, cross_inner, cross_total, query, pairs, crossed, crossed_inner
        )
        state_two, normed = advance(
            place.scatter(parts), state_one, valid_rows, scale_two, shift_two
        )

        ffn_pieces = place.gather(normed)
        ready = mask if layer + 1 == layers else tied(mask, coming[1])
        parts, ffn_saved = ffn(ffn_pieces, ready, near, far, cross_in, ffn_out, ffn_at)
        fetched.append((self_in, heads, cross_in, ffn_out, near, far, far_heads))
        saved.append(
            (
                (state, state_one, state_two), self_saved, cross_saved,
                (text_raws, text_inner, text_total), (ffn_pieces, ffn_saved), gain,
            )
        )
        following = factors[min(layer + 1, layers - 1)]
        state, normed = advance(
            place.scatter(parts), state_two, gate_two, following[2], following[4]
        )

    grad = cotangent.astype(f32)
    out = (grad * factors[-1][1]).astype(bf16)
    grad_text = 0.0
    whole_grads, part_grads, wide_grads = [], [], []
    for layer in reversed(range(layers)):
        self_in, heads, cross_in, ffn_out, near, far, far_heads = fetched[layer]
        gate_one, gate_two, scale_one, scale_two, shift_one, shift_two = factors[layer]
        (
            (state_zero, state_one, state_two), self_saved, cross_saved,
            (text_raws, text_inner, text_total), (ffn_pieces, ffn_saved), gain,
        ) = saved[layer]
        parts, (down_a, up_b, up_a, down_b) = ffn_back(
            place.gather(out), ffn_pieces, ffn_saved, mask, near, far, cross_in, ffn_out, ffn_at
        )
        grad, out = retreat(place.scatter(parts), state_two, grad, scale_two, valid_rows)

        pieces, raws, inner, total, query, pairs, result, result_inner = cross_saved
        grad_query, pair_grads, cross_out_a, cross_out_b = attend_back(
            place.gather(out), query, rows_of[1], pairs, cross_columns, result, result_inner,
            mask, heads, near, far_heads, crossed_at,
        )
        scaled, stats = back_stats([(grad_query,)], raws, gain[2:3], total, width)
        parts, cross_a, cross_b = project_back(
            scaled, raws, total, arrivals(stats), inner, mask, cross_in, near, far_heads, pieces,
            cross_at,
        )
        terms = place.collect(pair_grads)
        scaled, stats = back_stats([terms], text_raws[:1], gain[3:], text_total, width, (), True)
        (text_grad,), text_a, text_b = project_back(
            scaled, text_raws[:1], text_total, arrivals(stats), text_inner, text_mask, cross_in,
            near, far_heads, text, text_at, False,
        )
        grad_text = grad_text + text_grad
        grad, out = retreat(
            place.scatter(parts), state_one, grad, gains[layer, 4][None], gate_one
        )

        pieces, raws, inner, total, query, pairs, result, result_inner = self_saved
        grad_query, pair_grads, self_out_a, self_out_b = attend_back(
            place.gather(out), query, rows_of[0], pairs, self_columns, result, result_inner,
            mask, heads, near, far_heads, out_at,
        )
        terms = place.collect(pair_grads)
        scaled, stats = back_stats(
            [(grad_query,), terms], raws[:2], gain[:2], total, width, tables, True
        )
        parts, self_a, self_b = project_back(
            scaled, raws[:2], total, arrivals(stats), inner, mask, self_in, near, far_heads, pieces,
            in_at,
        )
        gate = factors[max(layer - 1, 0)][1]
        grad, out = retreat(place.scatter(parts), state_zero, grad, scale_one, gate)

        whole_grads.append(
            jnp.concatenate([self_a, cross_a, text_a, up_a, self_out_b, cross_out_b, down_b], 0)
        )
        part_grads.append(
            jnp.concatenate([self_out_a, cross_out_a, self_b, cross_b, text_b], 0)
        )
        wide_grad = jnp.concatenate([down_a, up_b], 0).reshape(2 * rank, place.size, -1)
        wide_grads.append(wide_grad[:, :, : wide // place.size].reshape(2 * rank, wide))

    def flat(lists):
        return jnp.concatenate(lists[::-1], 0).T

    grad_text = grad_text.astype(bf16)
    count, half = grad_text.shape[0] // TENSOR, width // 2
    slots = [grad_text[k * count : (k + 1) * count] for k in range(TENSOR)]
    text_parts = [
        jnp.concatenate([v[:, at] for v in pair], 0)
        for at, pair in (
            (slice(0, half), (slots[0], slots[2])),
            (slice(0, half), (slots[1], slots[3])),
            (slice(half, width), (slots[0], slots[1])),
            (slice(half, width), (slots[2], slots[3])),
        )
    ]

    def added(terms):
        left, one, two, right, three, four = [v.astype(f32) for v in terms]
        count = two.shape[0]
        return jnp.concatenate(
            [left[:count] + one[:count] + two, right[:count] + three[:count] + four], 1
        )

    whole_all = flat(whole_grads)
    whole_wide = whole_all.shape[1]
    whole_all = whole_all.reshape(place.planes, 2, 2, -1, whole_wide)
    slots = [
        lax.dynamic_slice(
            whole_all,
            (0, (place.p ^ k) % 2, (place.p ^ k) // 2, 0, 0),
            (place.planes, 1, 1) + whole_all.shape[3:],
        ).reshape(-1, whole_wide)
        for k in range(TENSOR)
    ]
    count, half = slots[0].shape[0], whole_wide // 2
    from_parts = added(
        place.scatter(
            [
                jnp.concatenate([v[:, at] for v in pair], 0)
                for at, pair in (
                    (slice(0, half), (slots[0], slots[2])),
                    (slice(0, half), (slots[1], slots[3])),
                    (slice(half, whole_wide), (slots[0], slots[1])),
                    (slice(half, whole_wide), (slots[2], slots[3])),
                )
            ]
        )
    )

    def sum_set(values):
        values = values.astype(f32) + place.other_core(values.astype(bf16)).astype(f32)
        result = values
        for k in range(1, place.blocks):
            result = result + place.other_block(values.astype(bf16), k).astype(f32)
        return result.astype(bf16)

    def to_owner(values):
        planes = values.reshape(place.planes, -1, values.shape[1])
        pieces = []
        for k in range(place.rep):
            plane = (place.g ^ k) * place.blocks + place.b
            piece = lax.dynamic_index_in_dim(planes, plane, 0, False)
            pieces.append(place.other_group(piece, k) if k else piece)
        near = jnp.concatenate(pieces, 1)
        other = place.other_outer(near)
        low = jnp.where(place.o == 0, near, other)
        high = jnp.where(place.o == 0, other, near)
        return jnp.split(jnp.concatenate([low, high], 0), place.rep, 1)

    def heads_to_owner(values):
        planes = values.reshape(place.blocks, -1, values.shape[1])
        mine = lax.dynamic_index_in_dim(planes, place.b, 0, False)
        mine = place.send(mine, lambda o, c, g, b, y: (g // 2, c, 2 * o + y, b, g % 2))
        mine = mine.reshape(2, -1, values.shape[1])
        pieces = []
        for k in range(TENSOR):
            piece = lax.dynamic_index_in_dim(mine, (place.y ^ k) % 2, 0, False)
            pieces.append(place.part(piece, k) if k else piece)
        return pieces

    whole_pieces = to_owner(sum_set(from_parts))
    part_pieces = heads_to_owner(sum_set(flat(part_grads)))
    wide_pieces = to_owner(sum_set(flat(wide_grads)))

    def chooser(adapters):
        column = (adapters[:, None] * ADAPTER_RANK + jnp.arange(ADAPTER_RANK)[None, :]).reshape(-1)
        return (jnp.arange(columns)[:, None] == column[None, :]).astype(bf16)

    def choosers(first):
        return jnp.concatenate(
            [
                chooser(lax.dynamic_index_in_dim(table, first ^ k, 0, False))
                for k in range(place.rep)
            ],
            1,
        )

    choose_near = choosers(place.g)
    choose_heads = choosers(place.p)

    def of_index(pieces, index):
        return jnp.concatenate([p[:, index * rank : (index + 1) * rank] for p in pieces], 1)

    whole_count, part_count = 10, 8
    lora_a, lora_b, lora_a_down, lora_b_up = [], [], [], []
    for layer in range(layers):
        near = [of_index(whole_pieces, layer * whole_count + k) for k in range(whole_count)]
        far = [of_index(part_pieces, layer * part_count + k) for k in range(part_count)]
        q_a, k_a, v_a, cq_a, ck_a, cv_a, up_a, o_b, co_b, down_b = near
        o_a, co_a, q_b, k_b, v_b, cq_b, ck_b, cv_b = far
        a_all = [(v, choose_near) for v in (q_a, k_a, v_a, cq_a, ck_a, cv_a, up_a)]
        a_all = a_all[:3] + [(o_a, choose_heads)] + a_all[3:6] + [(co_a, choose_heads)] + a_all[6:]
        b_all = [(v, choose_heads) for v in (q_b, k_b, v_b, cq_b, ck_b, cv_b)]
        b_all = b_all[:3] + [(o_b, choose_near)] + b_all[3:]
        b_all = b_all + [(co_b, choose_near), (down_b, choose_near)]
        lora_a.append(jnp.stack([dot_nt(v, chosen) for v, chosen in a_all]))
        lora_b.append(jnp.stack([dot_nt(chosen, v) for v, chosen in b_all]))
        lora_a_down.append(dot_nt(of_index(wide_pieces, 2 * layer), choose_near))
        lora_b_up.append(dot_nt(choose_near, of_index(wide_pieces, 2 * layer + 1)))

    grad_text = added(place.scatter(text_parts))
    grad_text = place.swap_back(grad_text.astype(bf16)).astype(f32)
    return (
        place.swap_back(state.astype(bf16)),
        place.swap_back(grad.astype(bf16)).astype(f32),
        grad_text.reshape(context.shape),
        jnp.stack(lora_a),
        jnp.stack(lora_a_down),
        jnp.stack(lora_b),
        jnp.stack(lora_b_up),
    )


def solution(mesh):
    rep, fsdp = AXES[:2], AXES[2:]
    sizes = (mesh.shape["rep"] // 2, 2, mesh.shape["fsdp"] // 2, 2)
    mesh = jax.sharding.Mesh(mesh.devices.reshape(sizes), AXES)
    in_specs = (
        P(AXES, None),
        P(rep, fsdp, None),
        P(AXES, None),
        P(None, AXES),
        P(rep),
        P(rep),
        P(rep),
        P(rep, None, None),
        P(),
        P(),
        P(None, None, fsdp, None),
        P(None, None, fsdp, None),
        P(None, fsdp, None),
        P(None, fsdp, None),
        P(None, None, fsdp, None),
        P(None, fsdp, None),
        P(None, None, None, fsdp),
        P(None, None, fsdp),
    )
    out_specs = (
        P(AXES, None),
        P(AXES, None),
        P(rep, fsdp, None),
        P(None, None, fsdp, None),
        P(None, fsdp, None),
        P(None, None, None, fsdp),
        P(None, None, fsdp),
    )
    return jax.shard_map(
        on_device, mesh=mesh, in_specs=in_specs, out_specs=out_specs, check_vma=False
    )
```
